128 devices in a mesh: wide: 16 (over y, z_hi, core), narrow: 8 (over x, z_lo).
Axes of the slice: x: 4, y: 4, z: 4 (z_hi: 2, z_lo: 2; z = z_hi * 2 + z_lo), core: 2. Of those that a mesh axis runs over, the one named last changes fastest.
Arguments:
- x_pre: bfloat16 [32, 240, 2048], P('wide', None, 'narrow'), may hold values from -64 to 64
- x_act: bfloat16 [32, 50, 1024], P('wide', None, 'narrow'), may hold values from -64 to 64
- lengths: int32 [32], P('wide'), may hold values from 5 to 48, as said below
- cot_pre: float32 [32, 240, 2048], P('wide', None, 'narrow'), may hold values from -6 to 6
- cot_act: float32 [32, 50, 1024], P('wide', None, 'narrow'), may hold values from -6 to 6
- attn_gain_pre: float32 [2048], P('narrow'), may hold values from 0.1 to 1.9
- query_pre: bfloat16 [2048, 2048], P('wide', 'narrow'), may hold values from -0.125 to 0.125
- key_pre: bfloat16 [2048, 256], P('wide', 'narrow'), may hold values from -0.125 to 0.125
- value_pre: bfloat16 [2048, 256], P('wide', 'narrow'), may hold values from -0.125 to 0.125
- out_pre: bfloat16 [2048, 2048], P('narrow', 'wide'), may hold values from -1 to 1
- ffn_gain_pre: float32 [2048], P('narrow'), may hold values from 0.1 to 1.9
- gate_pre: bfloat16 [2048, 16384], P('wide', 'narrow'), may hold values from -0.125 to 0.125
- up_pre: bfloat16 [2048, 16384], P('wide', 'narrow'), may hold values from -0.125 to 0.125
- down_pre: bfloat16 [16384, 2048], P('narrow', 'wide'), may hold values from -0.046875 to 0.046875
- attn_gain_act: float32 [1024], P('narrow'), may hold values from 0.1 to 1.9
- query_act: bfloat16 [1024, 2048], P('wide', 'narrow'), may hold values from -0.1875 to 0.1875
- key_act: bfloat16 [1024, 256], P('wide', 'narrow'), may hold values from -0.1875 to 0.1875
- value_act: bfloat16 [1024, 256], P('wide', 'narrow'), may hold values from -0.1875 to 0.1875
- out_act: bfloat16 [2048, 1024], P('narrow', 'wide'), may hold values from -1 to 1
- ffn_gain_act: float32 [1024], P('narrow'), may hold values from 0.1 to 1.9
- gate_act: bfloat16 [1024, 4096], P('wide', 'narrow'), may hold values from -0.1875 to 0.1875
- up_act: bfloat16 [1024, 4096], P('wide', 'narrow'), may hold values from -0.1875 to 0.1875
- down_act: bfloat16 [4096, 1024], P('narrow', 'wide'), may hold values from -0.09375 to 0.09375
Outputs:
- y_pre: bfloat16 [32, 240, 2048], P('wide', None, 'narrow')
- y_act: bfloat16 [32, 50, 1024], P('wide', None, 'narrow')
- grad_x_pre: float32 [32, 240, 2048], P('wide', None, 'narrow')
- grad_x_act: float32 [32, 50, 1024], P('wide', None, 'narrow')
- grad_attn_gain_pre: float32 [2048], P('narrow')
- grad_query_pre: float32 [2048, 2048], P('wide', 'narrow')
- grad_key_pre: float32 [2048, 256], P('wide', 'narrow')
- grad_value_pre: float32 [2048, 256], P('wide', 'narrow')
- grad_out_pre: float32 [2048, 2048], P('narrow', 'wide')
- grad_ffn_gain_pre: float32 [2048], P('narrow')
- grad_gate_pre: float32 [2048, 16384], P('wide', 'narrow')
- grad_up_pre: float32 [2048, 16384], P('wide', 'narrow')
- grad_down_pre: float32 [16384, 2048], P('narrow', 'wide')
- grad_attn_gain_act: float32 [1024], P('narrow')
- grad_query_act: float32 [1024, 2048], P('wide', 'narrow')
- grad_key_act: float32 [1024, 256], P('wide', 'narrow')
- grad_value_act: float32 [1024, 256], P('wide', 'narrow')
- grad_out_act: float32 [2048, 1024], P('narrow', 'wide')
- grad_ffn_gain_act: float32 [1024], P('narrow')
- grad_gate_act: float32 [1024, 4096], P('wide', 'narrow')
- grad_up_act: float32 [1024, 4096], P('wide', 'narrow')
- grad_down_act: float32 [4096, 1024], P('narrow', 'wide')
The draws below stay inside these ranges and needn't reach their ends.
Inputs may be any that keep to these rules, and one draw needn't show every extreme that they name: `lengths`: some item has exactly 48 live instruction tokens and another exactly 5.
All inputs are finite; a program needn't handle non-finite values.
Results may differ from the reference program's by a relative error of at most 0.023.
Values may be sent and summed in bfloat16 or wider, within the bound.
A program may use at most 192 MiB of HBM per device.

```python
from functools import partial
import jax
import jax.numpy as jnp
from jax import lax

D_P = 2048
FF_P = 16384
D_A = 1024
FF_A = 4096
HEADS = 8
HEAD = 256
IMG = 192
TXT = 48
ACT = 50
P_SIZE = 240
ITEMS = 32


def field_scales(key, items, tokens, width, row_lower, row_upper):
    row_key, column_key = jax.random.split(key)
    row_scale = jnp.exp(jax.random.uniform(row_key, (items, tokens, 1), jnp.float32, jnp.log(row_lower), jnp.log(row_upper)))
    columns = jnp.arange(width).astype(jnp.float32) / width
    column_scale = 0.6 * jnp.exp(columns * jnp.log(3.0)) * jnp.exp(jax.random.uniform(column_key, (width,), jnp.float32, -0.3, 0.3))
    return row_scale * column_scale


def draw_x_pre(key, part):
    key = jax.random.fold_in(key, 1)
    noise_key, scale_key = jax.random.split(key)
    noise_field = jax.random.truncated_normal(noise_key, -4.0, 4.0, (ITEMS, IMG + TXT, D_P), jnp.float32)
    return (noise_field * field_scales(scale_key, ITEMS, IMG + TXT, D_P, 0.5, 5.0)).astype(jnp.bfloat16)


def draw_x_act(key, part):
    key = jax.random.fold_in(key, 2)
    noise_key, scale_key = jax.random.split(key)
    noise_field = jax.random.truncated_normal(noise_key, -4.0, 4.0, (ITEMS, ACT, D_A), jnp.float32)
    return (noise_field * field_scales(scale_key, ITEMS, ACT, D_A, 0.5, 5.0)).astype(jnp.bfloat16)


def draw_lengths(key, part):
    key = jax.random.fold_in(key, 3)
    value_key, spot_key = jax.random.split(key)
    counts = jax.random.randint(value_key, (ITEMS,), 5, TXT + 1).astype(jnp.int32)
    location = jax.random.randint(spot_key, (), 0, ITEMS)
    counts = counts.at[location].set(TXT)
    counts = counts.at[(location + 1) % ITEMS].set(5)
    return counts


def levels(rng, dims, pieces, least, high):
    factor_of, own = 1.0, jax.random.fold_in(rng, 6)
    for position, blocks in pieces:
        heights = jnp.exp(jax.random.uniform(jax.random.fold_in(own, position), (blocks,), jnp.float32, least / len(pieces), high / len(pieces)))
        factor_of = factor_of * jnp.repeat(heights, dims[position] // blocks).reshape([-1 if axis == position else 1 for axis in range(len(dims))])
    return factor_of


def gaussian(key, extent, spread, reach, cuts=(), kind=jnp.bfloat16):
    drawn = jax.random.normal(key, extent, jnp.float32) * spread
    if len(cuts) > 0:
        drawn = levels(key, extent, cuts, -0.22, 0.18) * drawn
    return jnp.clip(drawn, min=-reach, max=reach).astype(kind)


def setup_inputs(seed: int = 0) -> dict:
    streams_of = jax.random.split(jax.random.key(seed), 24)
    x_pre = draw_x_pre(jax.random.fold_in(streams_of[23], 71), 0)
    x_act = draw_x_act(jax.random.fold_in(streams_of[23], 71), 0)
    lengths = draw_lengths(jax.random.fold_in(streams_of[23], 71), 0)
    cot_pre = gaussian(streams_of[3], (ITEMS, P_SIZE, D_P), 1.0, 6.0, ((0, 16), (2, 8)), jnp.float32)
    cot_act = gaussian(streams_of[4], (ITEMS, ACT, D_A), 1.0, 6.0, ((0, 16), (2, 8)), jnp.float32)
    attn_gain_pre = jnp.clip(1.0 + 0.18 * jax.random.normal(streams_of[5], (D_P,), jnp.float32), 0.1, 1.9)
    query_pre = gaussian(streams_of[6], (D_P, HEADS * HEAD), D_P ** -0.5, 0.125, ((0, 16), (1, 8)))
    key_pre = gaussian(streams_of[7], (D_P, HEAD), D_P ** -0.5, 0.125, ((0, 16), (1, 8)))
    value_pre = gaussian(streams_of[8], (D_P, HEAD), D_P ** -0.5, 0.125, ((0, 16), (1, 8)))
    out_pre = gaussian(streams_of[9], (HEADS * HEAD, D_P), (HEADS * HEAD // 64) ** -0.5, 1.0, ((0, 8), (1, 16)))
    ffn_gain_pre = jnp.clip(1.0 + 0.18 * jax.random.normal(streams_of[10], (D_P,), jnp.float32), 0.1, 1.9)
    gate_pre = gaussian(streams_of[11], (D_P, FF_P), D_P ** -0.5, 0.125, ((0, 16), (1, 8)))
    up_pre = gaussian(streams_of[12], (D_P, FF_P), D_P ** -0.5, 0.125, ((0, 16), (1, 8)))
    down_pre = gaussian(streams_of[13], (FF_P, D_P), FF_P ** -0.5, 0.046875, ((0, 8), (1, 16)))
    attn_gain_act = jnp.clip(1.0 + 0.18 * jax.random.normal(streams_of[14], (D_A,), jnp.float32), 0.1, 1.9)
    query_act = gaussian(streams_of[15], (D_A, HEADS * HEAD), D_A ** -0.5, 0.1875, ((0, 16), (1, 8)))
    key_act = gaussian(streams_of[16], (D_A, HEAD), D_A ** -0.5, 0.1875, ((0, 16), (1, 8)))
    value_act = gaussian(streams_of[17], (D_A, HEAD), D_A ** -0.5, 0.1875, ((0, 16), (1, 8)))
    out_act = gaussian(streams_of[18], (HEADS * HEAD, D_A), (HEADS * HEAD // 64) ** -0.5, 1.0, ((0, 8), (1, 16)))
    ffn_gain_act = jnp.clip(1.0 + 0.18 * jax.random.normal(streams_of[19], (D_A,), jnp.float32), 0.1, 1.9)
    gate_act = gaussian(streams_of[20], (D_A, FF_A), D_A ** -0.5, 0.1875, ((0, 16), (1, 8)))
    up_act = gaussian(streams_of[21], (D_A, FF_A), D_A ** -0.5, 0.1875, ((0, 16), (1, 8)))
    down_act = gaussian(streams_of[22], (FF_A, D_A), FF_A ** -0.5, 0.09375, ((0, 8), (1, 16)))
    return {"x_pre": x_pre, "x_act": x_act, "lengths": lengths, "cot_pre": cot_pre, "cot_act": cot_act, "attn_gain_pre": attn_gain_pre, "query_pre": query_pre, "key_pre": key_pre, "value_pre": value_pre, "out_pre": out_pre, "ffn_gain_pre": ffn_gain_pre, "gate_pre": gate_pre, "up_pre": up_pre, "down_pre": down_pre, "attn_gain_act": attn_gain_act, "query_act": query_act, "key_act": key_act, "value_act": value_act, "out_act": out_act, "ffn_gain_act": ffn_gain_act, "gate_act": gate_act, "up_act": up_act, "down_act": down_act}


EPSILON = 1e-06
MASKED_SCORE = -1000000000.0

@jax.custom_vjp
def low(v):
    return lax.optimization_barrier(v.astype(jnp.bfloat16)).astype(jnp.float32)

@jax.custom_vjp
def low_back(v):
    return v

def low_keep(v):
    return (low(v), None)

def low_pass(kept, grad):
    return (grad,)

def back_keep(v):
    return (v, None)

def back_low(kept, grad):
    return (low(grad),)
low.defvjp(low_keep, low_pass)
low_back.defvjp(back_keep, back_low)

def product(left, right):
    return jnp.dot(left, right, precision=lax.Precision.HIGHEST, preferred_element_type=jnp.float32)

def rms_norm(values, gain):
    return values * lax.rsqrt(lax.optimization_barrier(jnp.mean(values * values, axis=-1, keepdims=True)) + EPSILON) * gain

def feed_forward(hidden, gain, gate_weight, up_weight, down_weight):
    normed = low(rms_norm(hidden, gain))
    gate = low_back(product(normed, gate_weight))
    upper = low_back(product(normed, up_weight))
    active = low(jax.nn.gelu(gate, approximate=True) * upper)
    return hidden + low_back(product(active, down_weight))

def visible_keys(length):
    places = jnp.arange(IMG + TXT + ACT)
    prefix = IMG + TXT
    key_live = (places < IMG) | (places >= prefix) | (places - IMG < length)
    return key_live[None, :] & ((places[None, :] < prefix) | (places[:, None] >= prefix))

def layer(length, weights, x_prefix, x_action):
    attn_gain_pre, query_pre, key_pre, value_pre, out_pre, ffn_gain_pre, gate_pre, up_pre, down_pre, attn_gain_act, query_act, key_act, value_act, out_act, ffn_gain_act, gate_act, up_act, down_act = weights
    prefix = IMG + TXT
    total = IMG + TXT + ACT
    normed_prefix = low(rms_norm(x_prefix, attn_gain_pre))
    normed_action = low(rms_norm(x_action, attn_gain_act))
    queries = low(low_back(jnp.concatenate([product(normed_prefix, query_pre), product(normed_action, query_act)], axis=0)))
    keys = low(low_back(jnp.concatenate([product(normed_prefix, key_pre), product(normed_action, key_act)], axis=0)))
    values = low(low_back(jnp.concatenate([product(normed_prefix, value_pre), product(normed_action, value_act)], axis=0)))
    query_heads = queries.reshape(total, HEADS, HEAD)
    scores = jnp.einsum('shd,td->hst', query_heads, keys, precision=lax.Precision.HIGHEST) * HEAD ** (-0.5)
    scores = low_back(jnp.where(visible_keys(length)[None], scores, MASKED_SCORE))
    attention = jnp.exp(scores - lax.optimization_barrier(jnp.max(scores, axis=-1, keepdims=True)))
    attention = attention / lax.optimization_barrier(jnp.sum(attention, axis=-1, keepdims=True))
    mixture = jnp.einsum('hst,td->shd', low(attention), values, precision=lax.Precision.HIGHEST)
    mixture = low(low_back(mixture.reshape(total, HEADS * HEAD)))
    hidden_prefix = x_prefix + low_back(product(mixture[:prefix], out_pre))
    hidden_action = x_action + low_back(product(mixture[prefix:], out_act))
    result_prefix = feed_forward(hidden_prefix, ffn_gain_pre, gate_pre, up_pre, down_pre)
    result_action = feed_forward(hidden_action, ffn_gain_act, gate_act, up_act, down_act)
    return (result_prefix, result_action)

def reference(x_pre, x_act, lengths, cot_pre, cot_act, attn_gain_pre, query_pre, key_pre, value_pre, out_pre, ffn_gain_pre, gate_pre, up_pre, down_pre, attn_gain_act, query_act, key_act, value_act, out_act, ffn_gain_act, gate_act, up_act, down_act):
    weights = tuple((matrix.astype(jnp.float32) for matrix in (attn_gain_pre, query_pre, key_pre, value_pre, out_pre, ffn_gain_pre, gate_pre, up_pre, down_pre, attn_gain_act, query_act, key_act, value_act, out_act, ffn_gain_act, gate_act, up_act, down_act)))
    inputs_prefix = x_pre.astype(jnp.float32)
    inputs_action = x_act.astype(jnp.float32)

    def one_sample(totals, sample):
        sample_prefix, sample_action, length, grad_prefix, grad_action = sample
        outputs, pullback = jax.vjp(partial(layer, length), weights, sample_prefix, sample_action)
        weight_grads, input_prefix, input_action = pullback((grad_prefix, grad_action))
        totals = jax.tree.map(jnp.add, totals, weight_grads)
        return (totals, (outputs[0], outputs[1], input_prefix, input_action))
    zeros = jax.tree.map(jnp.zeros_like, weights)
    totals, stacked = lax.scan(one_sample, zeros, (inputs_prefix, inputs_action, lengths, cot_pre.astype(jnp.float32), cot_act.astype(jnp.float32)))
    result_prefix, result_action, input_prefix, input_action = stacked
    return (result_prefix.astype(jnp.bfloat16), result_action.astype(jnp.bfloat16), input_prefix, input_action, totals[0], totals[1], totals[2], totals[3], totals[4], totals[5], totals[6], totals[7], totals[8], totals[9], totals[10], totals[11], totals[12], totals[13], totals[14], totals[15], totals[16], totals[17])
```

```python
import functools
import jax
import jax.numpy as jnp
from jax import lax
from jax.experimental import pallas as pl
from jax.experimental.pallas import tpu as pltpu
from jax.sharding import PartitionSpec as P

MESH = pl.DeviceIdType.MESH
BF = jnp.bfloat16
F32 = jnp.float32
SEMS = 256
VMEM_CAP = 62 * 1024 * 1024


class Place:
    def __init__(self):
        wide, narrow = lax.axis_index("wide"), lax.axis_index("narrow")
        self.core = lax.rem(wide, 2)
        self.zh = lax.rem(lax.div(wide, 2), 2)
        self.y = lax.div(wide, 4)
        self.zl = lax.rem(narrow, 2)
        self.x = lax.div(narrow, 2)
        self.z = self.zh * 2 + self.zl

    def wide_at(self, y, zh, core):
        return (y * 2 + zh) * 2 + core

    def coord(self, axis):
        return {"x": self.x, "y": self.y, "z": self.z}[axis]

    def off(self, axis, step):
        return lax.rem(self.coord(axis) + step + 4, 4)

    def peer(self, name):
        if name == "sib":
            return {"wide": self.wide_at(self.y, self.zh, 1 - self.core)}
        if name == "z2":
            return {"wide": self.wide_at(self.y, 1 - self.zh, self.core)}
        if name == "zl":
            return {"narrow": self.x * 2 + 1 - self.zl}
        axis, step = name[0], 1 if name[1] == "+" else -1
        at = self.off(axis, step)
        if axis == "y":
            return {"wide": self.wide_at(at, self.zh, self.core)}
        if axis == "x":
            return {"narrow": at * 2 + self.zl}
        return {"wide": self.wide_at(self.y, lax.div(at, 2), self.core), "narrow": self.x * 2 + lax.rem(at, 2)}


class Link:
    def __init__(self, out, into):
        self.out, self.into = out, into

    def arrive(self):
        self.into.wait_recv()

    def left(self):
        self.out.wait_send()


class Comm:
    def __init__(self, send_sems, recv_sems, local_sems):
        self.place = Place()
        self.send_sems, self.recv_sems, self.local_sems = send_sems, recv_sems, local_sems
        self.count, self.local_count = 0, 0
        self.links = []

    def enter(self, peers):
        barrier = pltpu.get_barrier_semaphore()
        for name in peers:
            pl.semaphore_signal(barrier, inc=1, device_id=self.place.peer(name), device_id_type=MESH)
        pl.semaphore_wait(barrier, len(peers))

    def send(self, src, dst, name, incoming):
        index = self.count
        self.count += 1
        make = lambda to: pltpu.make_async_remote_copy(
            src_ref=src, dst_ref=to, send_sem=self.send_sems.at[index], recv_sem=self.recv_sems.at[index],
            device_id=self.place.peer(name), device_id_type=MESH)
        out = make(dst)
        out.start()
        link = Link(out, make(incoming))
        self.links.append(link)
        return link

    def local(self, src, dst):
        index = self.local_count
        self.local_count += 1
        copy = pltpu.make_async_copy(src, dst, self.local_sems.at[index])
        copy.start()
        return copy

    def close(self):
        for link in self.links:
            link.left()

    def ring_gather(self, axis, view, parts, own=None):
        place = self.place
        at = lambda step: place.off(axis, step)
        src = own if own is not None else (lambda part: view(at(0), part))
        plus = [self.send(src(p), view(at(0), p), axis + "+", view(at(-1), p)) for p, _ in parts]
        minus = [self.send(src(p), view(at(0), p), axis + "-", view(at(1), p)) for p, _ in parts]
        yield
        far = []
        for (p, way), up in zip(parts, plus):
            up.arrive()
            if way > 0:
                far.append(self.send(view(at(-1), p), view(at(-1), p), axis + "+", view(at(-2), p)))
        for (p, way), down in zip(parts, minus):
            down.arrive()
            if way < 0:
                far.append(self.send(view(at(1), p), view(at(1), p), axis + "-", view(at(2), p)))
        yield
        for link in far:
            link.arrive()

    def pair_ring_gather(self, pair, axis, view, parts, own, give, whole):
        place = self.place
        mine = {"z2": place.zh, "zl": place.zl}[pair]
        here = place.coord(axis)
        swap = self.send(give, view(here, mine, whole), pair, view(here, 1 - mine, whole))
        first = self.ring_gather(axis, lambda k, p: view(k, mine, p), parts, own)
        next(first)
        yield
        swap.arrive()
        second = self.ring_gather(axis, lambda k, p: view(k, 1 - mine, p), parts)
        next(second)
        yield
        next(first)
        yield
        next(second)
        yield
        drain(first)
        drain(second)

    def plane_gather(self, view, parts_x, parts_z):
        place = self.place
        every = slice(None)
        ax = self.ring_gather("x", lambda k, p: view(k, place.z, p), parts_x)
        bz = self.ring_gather("z", lambda k, p: view(place.x, k, p), parts_z)
        next(ax), next(bz)
        yield
        next(ax), next(bz)
        yield
        drain(ax)
        az = self.ring_gather("z", lambda k, p: view(every, k, p), parts_x)
        next(az)
        drain(bz)
        bx = self.ring_gather("x", lambda k, p: view(k, every, p), parts_z)
        next(bx)
        yield
        next(az), next(bx)
        yield
        drain(az), drain(bx)

    def ring_sum(self, axis, view, parts, relay, plus, minus):
        place = self.place
        at = lambda step: place.off(axis, step)
        far = []
        for p, way in parts:
            far.append(self.send(view(at(2), p), relay(p), axis + ("+" if way > 0 else "-"), relay(p)))
        yield
        ups, downs = [], []
        for (p, way), link in zip(parts, far):
            link.arrive()
            add_to(view(at(way), p), relay(p))
            if way > 0:
                ups.append(self.send(view(at(1), p), plus(p), axis + "+", plus(p)))
            else:
                downs.append(self.send(view(at(-1), p), minus(p), axis + "-", minus(p)))
        for p, way in parts:
            if way > 0:
                downs.append(self.send(view(at(-1), p), minus(p), axis + "-", minus(p)))
            else:
                ups.append(self.send(view(at(1), p), plus(p), axis + "+", plus(p)))
        yield
        for link in ups + downs:
            link.arrive()
        for p, _ in parts:
            add_to(view(at(0), p), plus(p), minus(p))


def add_to(ref, *others):
    total = ref[...].astype(F32)
    for other in others:
        total = total + other[...].astype(F32)
    ref[...] = total.astype(ref.dtype)


def drain(task):
    for _ in task:
        pass


def rows(lo, hi):
    return pl.ds(lo, hi - lo)
T = 544
CH = 4


def halves(n):
    return [(rows(0, n // 2), 1), (rows(n // 2, n), -1)]


PARTS_8 = [(rows(0, 272), 1), (rows(272, 544), -1)]
PARTS_A = [(rows(0, 144), 1), (rows(144, 272), -1)]
PARTS_B = [(rows(272, 416), 1), (rows(416, 544), -1)]
PEERS = ("y+", "y-", "z2", "sib", "x+", "x-", "z+", "z-")


def wide_gather(comm, out, own, give, n):
    place = comm.place
    core = place.core
    copy = comm.local(own, out.at[place.y, place.zh, core])
    task = comm.pair_ring_gather(
        "z2", "y", lambda k, j, p: out.at[k, j, core, p], halves(n),
        lambda p: own.at[p], give, slice(None))
    yield from task
    copy.wait()
    link = comm.send(out.at[:, :, core], out.at[:, :, core], "sib", out.at[:, :, 1 - core])
    yield
    link.arrive()


def block_gather(comm, out, own, parts):
    place = comm.place
    copy = comm.local(own, out.at[place.x, place.zl])
    yield from comm.pair_ring_gather(
        "zl", "x", lambda k, j, p: out.at[k, j, p], parts, lambda p: own.at[p], own, slice(None))
    copy.wait()


def plane_spread(comm, out, own):
    place = comm.place
    copy = comm.local(own, out.at[place.x, place.z])
    copy.wait()
    yield from comm.plane_gather(lambda k, j, p: out.at[k, j, p], PARTS_A, PARTS_B)


def run(tasks):
    tasks = list(tasks)
    while tasks:
        left = []
        for task in tasks:
            try:
                next(task)
                left.append(task)
            except StopIteration:
                pass
        tasks = left


def gather_kernel(wf, wfa, wq, wqa, kvs, xb, cb, gb, out_f, out_fa, out_q, out_qa, out_kv, out_kva, out_x, out_c, out_g,
                  kv8, kvf, send_sems, recv_sems, local_sems):
    comm = Comm(send_sems, recv_sems, local_sems)
    place = comm.place
    comm.enter(PEERS)
    zh = place.zh
    every = slice(None)

    def kv_task():
        yield from block_gather(comm, kv8, kvs, halves(192))
        total = jnp.zeros((192, 512), F32)
        for n in range(8):
            lane = lax.broadcasted_iota(jnp.int32, (128, 512), 0)
            col = lax.broadcasted_iota(jnp.int32, (128, 512), 1)
            pick = ((lane < 32) & (col == 32 * n + lane)) | ((lane >= 32) & (lane < 64) & (col == 224 + 32 * n + lane))
            total = total + jnp.dot(kv8[n // 2, n % 2], pick.astype(F32).astype(BF), preferred_element_type=F32)
        kvf[...] = total.astype(BF)
        a, b = kvf.at[0:128], kvf.at[128:192]
        one = wide_gather(comm, out_kv, a, a, 128)
        two = wide_gather(comm, out_kva, b, b, 64)
        for _ in one:
            next(two, None)
            yield
        drain(two)

    tasks = [
        block_gather(comm, out_x, xb, PARTS_8),
        block_gather(comm, out_g, gb, [(slice(None), 1)]),
        kv_task(),
        wide_gather(comm, out_q, wq, wq, 128),
        wide_gather(comm, out_qa, wqa, wqa, 64),
        wide_gather(comm, out_fa, wfa.at[zh], wfa.at[1 - zh], 64),
    ]
    for i in range(CH):
        tasks.append(wide_gather(comm, out_f.at[i], wf.at[zh, i], wf.at[1 - zh, i], 128))
    tasks.append(plane_spread(comm, out_c, cb))
    run(tasks)
    comm.close()


def gather_all(wf, wfa, wq, wqa, kvs, xb, cb, gb):
    any_ = pl.BlockSpec(memory_space=pl.ANY)
    vm = pl.BlockSpec(memory_space=pltpu.VMEM)
    shapes = [(CH, 4, 2, 2, 128, 768), (4, 2, 2, 64, 768), (4, 2, 2, 128, 512), (4, 2, 2, 64, 512),
              (4, 2, 2, 128, 512), (4, 2, 2, 64, 512), (4, 2, T, 256), (4, 4, T, 256)]
    return pl.pallas_call(
        gather_kernel,
        out_shape=[jax.ShapeDtypeStruct(s, BF) for s in shapes] + [jax.ShapeDtypeStruct((4, 2, 8, 256), F32)],
        in_specs=[any_] * 8,
        out_specs=[any_] * 9,
        scratch_shapes=[pltpu.VMEM((4, 2, 192, 128), BF), pltpu.VMEM((192, 512), BF),
                        pltpu.SemaphoreType.DMA((SEMS,)), pltpu.SemaphoreType.DMA((SEMS,)), pltpu.SemaphoreType.DMA((32,))],
        compiler_params=pltpu.CompilerParams(collective_id=0, has_side_effects=True, vmem_limit_bytes=VMEM_CAP),
    )(wf, wfa, wq, wqa, kvs, xb, cb, gb)


def pack_hidden(gate, up, down):
    n, hidden = gate.shape
    cut = lambda m: m.reshape(n, 2, hidden // 512, 256)
    return jnp.concatenate([cut(gate), cut(up), cut(down.T)], axis=-1).transpose(1, 2, 0, 3)


def pack_tokens(pre, act):
    low = jnp.concatenate([act[0], act[1]], axis=1)
    low = jnp.pad(low, ((0, 14), (0, 0)))
    return jnp.concatenate([pre.reshape(480, 256), low], axis=0).astype(BF)
def whole(ref):
    return ref


def loop_add(ref, n, *others):
    def step(i, carry):
        add_to(ref.at[i], *[other.at[i] for other in others])
        return carry
    lax.fori_loop(0, n, step, 0)


def pair_ring_sum(comm, pair, axis, view, parts, lands, swap):
    relay, plus, minus = lands
    yield from comm.ring_sum(axis, view, parts, lambda p: relay.at[:, p], lambda p: plus.at[:, p], lambda p: minus.at[:, p])


def block_sum(comm, blocks, lands, swap):
    place = comm.place
    relay, plus, minus = lands
    yield from comm.ring_sum(
        "x", lambda k, p: blocks.at[k, :, p], PARTS_8,
        lambda p: relay.at[:, p], lambda p: plus.at[:, p], lambda p: minus.at[:, p])
    link = comm.send(blocks.at[place.x, 1 - place.zl], swap, "zl", swap)
    yield
    link.arrive()
    add_to(blocks.at[place.x, place.zl], swap)


def plane_sum(comm, blocks, lands_far, lands_near):
    place = comm.place
    az = comm.ring_sum("z", lambda k, p: blocks.at[:, k, p], PARTS_A,
                       lambda p: lands_far.at[0, :, p], lambda p: lands_far.at[1, :, p], lambda p: lands_far.at[2, :, p])
    bx = comm.ring_sum("x", lambda k, p: blocks.at[k, :, p], PARTS_B,
                       lambda p: lands_far.at[0, :, p], lambda p: lands_far.at[1, :, p], lambda p: lands_far.at[2, :, p])
    next(az), next(bx)
    yield
    next(az), next(bx)
    yield
    drain(az)
    ax = comm.ring_sum("x", lambda k, p: blocks.at[k, place.z, p], PARTS_A,
                       lambda p: lands_near.at[0, p], lambda p: lands_near.at[1, p], lambda p: lands_near.at[2, p])
    next(ax)
    drain(bx)
    bz = comm.ring_sum("z", lambda k, p: blocks.at[place.x, k, p], PARTS_B,
                       lambda p: lands_near.at[0, p], lambda p: lands_near.at[1, p], lambda p: lands_near.at[2, p])
    next(bz)
    yield
    next(ax), next(bz)
    yield
    drain(ax), drain(bz)


def wide_sum(comm, grad, half, relay, plus, minus, swap, n, add):
    place = comm.place
    core, zh = place.core, place.zh
    link = comm.send(grad.at[1 - core], half, "sib", half)
    yield
    link.arrive()
    loop_add(grad.at[core], 4, half)
    yield from comm.ring_sum(
        "y", lambda k, p: grad.at[core, k, :, p], halves(n),
        lambda p: relay.at[:, p], lambda p: plus.at[:, p], lambda p: minus.at[:, p])
    link = comm.send(grad.at[core, place.y, 1 - zh], swap, "z2", swap)
    yield
    link.arrive()
    if add:
        add_to(grad.at[core, place.y, zh], swap)


SEM_SCRATCH = [pltpu.SemaphoreType.DMA((SEMS,)), pltpu.SemaphoreType.DMA((SEMS,)), pltpu.SemaphoreType.DMA((32,))]
ANY = pl.BlockSpec(memory_space=pl.ANY)


def call(kernel, shapes, scratch, ident, *args):
    return pl.pallas_call(
        kernel,
        out_shape=[jax.ShapeDtypeStruct(s, d) for s, d in shapes],
        in_specs=[ANY] * len(args),
        out_specs=[ANY] * len(shapes),
        scratch_shapes=list(scratch) + SEM_SCRATCH,
        compiler_params=pltpu.CompilerParams(collective_id=ident, has_side_effects=True, vmem_limit_bytes=VMEM_CAP),
    )(*args)


LAND_8 = [pltpu.VMEM((2, T, 256), BF)] * 3 + [pltpu.VMEM((T, 256), BF)]


def hidden_kernel(terms, xb, out_h, out_full, blocks, xv, hv, full, r0, r1, r2, r3, *sems):
    comm = Comm(*sems)
    place = comm.place
    one, two = comm.local(terms, blocks), comm.local(xb, xv)
    comm.enter(PEERS)
    one.wait(), two.wait()
    drain(block_sum(comm, blocks, (r0, r1, r2), r3))
    hv[...] = xv[...].astype(F32) + blocks[place.x, place.zl].astype(F32)
    three = comm.local(hv, out_h)
    full[place.x, place.z] = hv[...].astype(BF)
    drain(comm.plane_gather(lambda k, j, p: full.at[k, j, p], PARTS_A, PARTS_B))
    four = comm.local(full, out_full)
    three.wait(), four.wait()
    comm.close()


def hidden_exchange(terms, xb):
    return call(hidden_kernel, [((T, 256), F32), ((4, 4, T, 256), BF)],
                [pltpu.VMEM((4, 2, T, 256), BF), pltpu.VMEM((T, 256), BF), pltpu.VMEM((T, 256), F32),
                 pltpu.VMEM((4, 4, T, 256), BF)] + LAND_8, 1, terms, xb)


LAND_16 = [pltpu.VMEM((3, 4, T, 256), BF), pltpu.VMEM((3, T, 256), BF)]


def feed_kernel(back, down, out_b, out_y, bb, yb, full, bf, bn, yf, yn, *sems):
    comm = Comm(*sems)
    place = comm.place
    one, two = comm.local(back, bb), comm.local(down, yb)
    comm.enter(PEERS)
    one.wait(), two.wait()
    run([plane_sum(comm, bb, bf, bn), plane_sum(comm, yb, yf, yn)])
    full[place.x, place.zl] = bb[place.x, place.z]
    three = comm.local(yb.at[place.x, place.z], out_y)
    drain(comm.pair_ring_gather("zl", "x", lambda k, j, p: full.at[k, j, p], PARTS_8,
                                lambda p: full.at[place.x, place.zl, p], full.at[place.x, place.zl], slice(None)))
    four = comm.local(full, out_b)
    three.wait(), four.wait()
    comm.close()


def feed_exchange(back, down):
    return call(feed_kernel, [((4, 2, T, 256), BF), ((T, 256), BF)],
                [pltpu.VMEM((4, 4, T, 256), BF)] * 2 + [pltpu.VMEM((4, 2, T, 256), BF)] + LAND_16 * 2, 2, back, down)


def sum_scratch(n, c):
    return [pltpu.VMEM((2, 4, 2, n, c), BF), pltpu.VMEM((4, 2, n, c), BF)] + [pltpu.VMEM((2, n, c), BF)] * 3 + [pltpu.VMEM((n, c), BF)]


PIECES = [(128, 768)] * CH + [(64, 768), (128, 512), (128, 512), (64, 512), (64, 512)]


def sum_kernel(*refs):
    count = len(PIECES)
    ins, terms = refs[:count], refs[count]
    outs, out_t = refs[count + 1:2 * count + 1], refs[2 * count + 1]
    scratch = refs[2 * count + 2:]
    comm = Comm(*scratch[-3:])
    place = comm.place
    blocks, r0, r1, r2, r3 = scratch[6 * count:6 * count + 5]
    copies = [comm.local(terms, blocks)]
    sets = [scratch[6 * i:6 * i + 6] for i in range(count)]
    for i in range(count):
        copies.append(comm.local(ins[i], sets[i][0]))
    comm.enter(PEERS)
    for copy in copies:
        copy.wait()
    tasks = [wide_sum(comm, *sets[i], PIECES[i][0], i > CH) for i in range(count)]
    run(tasks + [block_sum(comm, blocks, (r0, r1, r2), r3)])
    copies = [comm.local(blocks.at[place.x, place.zl], out_t)]
    for i in range(count):
        own = sets[i][0].at[place.core, place.y, place.zh]
        if i > CH:
            copies.append(comm.local(own, outs[i]))
        else:
            copies.append(comm.local(own, outs[i].at[place.zh]))
            copies.append(comm.local(sets[i][5], outs[i].at[1 - place.zh]))
    for copy in copies:
        copy.wait()
    comm.close()


def sum_exchange(grads, terms):
    shapes = [((n, c) if i > CH else (2, n, c), BF) for i, (n, c) in enumerate(PIECES)] + [((T, 256), BF)]
    scratch = []
    for n, c in PIECES:
        scratch += sum_scratch(n, c)
    scratch += [pltpu.VMEM((4, 2, T, 256), BF)] + LAND_8
    return call(sum_kernel, shapes, scratch, 3, *grads, terms)
EPSILON = 1e-06
MASKED = -1000000000.0


def dot(a, b, ca, cb):
    return lax.dot_general(a, b, (((ca,), (cb,)), ((), ())), preferred_element_type=F32)


def unblock(blocks):
    both = blocks.reshape(8, T, 256)
    pre = both[:, :480].transpose(1, 0, 2).reshape(480, 2048)
    act = both[:, 480:].reshape(8, 64, 2, 128).transpose(2, 1, 0, 3).reshape(128, 1024)
    return pre, act


def unblock16(full):
    pairs = [unblock(full[:, 2 * zh:2 * zh + 2]) for zh in range(2)]
    return jnp.concatenate([p for p, _ in pairs]), jnp.concatenate([a for _, a in pairs])


def block(pre, act):
    low = act.reshape(2, 64, 8, 128).transpose(2, 1, 0, 3).reshape(8, 64, 256)
    top = pre.reshape(480, 8, 256).transpose(1, 0, 2)
    return jnp.concatenate([top, low], axis=1).reshape(4, 2, T, 256)


def block16(pre, act):
    parts = [block(pre[480 * zh:480 * zh + 480], act[128 * zh:128 * zh + 128]) for zh in range(2)]
    return jnp.concatenate(parts, axis=1)


def inv(v):
    return lax.rsqrt(jnp.mean(v * v, axis=1, keepdims=True) + EPSILON)


def norm_back(grad, gain, unit, scale):
    inner = grad * gain
    return scale * (inner - unit * jnp.mean(inner * unit, axis=1, keepdims=True))


def gelu_parts(z):
    a, b = 0.7978845608028654, 0.044715
    t = jnp.tanh(a * (z + b * z * z * z))
    half = 0.5 * (1.0 + t)
    return z * half, half + 0.5 * z * (1.0 - t * t) * a * (1.0 + 3.0 * b * z * z)


def seen(length):
    s = lax.broadcasted_iota(jnp.int32, (304, 304), 0)
    t = lax.broadcasted_iota(jnp.int32, (304, 304), 1)
    live = (t < 192) | ((t >= 240) & (t < 290)) | (t - 192 < length)
    return live & ((t < 240) | (s >= 240))


def soft(q, k, length):
    scores = dot(q, k, 1, 1) * 0.0625
    scores = jnp.where(seen(length), scores, MASKED)
    weights = jnp.exp(scores - jnp.max(scores, axis=1, keepdims=True))
    return weights / jnp.sum(weights, axis=1, keepdims=True)


def hidden_unit(n2, gc, w):
    gate, up, dact = dot(n2, w[:, :256], 1, 0), dot(n2, w[:, 256:512], 1, 0), dot(gc, w[:, 512:], 1, 0)
    value, slope = gelu_parts(gate)
    return (value * up).astype(BF), (dact * up * slope).astype(BF), (dact * value).astype(BF)


def by_core(grad):
    n = grad.shape[0] // 16
    return grad.astype(BF).reshape(4, 2, 2, n, grad.shape[1]).transpose(2, 0, 1, 3, 4)


def local(x_pre, x_act, lengths, cot_pre, cot_act, attn_gain_pre, query_pre, key_pre, value_pre, out_pre, ffn_gain_pre,
          gate_pre, up_pre, down_pre, attn_gain_act, query_act, key_act, value_act, out_act, ffn_gain_act, gate_act,
          up_act, down_act):
    wf, wfa = pack_hidden(gate_pre, up_pre, down_pre), pack_hidden(gate_act, up_act, down_act)[:, 0]
    wq, wqa = jnp.concatenate([query_pre, out_pre.T], axis=1), jnp.concatenate([query_act, out_act.T], axis=1)
    kvs = jnp.concatenate([jnp.concatenate([key_pre, value_pre], axis=1), jnp.concatenate([key_act, value_act], axis=1)])
    kvs = jnp.pad(kvs, ((0, 0), (0, 64)))
    xb, cb = pack_tokens(x_pre, x_act), pack_tokens(cot_pre, cot_act)
    gb = jnp.pad(jnp.stack([attn_gain_pre, ffn_gain_pre, jnp.concatenate([attn_gain_act, ffn_gain_act])]), ((0, 5), (0, 0)))
    f, fa, qo, qoa, kv, kva, x8, c16, g8 = gather_all(wf, wfa, wq, wqa, kvs, xb, cb, gb)
    f, fa = f.reshape(CH, 2048, 768), fa.reshape(1024, 768)
    qo, qoa, kv, kva = qo.reshape(2048, 512), qoa.reshape(1024, 512), kv.reshape(2048, 512), kva.reshape(1024, 512)
    g8 = g8.reshape(8, 8, 256)
    gains = g8[:, 0].reshape(2048), g8[:, 1].reshape(2048), g8[:, 2, :128].reshape(1024), g8[:, 2, 128:].reshape(1024)
    zh = lax.rem(lax.div(lax.axis_index("wide"), 2), 2)
    xp, xa = unblock(x8.astype(F32))
    r1p, r1a = inv(xp), inv(xa)
    u1p, u1a = xp * r1p, xa * r1a
    n1p, n1a = (u1p * gains[0]).astype(BF), (u1a * gains[2]).astype(BF)
    def items(pre, act):
        return [jnp.concatenate([pre[240 * i:240 * i + 240], act[64 * i:64 * i + 64]]) for i in range(2)]
    def split(pair):
        return jnp.concatenate([v[:240] for v in pair]), jnp.concatenate([v[240:] for v in pair])
    q = items(dot(n1p, qo[:, :256], 1, 0).astype(BF), dot(n1a, qoa[:, :256], 1, 0).astype(BF))
    k = items(dot(n1p, kv[:, :256], 1, 0).astype(BF), dot(n1a, kva[:, :256], 1, 0).astype(BF))
    v = items(dot(n1p, kv[:, 256:], 1, 0).astype(BF), dot(n1a, kva[:, 256:], 1, 0).astype(BF))
    probs = [soft(q[i], k[i], lengths[i]) for i in range(2)]
    op, oa = split([dot(probs[i].astype(BF), v[i], 1, 0).astype(BF) for i in range(2)])
    terms = block(dot(op, qo[:, 256:], 1, 1).astype(BF), dot(oa, qoa[:, 256:], 1, 1).astype(BF))
    h_own, h16 = hidden_exchange(terms, xb)
    hp, ha = unblock16(h16.astype(F32))
    r2p, r2a = inv(hp), inv(ha)
    n2p, n2a = (hp * r2p * gains[1]).astype(BF), (ha * r2a * gains[3]).astype(BF)
    gcp, gca = unblock16(c16)
    units = [hidden_unit(n2p, gcp, f[i]) for i in range(CH)]
    ua = hidden_unit(n2a, gca, fa)
    down = sum(dot(units[i][0], f[i, :, 512:], 1, 1) for i in range(CH))
    back = sum(dot(units[i][1], f[i, :, :256], 1, 1) + dot(units[i][2], f[i, :, 256:512], 1, 1) for i in range(CH))
    down_a = dot(ua[0], fa[:, 512:], 1, 1)
    back_a = dot(ua[1], fa[:, :256], 1, 1) + dot(ua[2], fa[:, 256:512], 1, 1)
    b8, y_add = feed_exchange(block16(back.astype(BF), back_a.astype(BF)), block16(down.astype(BF), down_a.astype(BF)))
    grads = [jnp.concatenate([dot(n2p, u[1], 0, 0), dot(n2p, u[2], 0, 0), dot(gcp, u[0], 0, 0)], axis=1) for u in units]
    grads.append(jnp.concatenate([dot(n2a, ua[1], 0, 0), dot(n2a, ua[2], 0, 0), dot(gca, ua[0], 0, 0)], axis=1))
    own = lambda m: lax.dynamic_slice_in_dim(m, zh * (m.shape[0] // 2), m.shape[0] // 2, 0)
    bp, ba = unblock(b8.astype(F32))
    hp, ha, r2p, r2a = own(hp), own(ha), own(r2p), own(r2a)
    dhp = own(gcp).astype(F32) + norm_back(bp, gains[1], hp * r2p, r2p)
    dha = own(gca).astype(F32) + norm_back(ba, gains[3], ha * r2a, r2a)
    ghp, gha = dhp.astype(BF), dha.astype(BF)
    dop, doa = dot(ghp, qo[:, 256:], 1, 0).astype(BF), dot(gha, qoa[:, 256:], 1, 0).astype(BF)
    do = items(dop, doa)
    dq, dk, dv = [], [], []
    for i in range(2):
        low = probs[i].astype(BF)
        dprobs = dot(do[i], v[i], 1, 1)
        dscores = (probs[i] * (dprobs - jnp.sum(probs[i] * dprobs, axis=1, keepdims=True))).astype(BF)
        dq.append((dot(dscores, k[i], 1, 0) * 0.0625).astype(BF))
        dk.append((dot(dscores, q[i], 0, 0) * 0.0625).astype(BF))
        dv.append(dot(low, do[i], 0, 0).astype(BF))
    (dqp, dqa), (dkp, dka), (dvp, dva) = split(dq), split(dk), split(dv)
    grads.append(jnp.concatenate([dot(n1p, dqp, 0, 0), dot(ghp, op, 0, 0)], axis=1))
    grads.append(jnp.concatenate([dot(n1p, dkp, 0, 0), dot(n1p, dvp, 0, 0)], axis=1))
    grads.append(jnp.concatenate([dot(n1a, dqa, 0, 0), dot(gha, oa, 0, 0)], axis=1))
    grads.append(jnp.concatenate([dot(n1a, dka, 0, 0), dot(n1a, dva, 0, 0)], axis=1))
    dn1p = dot(dqp, qo[:, :256], 1, 1) + dot(dkp, kv[:, :256], 1, 1) + dot(dvp, kv[:, 256:], 1, 1)
    dn1a = dot(dqa, qoa[:, :256], 1, 1) + dot(dka, kva[:, :256], 1, 1) + dot(dva, kva[:, 256:], 1, 1)
    *sums, d1 = sum_exchange([by_core(g) for g in grads], block(dn1p.astype(BF), dn1a.astype(BF)))
    narrow = lax.axis_index("narrow")
    def slab(pre, act):
        p = lax.dynamic_slice_in_dim(pre, narrow * 256, 256, 1)
        a = lax.dynamic_slice_in_dim(act, narrow * 128, 128, 1)
        return p, a
    d1p, d1a = d1[:480].astype(F32), d1[480:].astype(F32).reshape(64, 2, 128).transpose(1, 0, 2).reshape(128, 128)
    xps, xas = slab(u1p, u1a)
    dhps, dhas = slab(dhp - own(gcp).astype(F32), dha - own(gca).astype(F32))
    dhps = dhps + cot_pre.reshape(480, 256)
    dhas = dhas + jnp.pad(cot_act, ((0, 0), (0, 14), (0, 0))).reshape(128, 128)
    innp, inna = d1p * attn_gain_pre, d1a * attn_gain_act
    meanp, meana = lax.psum((jnp.sum(innp * xps, axis=1, keepdims=True), jnp.sum(inna * xas, axis=1, keepdims=True)), "narrow")
    gxp = dhps + r1p * (innp - xps * (meanp / 2048))
    gxa = dhas + r1a * (inna - xas * (meana / 1024))
    u2ps, u2as = slab(hp * r2p, ha * r2a)
    b2ps, b2as = slab(bp, ba)
    gg = lax.psum((jnp.sum(d1p * xps, axis=0), jnp.sum(b2ps * u2ps, axis=0), jnp.sum(d1a * xas, axis=0), jnp.sum(b2as * u2as, axis=0)), "wide")
    y = h_own + y_add.astype(F32)
    unact = lambda m: m.reshape(64, 2, 128)[:50].transpose(1, 0, 2)
    yp, ya = y[:480].reshape(2, 240, 256).astype(BF), unact(y[480:]).astype(BF)
    def open_hidden(m, n):
        m = m.astype(F32).reshape(2, -1, n, 768).transpose(2, 0, 1, 3)
        gate, up, down = (m[..., 256 * j:256 * j + 256].reshape(n, -1) for j in range(3))
        return gate, up, down.T
    fg = jnp.stack(sums[:CH], axis=1)
    dgate_p, dup_p, ddown_p = open_hidden(fg, 128)
    dgate_a, dup_a, ddown_a = open_hidden(sums[CH], 64)
    qp, kvp, qa, kva_ = (m.astype(F32) for m in sums[CH + 1:CH + 5])
    def kv_share(a, b):
        both = jnp.concatenate([a, b])
        both = both.reshape(192, 2, 8, 32).astype(BF)
        s = lax.psum_scatter(both, "narrow", scatter_dimension=2).astype(F32)
        return s[:128, 0], s[:128, 1], s[128:, 0], s[128:, 1]
    dkey_p, dval_p, dkey_a, dval_a = kv_share(kvp, kva_)
    return (yp, ya, gxp.reshape(2, 240, 256), gxa.reshape(2, 64, 128)[:, :50], gg[0], qp[:, :256], dkey_p, dval_p,
            qp[:, 256:].T, gg[1], dgate_p, dup_p, ddown_p, gg[2], qa[:, :256], dkey_a, dval_a, qa[:, 256:].T, gg[3],
            dgate_a, dup_a, ddown_a)


def solution(mesh):
    tok, row, col, vec = P("wide", None, "narrow"), P("wide", "narrow"), P("narrow", "wide"), P("narrow")
    expert = (vec, row, row, row, col, vec, row, row, col)
    return jax.shard_map(
        local, mesh=mesh, in_specs=(tok, tok, P("wide"), tok, tok) + expert + expert,
        out_specs=(tok,) * 4 + expert + expert, check_vma=False)
```

```python
import functools
import jax
import jax.numpy as jnp
from jax import lax
from jax.experimental import pallas as pl
from jax.experimental.pallas import tpu as pltpu
from jax.sharding import PartitionSpec as P

MESH = pl.DeviceIdType.MESH
BF = jnp.bfloat16
F32 = jnp.float32
SEMS = 256
VMEM_CAP = 62 * 1024 * 1024


class Place:
    def __init__(self):
        wide, narrow = lax.axis_index("wide"), lax.axis_index("narrow")
        self.core = lax.rem(wide, 2)
        self.zh = lax.rem(lax.div(wide, 2), 2)
        self.y = lax.div(wide, 4)
        self.zl = lax.rem(narrow, 2)
        self.x = lax.div(narrow, 2)
        self.z = self.zh * 2 + self.zl

    def wide_at(self, y, zh, core):
        return (y * 2 + zh) * 2 + core

    def coord(self, axis):
        return {"x": self.x, "y": self.y, "z": self.z}[axis]

    def off(self, axis, step):
        return lax.rem(self.coord(axis) + step + 4, 4)

    def peer(self, name):
        if name == "sib":
            return {"wide": self.wide_at(self.y, self.zh, 1 - self.core)}
        if name == "z2":
            return {"wide": self.wide_at(self.y, 1 - self.zh, self.core)}
        if name == "zl":
            return {"narrow": self.x * 2 + 1 - self.zl}
        axis, step = name[0], 1 if name[1] == "+" else -1
        at = self.off(axis, step)
        if axis == "y":
            return {"wide": self.wide_at(at, self.zh, self.core)}
        if axis == "x":
            return {"narrow": at * 2 + self.zl}
        return {"wide": self.wide_at(self.y, lax.div(at, 2), self.core), "narrow": self.x * 2 + lax.rem(at, 2)}


class Link:
    def __init__(self, out, into):
        self.out, self.into = out, into

    def arrive(self):
        self.into.wait_recv()

    def left(self):
        self.out.wait_send()


class Comm:
    def __init__(self, send_sems, recv_sems, local_sems):
        self.place = Place()
        self.send_sems, self.recv_sems, self.local_sems = send_sems, recv_sems, local_sems
        self.count, self.local_count = 0, 0
        self.links = []

    def enter(self, peers):
        barrier = pltpu.get_barrier_semaphore()
        for name in peers:
            pl.semaphore_signal(barrier, inc=1, device_id=self.place.peer(name), device_id_type=MESH)
        pl.semaphore_wait(barrier, len(peers))

    def send(self, src, dst, name, incoming):
        index = self.count
        self.count += 1
        make = lambda to: pltpu.make_async_remote_copy(
            src_ref=src, dst_ref=to, send_sem=self.send_sems.at[index], recv_sem=self.recv_sems.at[index],
            device_id=self.place.peer(name), device_id_type=MESH)
        out = make(dst)
        out.start()
        link = Link(out, make(incoming))
        self.links.append(link)
        return link

    def local(self, src, dst):
        index = self.local_count
        self.local_count += 1
        copy = pltpu.make_async_copy(src, dst, self.local_sems.at[index])
        copy.start()
        return copy

    def settle(self):
        for link in self.links:
            link.left()
        self.links = []

    def close(self):
        self.settle()

    def ring_gather(self, axis, view, parts, own=None):
        place = self.place
        at = lambda step: place.off(axis, step)
        src = own if own is not None else (lambda part: view(at(0), part))
        plus = [self.send(src(p), view(at(0), p), axis + "+", view(at(-1), p)) for p, _ in parts]
        minus = [self.send(src(p), view(at(0), p), axis + "-", view(at(1), p)) for p, _ in parts]
        yield
        far = []
        for (p, way), up in zip(parts, plus):
            up.arrive()
            if way > 0:
                far.append(self.send(view(at(-1), p), view(at(-1), p), axis + "+", view(at(-2), p)))
        for (p, way), down in zip(parts, minus):
            down.arrive()
            if way < 0:
                far.append(self.send(view(at(1), p), view(at(1), p), axis + "-", view(at(2), p)))
        yield
        for link in far:
            link.arrive()

    def pair_ring_gather(self, pair, axis, view, parts, own, give, whole):
        place = self.place
        mine = {"z2": place.zh, "zl": place.zl}[pair]
        here = place.coord(axis)
        swap = self.send(give, view(here, mine, whole), pair, view(here, 1 - mine, whole))
        first = self.ring_gather(axis, lambda k, p: view(k, mine, p), parts, own)
        next(first)
        yield
        swap.arrive()
        second = self.ring_gather(axis, lambda k, p: view(k, 1 - mine, p), parts)
        next(second)
        yield
        next(first)
        yield
        next(second)
        yield
        drain(first)
        drain(second)

    def plane_gather(self, view, parts_x, parts_z):
        place = self.place
        every = slice(None)
        ax = self.ring_gather("x", lambda k, p: view(k, place.z, p), parts_x)
        bz = self.ring_gather("z", lambda k, p: view(place.x, k, p), parts_z)
        next(ax), next(bz)
        yield
        next(ax), next(bz)
        yield
        drain(ax)
        az = self.ring_gather("z", lambda k, p: view(every, k, p), parts_x)
        next(az)
        drain(bz)
        bx = self.ring_gather("x", lambda k, p: view(k, every, p), parts_z)
        next(bx)
        yield
        next(az), next(bx)
        yield
        drain(az), drain(bx)

    def ring_sum(self, axis, view, parts, relay, plus, minus):
        place = self.place
        at = lambda step: place.off(axis, step)
        far = []
        for p, way in parts:
            far.append(self.send(view(at(2), p), relay(p), axis + ("+" if way > 0 else "-"), relay(p)))
        yield
        ups, downs = [], []
        for (p, way), link in zip(parts, far):
            link.arrive()
            add_to(view(at(way), p), relay(p))
            if way > 0:
                ups.append(self.send(view(at(1), p), plus(p), axis + "+", plus(p)))
            else:
                downs.append(self.send(view(at(-1), p), minus(p), axis + "-", minus(p)))
        for p, way in parts:
            if way > 0:
                downs.append(self.send(view(at(-1), p), minus(p), axis + "-", minus(p)))
            else:
                ups.append(self.send(view(at(1), p), plus(p), axis + "+", plus(p)))
        yield
        for link in ups + downs:
            link.arrive()
        for p, _ in parts:
            add_to(view(at(0), p), plus(p), minus(p))


def add_to(ref, *others):
    total = ref[...].astype(F32)
    for other in others:
        total = total + other[...].astype(F32)
    ref[...] = total.astype(ref.dtype)


def drain(task):
    for _ in task:
        pass


def rows(lo, hi):
    return pl.ds(lo, hi - lo)
T = 544
CH = 4


def halves(n):
    return [(rows(0, n // 2), 1), (rows(n // 2, n), -1)]


PARTS_8 = [(rows(0, 272), 1), (rows(272, 544), -1)]
PARTS_A = [(rows(0, 144), 1), (rows(144, 272), -1)]
PARTS_B = [(rows(272, 416), 1), (rows(416, 544), -1)]
PEERS = ("y+", "y-", "z2", "sib", "x+", "x-", "z+", "z-")


def wide_gather(comm, out, own, give, n, parts=None):
    place = comm.place
    core = place.core
    copy = comm.local(own, out.at[place.y, place.zh, core])
    task = comm.pair_ring_gather(
        "z2", "y", lambda k, j, p: out.at[k, j, core, p], parts or halves(n),
        lambda p: own.at[p], give, slice(None))
    yield from task
    copy.wait()
    link = comm.send(out.at[:, :, core], out.at[:, :, core], "sib", out.at[:, :, 1 - core])
    yield
    link.arrive()


def block_gather(comm, out, own, parts):
    place = comm.place
    copy = comm.local(own, out.at[place.x, place.zl])
    yield from comm.pair_ring_gather(
        "zl", "x", lambda k, j, p: out.at[k, j, p], parts, lambda p: own.at[p], own, slice(None))
    copy.wait()


def plane_spread(comm, out, own):
    place = comm.place
    copy = comm.local(own, out.at[place.x, place.z])
    copy.wait()
    yield from comm.plane_gather(lambda k, j, p: out.at[k, j, p], PARTS_A, PARTS_B)


def pack_hidden(gate, up, down):
    n, hidden = gate.shape
    cut = lambda m: m.reshape(n, 2, hidden // 512, 256)
    return jnp.concatenate([cut(gate), cut(up), cut(down.T)], axis=-1).transpose(1, 2, 0, 3)


def pack_tokens(pre, act):
    low = jnp.concatenate([act[0], act[1]], axis=1)
    low = jnp.pad(low, ((0, 14), (0, 0)))
    return jnp.concatenate([pre.reshape(480, 256), low], axis=0)
def loop_add(ref, n, *others):
    def step(i, carry):
        add_to(ref.at[i], *[other.at[i] for other in others])
        return carry
    lax.fori_loop(0, n, step, 0)


def block_sum(comm, blocks, lands, swap, parts=PARTS_8):
    place = comm.place
    relay, plus, minus = lands
    yield from comm.ring_sum(
        "x", lambda k, p: blocks.at[k, :, p], parts,
        lambda p: relay.at[:, p], lambda p: plus.at[:, p], lambda p: minus.at[:, p])
    link = comm.send(blocks.at[place.x, 1 - place.zl], swap, "zl", swap)
    yield
    link.arrive()
    add_to(blocks.at[place.x, place.zl], swap)


def plane_sum(comm, blocks, lands_far, lands_near):
    place = comm.place
    az = comm.ring_sum("z", lambda k, p: blocks.at[:, k, p], PARTS_A,
                       lambda p: lands_far.at[0, :, p], lambda p: lands_far.at[1, :, p], lambda p: lands_far.at[2, :, p])
    bx = comm.ring_sum("x", lambda k, p: blocks.at[k, :, p], PARTS_B,
                       lambda p: lands_far.at[0, :, p], lambda p: lands_far.at[1, :, p], lambda p: lands_far.at[2, :, p])
    next(az), next(bx)
    yield
    next(az), next(bx)
    yield
    drain(az)
    ax = comm.ring_sum("x", lambda k, p: blocks.at[k, place.z, p], PARTS_A,
                       lambda p: lands_near.at[0, p], lambda p: lands_near.at[1, p], lambda p: lands_near.at[2, p])
    next(ax)
    drain(bx)
    bz = comm.ring_sum("z", lambda k, p: blocks.at[place.x, k, p], PARTS_B,
                       lambda p: lands_near.at[0, p], lambda p: lands_near.at[1, p], lambda p: lands_near.at[2, p])
    next(bz)
    yield
    next(ax), next(bz)
    yield
    drain(ax), drain(bz)


def wide_sum(comm, grad, half, relay, plus, minus, swap, n, add):
    place = comm.place
    core, zh = place.core, place.zh
    link = comm.send(grad.at[1 - core], half, "sib", half)
    yield
    link.arrive()
    loop_add(grad.at[core], 4, half)
    yield from comm.ring_sum(
        "y", lambda k, p: grad.at[core, k, :, p], halves(n),
        lambda p: relay.at[:, p], lambda p: plus.at[:, p], lambda p: minus.at[:, p])
    link = comm.send(grad.at[core, place.y, 1 - zh], swap, "z2", swap)
    yield
    link.arrive()
    if add:
        add_to(grad.at[core, place.y, zh], swap)


SEM_SCRATCH = [pltpu.SemaphoreType.DMA((SEMS,)), pltpu.SemaphoreType.DMA((SEMS,)), pltpu.SemaphoreType.DMA((32,))]
ANY = pl.BlockSpec(memory_space=pl.ANY)


LAND_8 = [pltpu.VMEM((2, T, 256), BF)] * 3 + [pltpu.VMEM((T, 256), BF)]


LAND_16 = [pltpu.VMEM((3, 4, T, 256), BF), pltpu.VMEM((3, T, 256), BF)]


EPSILON = 1e-06
MASKED = -1000000000.0
KEYS = 384


def dot(a, b, ca, cb):
    return lax.dot_general(a, b, (((ca,), (cb,)), ((), ())), preferred_element_type=F32)


_open = []


def mark(name):
    if _open:
        _open.pop().__exit__(None, None, None)
    if name:
        scope = jax.named_scope(name)
        scope.__enter__()
        _open.append(scope)


def pump(*tasks):
    for task in tasks:
        next(task, None)


def seen(length):
    s = lax.broadcasted_iota(jnp.int32, (304, KEYS), 0)
    t = lax.broadcasted_iota(jnp.int32, (304, KEYS), 1)
    live = (t < 192) | ((t >= 240) & (t < 290)) | ((t < 240) & (t - 192 < length))
    return live & ((t < 240) | (s >= 240))


def soft(q, k, length):
    scores = dot(q, k, 1, 1) * 0.0625
    scores = jnp.where(seen(length), scores, MASKED)
    weights = jnp.exp(scores - jnp.max(scores, axis=1, keepdims=True))
    return weights / jnp.sum(weights, axis=1, keepdims=True)


def pairs8():
    return [(x, zl) for x in range(4) for zl in range(2)]


def norm_block_rows(get, gain, width, put):
    total = sum(jnp.sum(get(n) * get(n), axis=1, keepdims=True) for n in range(8))
    scale = lax.rsqrt(total / (8 * width) + EPSILON)
    for n in range(8):
        put(n, (get(n) * scale * gain(n)).astype(BF))
    return scale


def attend_kernel(lens, wf, wfa, wq, wqa, kvs, xb, cb, gb,
                  out_f, out_fa, out_q, out_qa, out_kv, out_kva, out_c, out_g, out_n1p, out_n1a, out_qkvo, out_r1,
                  out_h, out_h16, out_n2p, out_n2a, out_r2,
                  kv8, kvf, qo, qoa, kv, kva, x8, c16, g8, n1p, n1a, qkvo, r1, xv, hv, full, n2p, n2a, r2,
                  blocks, l0, l1, l2, l3, *sems):
    comm = Comm(*sems)
    place = comm.place
    zh = place.zh
    first = comm.local(xb, xv)
    zero = jnp.zeros((KEYS - 304, 256), BF)
    for i in range(2):
        for j in (1, 2):
            qkvo[j, i, 304:KEYS, :] = zero
    comm.enter(PEERS)

    mark('start')
    kv_task = block_gather(comm, kv8, kvs, halves(192))
    g_task = block_gather(comm, g8, gb, [(slice(None), 1)])
    x_task = block_gather(comm, x8, xb, PARTS_8)
    q_tasks = [wide_gather(comm, qo, wq, wq, 128), wide_gather(comm, qoa, wqa, wqa, 64)]
    f_tasks = [wide_gather(comm, out_f.at[i], wf.at[zh, i], wf.at[1 - zh, i], 128) for i in range(CH)]
    f_tasks.append(wide_gather(comm, out_fa, wfa.at[zh], wfa.at[1 - zh], 64))
    c_task = plane_spread(comm, c16, cb)
    pump(kv_task, x_task, *q_tasks, g_task)
    pump(kv_task, g_task), pump(kv_task, g_task), drain(kv_task)
    total = jnp.zeros((192, 512), F32)
    lane = lax.broadcasted_iota(jnp.int32, (128, 512), 0)
    col = lax.broadcasted_iota(jnp.int32, (128, 512), 1)
    for n in range(8):
        pick = ((lane < 32) & (col == 32 * n + lane)) | ((lane >= 32) & (lane < 64) & (col == 224 + 32 * n + lane))
        total = total + dot(kv8[n // 2, n % 2], pick.astype(F32).astype(BF), 1, 0)
    kvf[...] = total.astype(BF)
    kv_a, kv_b = kvf.at[0:128], kvf.at[128:192]
    kv_tasks = [wide_gather(comm, kv, kv_a, kv_a, 128), wide_gather(comm, kva, kv_b, kv_b, 64)]
    pump(*kv_tasks)
    pump(x_task, *q_tasks)
    pump(f_tasks[0], f_tasks[1])
    pump(*kv_tasks)
    pump(*q_tasks)
    pump(x_task)
    pump(*q_tasks)
    pump(*kv_tasks)
    pump(f_tasks[0], f_tasks[2], f_tasks[3], f_tasks[4])
    pump(*q_tasks)
    pump(x_task)
    pump(*kv_tasks)
    mark('xwait')
    drain(g_task)
    drain(x_task)
    pump(c_task)

    mark('norm1')
    for i in range(2):
        here = pl.ds(240 * i, 240)
        get = lambda n: x8[n // 2, n % 2, here, :].astype(F32)
        def put(n, v):
            n1p[here, 256 * n:256 * n + 256] = v
        r1[here, :] = jnp.broadcast_to(norm_block_rows(get, lambda n: g8[n // 2, n % 2, 0:1, :], 256, put), (240, 128))
        low = pl.ds(480, 64)
        get = lambda n: x8[n // 2, n % 2, low, 128 * i:128 * i + 128].astype(F32)
        def put(n, v):
            n1a[64 * i:64 * i + 64, 128 * n:128 * n + 128] = v
        r1[480 + 64 * i:544 + 64 * i, :] = jnp.broadcast_to(
            norm_block_rows(get, lambda n: g8[n // 2, n % 2, 2:3, 0:128], 128, put), (64, 128))
    for task in q_tasks:
        drain(task)
    pump(f_tasks[1])
    mark('qkv')
    def queries(i, carry):
        here = pl.ds(pl.multiple_of(240 * i, 16), 240)
        qkvo[0, i, 0:240, :] = dot(n1p[here, :], qo[:, :, :, :, 0:256].reshape(2048, 256), 1, 0).astype(BF)
        return carry
    lax.fori_loop(0, 2, queries, 0)
    for task in kv_tasks:
        drain(task)
    def keys(i, carry):
        here = pl.ds(pl.multiple_of(240 * i, 16), 240)
        for j in range(2):
            qkvo[1 + j, i, 0:240, :] = dot(
                n1p[here, :], kv[:, :, :, :, 256 * j:256 * j + 256].reshape(2048, 256), 1, 0).astype(BF)
        return carry
    lax.fori_loop(0, 2, keys, 0)
    low = [dot(n1a[...], qoa[:, :, :, :, 0:256].reshape(1024, 256), 1, 0).astype(BF)]
    for j in range(2):
        low.append(dot(n1a[...], kva[:, :, :, :, 256 * j:256 * j + 256].reshape(1024, 256), 1, 0).astype(BF))
    for i in range(2):
        for j in range(3):
            qkvo[j, i, 240:304, :] = low[j][64 * i:64 * i + 64]
    saves = [comm.local(qo, out_q), comm.local(qoa, out_qa), comm.local(kv, out_kv), comm.local(kva, out_kva),
             comm.local(n1p, out_n1p), comm.local(n1a, out_n1a), comm.local(r1, out_r1), comm.local(g8, out_g)]
    pump(c_task, f_tasks[2])
    mark('attn')
    for i in range(2):
        probs = soft(qkvo[0, i, 0:304, :], qkvo[1, i], lens[i])
        qkvo[3, i, 0:304, :] = dot(probs.astype(BF), qkvo[2, i], 1, 0).astype(BF)
    saves.append(comm.local(qkvo, out_qkvo))
    pump(f_tasks[3], f_tasks[0])
    mark('outproj')
    oa = jnp.concatenate([qkvo[3, 0, 240:304, :], qkvo[3, 1, 240:304, :]], axis=0)

    def terms(step):
        k = place.off("x", step)
        for j in range(2):
            weight = qo[k, j, :, :, 256:512].reshape(256, 256)
            for i in range(2):
                blocks[k, j, 240 * i:240 * i + 240, :] = dot(qkvo[3, i, 0:240, :], weight, 1, 1).astype(BF)
            small = dot(oa, qoa[k, j, :, :, 256:512].reshape(128, 256), 1, 1).astype(BF)
            for i in range(2):
                blocks[k, j, 480:544, 128 * i:128 * i + 128] = small[64 * i:64 * i + 64]

    mark('rs8')
    sum_task = block_sum(comm, blocks, (l0, l1, l2), l3)
    terms(2)
    pump(sum_task)
    terms(1), terms(3)
    pump(c_task)
    pump(sum_task)
    terms(0)
    pump(f_tasks[4], f_tasks[1])
    pump(f_tasks[0], f_tasks[2])
    pump(sum_task)
    drain(c_task)
    saves.append(comm.local(c16, out_c))
    pump(f_tasks[1])
    drain(sum_task)
    mark('hmake')
    first.wait()
    hv[...] = xv[...].astype(F32) + blocks[place.x, place.zl].astype(F32)
    full[place.x, place.z] = hv[...].astype(BF)
    saves.append(comm.local(hv, out_h))
    mark('hplane')
    h_task = comm.plane_gather(lambda k, j, p: full.at[k, j, p], PARTS_A, PARTS_B)
    pump(h_task)
    pump(f_tasks[0], f_tasks[3])
    pump(h_task)
    pump(f_tasks[1], f_tasks[2], f_tasks[4])
    pump(h_task)
    pump(f_tasks[3], f_tasks[4])
    pump(h_task)
    drain(h_task)
    saves.append(comm.local(full, out_h16))
    mark('norm2')
    for zhi in range(2):
        def rows_norm(i, carry):
            here = pl.ds(pl.multiple_of(240 * i, 16), 240)
            there = pl.ds(pl.multiple_of(480 * zhi + 240 * i, 16), 240)
            get = lambda n: full[n // 2, 2 * zhi + n % 2, here, :].astype(F32)
            def put(n, v):
                n2p[there, 256 * n:256 * n + 256] = v
            scale = norm_block_rows(get, lambda n: g8[n // 2, n % 2, 1:2, :], 256, put)
            r2[zhi, here, :] = jnp.broadcast_to(scale, (240, 128))
            return carry
        lax.fori_loop(0, 2, rows_norm, 0)
        for i in range(2):
            get = lambda n: full[n // 2, 2 * zhi + n % 2, 480:544, 128 * i:128 * i + 128].astype(F32)
            base = 128 * zhi + 64 * i
            def put(n, v):
                n2a[base:base + 64, 128 * n:128 * n + 128] = v
            scale = norm_block_rows(get, lambda n: g8[n // 2, n % 2, 2:3, 128:256], 128, put)
            r2[zhi, 480 + 64 * i:544 + 64 * i, :] = jnp.broadcast_to(scale, (64, 128))
    mark('tail')
    saves += [comm.local(n2p, out_n2p), comm.local(n2a, out_n2a), comm.local(r2.at[zh], out_r2)]
    for task in f_tasks:
        drain(task)
    for copy in saves:
        copy.wait()
    mark(None)
    comm.close()


def attend(lens, *args):
    wide5 = lambda n, c: (4, 2, 2, n, c)
    outs = [((CH,) + wide5(128, 768), BF), (wide5(64, 768), BF), (wide5(128, 512), BF), (wide5(64, 512), BF),
            (wide5(128, 512), BF), (wide5(64, 512), BF), ((4, 4, T, 256), BF), ((4, 2, 8, 256), F32),
            ((480, 2048), BF), ((128, 1024), BF), ((4, 2, KEYS, 256), BF), ((608, 128), F32), ((T, 256), F32),
            ((4, 4, T, 256), BF), ((960, 2048), BF), ((256, 1024), BF), ((608, 128), F32)]
    vm = pltpu.VMEM
    scratch = [vm((4, 2, 192, 128), BF), vm((192, 512), BF)] + [vm(s, d) for s, d in outs[2:6]] + [
        vm((4, 2, T, 256), BF), vm((4, 4, T, 256), BF), vm((4, 2, 8, 256), F32), vm((480, 2048), BF), vm((128, 1024), BF),
        vm((4, 2, KEYS, 256), BF), vm((608, 128), F32), vm((T, 256), BF), vm((T, 256), F32), vm((4, 4, T, 256), BF),
        vm((960, 2048), BF), vm((256, 1024), BF), vm((2, 608, 128), F32), vm((4, 2, T, 256), BF)] + LAND_8
    return pl.pallas_call(
        attend_kernel,
        out_shape=[jax.ShapeDtypeStruct(s, d) for s, d in outs],
        in_specs=[pl.BlockSpec(memory_space=pltpu.SMEM)] + [ANY] * len(args),
        out_specs=[ANY] * len(outs),
        scratch_shapes=scratch + SEM_SCRATCH,
        compiler_params=pltpu.CompilerParams(collective_id=0, has_side_effects=True, vmem_limit_bytes=VMEM_CAP),
        name="attend",
    )(lens, *args)
EARLY = 2
TILE = 240


def gelu_parts(z):
    a, b = 0.7978845608028654, 0.044715
    t = jnp.tanh(a * (z + b * z * z * z))
    half = 0.5 * (1.0 + t)
    return z * half, half + 0.5 * z * (1.0 - t * t) * a * (1.0 + 3.0 * b * z * z)


def side_rows(full, z_low, base, count):
    return jnp.concatenate([full[x, z_low + zl, pl.ds(base, count), :] for x, zl in pairs8()], axis=1)


def feed_forward_kernel(f, fa, n2p, n2a, c16, out_g2, out_g3, out_s0, out_s1, out_sa, out_d8, out_y,
                        wv, wav, np_, na, gc, ga, dd, aa, dda, aaa, bb, bf, bn, d8, yb, g0, g1, ga_, s0, s1, sa,
                        r0, r1, ra, z0, z1, za, *sems):
    comm = Comm(*sems)
    place = comm.place
    loads = [comm.local(n2p, np_), comm.local(f.at[0], wv.at[0]), comm.local(c16, gc), comm.local(n2a, na),
             comm.local(f.at[1], wv.at[1]), comm.local(f.at[2], wv.at[2]), comm.local(f.at[3], wv.at[3]),
             comm.local(fa, wav)]
    comm.enter(PEERS)
    mark("units")
    loads[0].wait()
    for i in range(CH):
        loads[(1, 4, 5, 6)[i]].wait()
        if i == 0:
            loads[2].wait()
        def unit(t, carry):
            here = pl.ds(pl.multiple_of(TILE * t, 16), TILE)
            weight = lambda j: wv[i, :, :, :, :, 256 * j:256 * j + 256].reshape(2048, 256)
            rows_n = np_[here, :]
            gate, up = dot(rows_n, weight(0), 1, 0), dot(rows_n, weight(1), 1, 0)
            rows_c = side_rows(gc, 2 * lax.div(t, 2), pl.multiple_of(TILE * lax.rem(t, 2), 16), TILE)
            dact = dot(rows_c, weight(2), 1, 0)
            value, slope = gelu_parts(gate)
            aa[here, 256 * i:256 * i + 256] = (value * up).astype(BF)
            dd[here, 512 * i:512 * i + 256] = (dact * up * slope).astype(BF)
            dd[here, 512 * i + 256:512 * i + 512] = (dact * value).astype(BF)
            return carry
        lax.fori_loop(0, 4, unit, 0)
    loads[3].wait(), loads[7].wait()
    for zhi in range(2):
        for i in range(2):
            base = 128 * zhi + 64 * i
            for n in range(8):
                ga[base:base + 64, 128 * n:128 * n + 128] = gc[n // 2, 2 * zhi + n % 2, 480:544, 128 * i:128 * i + 128]
    weight = lambda j: wav[:, :, :, :, 256 * j:256 * j + 256].reshape(1024, 256)
    gate, up, dact = dot(na[...], weight(0), 1, 0), dot(na[...], weight(1), 1, 0), dot(ga[...], weight(2), 1, 0)
    value, slope = gelu_parts(gate)
    aaa[...] = (value * up).astype(BF)
    dda[:, 0:256] = (dact * up * slope).astype(BF)
    dda[:, 256:512] = (dact * value).astype(BF)

    mark("back")

    def product(ref, x, z, left, left_a, lo, hi):
        zh_, zl_ = lax.div(z, 2), lax.rem(z, 2)
        here = pl.ds(pl.multiple_of(480 * zh_, 16), 480)
        rows_w = jnp.concatenate([wv[i, x, zl_, :, :, lo:hi].reshape(256, hi - lo) for i in range(CH)], axis=1)
        ref[0:480, :] = dot(left[here, :], rows_w, 1, 1).astype(BF)
        there = pl.ds(pl.multiple_of(128 * zh_, 16), 128)
        small = dot(left_a[there, :], wav[x, zl_, :, :, lo:hi].reshape(128, hi - lo), 1, 1).astype(BF)
        ref[480:544, 0:128] = small[0:64]
        ref[480:544, 128:256] = small[64:128]

    far_x, far_z = place.off("x", 2), place.off("z", 2)

    def far_terms(t, carry):
        x = jnp.where(t < 4, t, far_x)
        z = jnp.where(t < 4, far_z, lax.rem(far_z + jnp.where(t < 4, 0, t - 3), 4))
        product(bb.at[x, z], x, z, dd, dda, 0, 512)
        return carry

    def near_terms(t, carry):
        x, z = lax.rem(far_x + 1 + lax.div(t, 3), 4), lax.rem(far_z + 1 + lax.rem(t, 3), 4)
        product(bb.at[x, z], x, z, dd, dda, 0, 512)
        return carry

    lax.fori_loop(0, 7, far_terms, 0)
    b_task = plane_sum(comm, bb, bf, bn)
    pump(b_task)
    lax.fori_loop(0, 9, near_terms, 0)
    pump(b_task)

    mark("grads")

    def weight_grads(grad, i):
        def block_rows(y, carry):
            here = pl.ds(pl.multiple_of(512 * y, 512), 512)
            left_n = np_[:, here]
            left_c = jnp.concatenate(
                [jnp.concatenate([gc[y, zl, 0:480, :], gc[y, 2 + zl, 0:480, :]], axis=0) for zl in range(2)], axis=1)
            for j in range(3):
                if j < 2:
                    value = dot(left_n, dd[:, 512 * i + 256 * j:512 * i + 256 * j + 256], 0, 0).astype(BF)
                else:
                    value = dot(left_c, aa[:, 256 * i:256 * i + 256], 0, 0).astype(BF)
                for q in range(4):
                    grad[q % 2, y, q // 2, :, 256 * j:256 * j + 256] = value[128 * q:128 * q + 128]
            return carry
        lax.fori_loop(0, 4, block_rows, 0)

    weight_grads(g0, 0)
    w0 = wide_sum(comm, g0, s0, r0.at[0], r0.at[1], r0.at[2], z0, 128, False)
    pump(w0)
    weight_grads(g1, 1)
    w1 = wide_sum(comm, g1, s1, r1.at[0], r1.at[1], r1.at[2], z1, 128, False)
    pump(w0, w1)
    pump(b_task)
    for y in range(4):
        left_n, left_c = na[:, 256 * y:256 * y + 256], ga[:, 256 * y:256 * y + 256]
        for j in range(3):
            value = dot(left_n, dda[:, 256 * j:256 * j + 256], 0, 0) if j < 2 else dot(left_c, aaa[...], 0, 0)
            value = value.astype(BF)
            for q in range(4):
                ga_[q % 2, y, q // 2, :, 256 * j:256 * j + 256] = value[64 * q:64 * q + 64]
    wa = wide_sum(comm, ga_, sa, ra.at[0], ra.at[1], ra.at[2], za, 64, False)
    pump(wa, w0, w1)
    pump(b_task)
    drain(b_task)
    mark("dn2")
    d8[place.x, place.zl] = bb[place.x, place.z]
    d_task = comm.pair_ring_gather("zl", "x", lambda k, j, p: d8.at[k, j, p], PARTS_8,
                                   lambda p: d8.at[place.x, place.zl, p], d8.at[place.x, place.zl], slice(None))
    pump(d_task)
    pump(wa, w0, w1)
    mark("late")
    late = []
    for i, out in ((2, out_g2), (3, out_g3)):
        pump(d_task)
        weight_grads(yb, i)
        late.append(comm.local(yb, out))
        late[-1].wait()
        pump(w0, w1, wa)
    mark("ydown")

    def down_terms(t, carry):
        x, z = lax.div(t, 4), lax.rem(t, 4)
        product(bb.at[x, z], x, z, aa, aaa, 512, 768)
        return carry

    drain(d_task)
    comm.settle()
    lax.fori_loop(0, 16, down_terms, 0)
    saves = [comm.local(bb, out_y), comm.local(d8, out_d8)]
    for task in (w0, w1, wa):
        drain(task)
    for grad, swap, out in ((g0, z0, out_s0), (g1, z1, out_s1), (ga_, za, out_sa)):
        saves.append(comm.local(grad.at[place.core, place.y, place.zh], out.at[place.zh]))
        saves.append(comm.local(swap, out.at[1 - place.zh]))
    for copy in saves:
        copy.wait()
    mark(None)
    comm.close()


def feed_forward(f, fa, n2p, n2a, c16):
    grad = (2, 4, 2, 128, 768)
    outs = [(grad, BF), (grad, BF), ((2, 128, 768), BF), ((2, 128, 768), BF), ((2, 64, 768), BF),
            ((4, 2, T, 256), BF), ((4, 4, T, 256), BF)]
    vm = lambda *s: pltpu.VMEM(s, BF)
    scratch = [vm(CH, 4, 2, 2, 128, 768), vm(4, 2, 2, 64, 768), vm(960, 2048), vm(256, 1024), vm(4, 4, T, 256),
               vm(256, 1024), vm(960, 2048), vm(960, 1024), vm(256, 512), vm(256, 256)]
    scratch += [vm(4, 4, T, 256)] + LAND_16 + [vm(4, 2, T, 256), vm(*grad)]
    scratch += [vm(*grad), vm(*grad), vm(2, 4, 2, 64, 768), vm(*grad[1:]), vm(*grad[1:]), vm(4, 2, 64, 768)]
    scratch += [vm(3, 2, 128, 768), vm(3, 2, 128, 768), vm(3, 2, 64, 768), vm(128, 768), vm(128, 768), vm(64, 768)]
    return pl.pallas_call(
        feed_forward_kernel,
        out_shape=[jax.ShapeDtypeStruct(s, d) for s, d in outs],
        in_specs=[ANY] * 5,
        out_specs=[ANY] * len(outs),
        scratch_shapes=scratch + SEM_SCRATCH,
        compiler_params=pltpu.CompilerParams(collective_id=2, has_side_effects=True, vmem_limit_bytes=VMEM_CAP),
        name="feed_forward",
    )(f, fa, n2p, n2a, c16)
def attend_back_kernel(lens, d8, h16, c16, r2, r1, g8, qo, qoa, kv, kva, n1p, n1a, qkvo, xb, cotb, g2, g3, yt, h_own,
                       out_s2, out_s3, out_q, out_qa, out_kv, out_x, out_y, out_g,
                       dv8, hv, cv, r2v, r1v, g8v, qov, qoav, kvv, kvav, npv, nav, qv, xv, cotv, g2v, g3v, yv, how,
                       mean, ghp, gha, dhb, dov, dqp, dqa, stat, st8, gains, gsum, gains16, outx, outy,
                       gq, gkv, gqa, gkva, kvb, blocks, yf, yn, l0, l1, l2, l3, k0, k1, k2, k3,
                       s2, s3, sq, skv, sqa, skva, t2, t3, tq, tkv, tqa, tkva, z2, z3, zq, zkv, zqa, zkva, *sems):
    comm = Comm(*sems)
    place = comm.place
    x, y, zh, zl, core = place.x, place.y, place.zh, place.zl, place.core
    side = pl.ds(2 * zh, 2)
    load = comm.local
    la = [load(d8, dv8), load(h16.at[:, side], hv), load(r2, r2v), load(g8, g8v), load(c16.at[:, side], cv), load(cotb, cotv)]
    lg = [load(g2, g2v), load(g3, g3v)]
    lb = [load(qo, qov), load(qoa, qoav), load(qkvo, qv)]
    ly = load(yt, yv)
    lc = [load(kv, kvv), load(kva, kvav), load(n1p, npv), load(n1a, nav), load(xb, xv), load(r1, r1v), load(h_own, how)]
    comm.enter(PEERS)
    mark("dh")
    for copy in la:
        copy.wait()
    for i in range(2):
        here = pl.ds(240 * i, 240)
        scale = r2v[here, 0:1]
        gain = lambda n: g8v[n // 2, n % 2, 1:2, :]
        grad = lambda n: dv8[n // 2, n % 2, here, :].astype(F32) * gain(n)
        unit = lambda n: hv[n // 2, n % 2, here, :].astype(F32) * scale
        m = sum(jnp.sum(grad(n) * unit(n), axis=1, keepdims=True) for n in range(8)) / 2048
        mean[here, :] = jnp.broadcast_to(m, (240, 128))
        for n in range(8):
            value = cv[n // 2, n % 2, here, :].astype(F32) + scale * (grad(n) - unit(n) * m)
            ghp[here, 256 * n:256 * n + 256] = value.astype(BF)
        here, there, lanes = pl.ds(480, 64), pl.ds(480 + 64 * i, 64), pl.ds(128 * i, 128)
        scale_a = r2v[there, 0:1]
        gain_a = lambda n: g8v[n // 2, n % 2, 2:3, 128:256]
        grad_a = lambda n: dv8[n // 2, n % 2, here, lanes].astype(F32) * gain_a(n)
        unit_a = lambda n: hv[n // 2, n % 2, here, lanes].astype(F32) * scale_a
        m = sum(jnp.sum(grad_a(n) * unit_a(n), axis=1, keepdims=True) for n in range(8)) / 1024
        mean[there, :] = jnp.broadcast_to(m, (64, 128))
        for n in range(8):
            value = cv[n // 2, n % 2, here, lanes].astype(F32) + scale_a * (grad_a(n) - unit_a(n) * m)
            gha[64 * i:64 * i + 64, 128 * n:128 * n + 128] = value.astype(BF)
    mark("attnback")
    for copy in lb:
        copy.wait()
    for i in range(2):
        here = pl.ds(240 * i, 240)
        dov[i, 0:240, :] = dot(ghp[here, :], qov[:, :, :, :, 256:512].reshape(2048, 256), 1, 0).astype(BF)
    low = dot(gha[...], qoav[:, :, :, :, 256:512].reshape(1024, 256), 1, 0).astype(BF)
    for i in range(2):
        dov[i, 240:304, :] = low[64 * i:64 * i + 64]
    for i in range(2):
        q, k, v, do = qv[0, i, 0:304, :], qv[1, i], qv[2, i], dov[i]
        probs = soft(q, k, lens[i])
        inner = probs * dot(do, v, 1, 1)
        dscores = (inner - probs * jnp.sum(inner, axis=1, keepdims=True)).astype(BF)
        dq = (dot(dscores, k, 1, 0) * 0.0625).astype(BF)
        dk = (dot(dscores, q, 0, 0) * 0.0625).astype(BF)[0:304]
        dv = dot(probs.astype(BF), do, 0, 0).astype(BF)[0:304]
        for j, value in enumerate((dq, dk, dv)):
            dqp[240 * i:240 * i + 240, 256 * j:256 * j + 256] = value[0:240]
            dqa[64 * i:64 * i + 64, 256 * j:256 * j + 256] = value[240:304]
        total = dq.astype(F32) * q.astype(F32) + dk.astype(F32) * k[0:304].astype(F32) + dv.astype(F32) * v[0:304].astype(F32)
        total = jnp.broadcast_to(jnp.sum(total, axis=1, keepdims=True), (304, 128))
        stat[240 * i:240 * i + 240, :] = total[0:240]
        stat[480 + 64 * i:544 + 64 * i, :] = total[240:304]
    stat[608:640, :] = jnp.zeros((32, 128), F32)
    st8[x, zl] = stat[...].T[0:8]
    for copy in lc:
        copy.wait()
    mark("terms")

    def terms(step):
        k = place.off("x", step)
        for j in range(2):
            weight = jnp.concatenate([qov[k, j, :, :, 0:256].reshape(256, 256), kvv[k, j].reshape(256, 512)], axis=1)
            blocks[k, j, 0:480, :] = dot(dqp[...], weight, 1, 1).astype(BF)
            weight = jnp.concatenate([qoav[k, j, :, :, 0:256].reshape(128, 256), kvav[k, j].reshape(128, 512)], axis=1)
            small = dot(dqa[...], weight, 1, 1).astype(BF)
            for i in range(2):
                blocks[k, j, 480:544, 128 * i:128 * i + 128] = small[64 * i:64 * i + 64]

    terms(2)
    sum_task = block_sum(comm, blocks, (l0, l1, l2), l3)
    pump(sum_task)
    stat_task = comm.pair_ring_gather("zl", "x", lambda k, j, p: st8.at[k, j, p], [(slice(None), 1)],
                                      lambda p: st8.at[x, zl, p], st8.at[x, zl], slice(None))
    pump(stat_task)
    terms(1), terms(3)
    pump(sum_task)
    terms(0)

    def outer(grad, n, left, right, lo, width):
        def block_rows(k, carry):
            here = pl.ds(pl.multiple_of(4 * n * k, 4 * n), 4 * n)
            value = dot(left[:, here], right, 0, 0).astype(BF)
            for c in range(4):
                grad[c % 2, k, c // 2, :, lo:lo + width] = value[n * c:n * c + n]
            return carry
        lax.fori_loop(0, 4, block_rows, 0)

    mark("attngrads")
    outer(gkv, 128, npv, dqp[:, 256:768], 0, 512)
    outer(gkva, 64, nav, dqa[:, 256:768], 0, 512)
    kv_tasks = [wide_sum(comm, gkv, skv, tkv.at[0], tkv.at[1], tkv.at[2], zkv, 128, True),
                wide_sum(comm, gkva, skva, tkva.at[0], tkva.at[1], tkva.at[2], zkva, 64, True)]
    pump(*kv_tasks)
    outer(gq, 128, npv, dqp[:, 0:256], 0, 256)
    o_act = jnp.concatenate([qv[3, 0, 240:304, :], qv[3, 1, 240:304, :]], axis=0)
    o_pre = jnp.concatenate([qv[3, 0, 0:240, :], qv[3, 1, 0:240, :]], axis=0)
    outer(gq, 128, ghp, o_pre, 256, 256)
    outer(gqa, 64, nav, dqa[:, 0:256], 0, 256)
    outer(gqa, 64, gha, o_act, 256, 256)
    q_tasks = [wide_sum(comm, gq, sq, tq.at[0], tq.at[1], tq.at[2], zq, 128, True),
               wide_sum(comm, gqa, sqa, tqa.at[0], tqa.at[1], tqa.at[2], zqa, 64, True)]
    pump(*q_tasks)
    pump(*kv_tasks)
    mark("late")
    for copy in lg:
        copy.wait()
    late = [wide_sum(comm, g2v, s2, t2.at[0], t2.at[1], t2.at[2], z2, 128, False),
            wide_sum(comm, g3v, s3, t3.at[0], t3.at[1], t3.at[2], z3, 128, False)]
    pump(*late)
    ly.wait()
    y_task = plane_sum(comm, yv, yf, yn)
    pump(y_task)
    pump(stat_task, sum_task)
    pump(*q_tasks), pump(*kv_tasks)
    pump(*late)
    pump(stat_task, y_task)
    drain(sum_task), drain(stat_task)
    mark("dx")
    g_pre, g_act = g8v[x, zl, 0:1, :], g8v[x, zl, 2:3, 0:128]
    f_pre, f_act = g8v[x, zl, 1:2, :], g8v[x, zl, 2:3, 128:256]
    total = sum(st8[n // 2, n % 2] for n in range(8))
    stat[...] = jnp.broadcast_to(total[0:1], (128, 640)).T

    def own_norm(here, there, lanes, gain_f, gain_a, width):
        s2_, s1_ = r2v[there, 0:1], r1v[there, 0:1]
        back, unit = dv8[x, zl, here, lanes].astype(F32), hv[x, zl, here, lanes].astype(F32) * s2_
        dh = cotv[here, lanes] + s2_ * (back * gain_f - unit * mean[there, 0:1])
        gain_f_grad = jnp.sum(back * unit, axis=0, keepdims=True)
        back, unit = blocks[x, zl, here, lanes].astype(F32), xv[here, lanes].astype(F32) * s1_
        outx[here, lanes] = dh + s1_ * (back * gain_a - unit * (stat[there, 0:1] / width))
        return jnp.sum(back * unit, axis=0, keepdims=True), gain_f_grad

    pre = [own_norm(pl.ds(240 * i, 240), pl.ds(240 * i, 240), pl.ds(0, 256), f_pre, g_pre, 2048) for i in range(2)]
    act = [own_norm(pl.ds(480, 64), pl.ds(480 + 64 * i, 64), pl.ds(128 * i, 128), f_act, g_act, 1024) for i in range(2)]
    gains[...] = jnp.concatenate(
        [pre[0][0] + pre[1][0], pre[0][1] + pre[1][1],
         jnp.concatenate([act[0][0] + act[1][0], act[0][1] + act[1][1]], axis=1), jnp.zeros((5, 256), F32)], axis=0)
    saves = [load(outx, out_x)]
    g_task = wide_gather(comm, gains16, gains, gains, 8, [(slice(None), 1)])
    pump(g_task)
    mark("tail")
    pump(y_task, g_task), pump(*late), pump(g_task)
    pump(*kv_tasks), pump(*q_tasks), pump(g_task, y_task)
    drain(kv_tasks[0]), drain(kv_tasks[1])
    own = jnp.concatenate([gkv[core, y, zh], gkva[core, y, zh]], axis=0)
    lane = lax.broadcasted_iota(jnp.int32, (128, 512), 0)
    col = lax.broadcasted_iota(jnp.int32, (128, 512), 1)
    for n in range(8):
        pick = ((lane < 32) & (col == 32 * n + lane)) | ((lane >= 32) & (lane < 64) & (col == 224 + 32 * n + lane))
        kvb[n // 2, n % 2] = dot(own, pick.astype(F32).astype(BF), 1, 1).astype(BF)
    share = block_sum(comm, kvb, (k0, k1, k2), k3, halves(192))
    pump(share)
    pump(g_task), pump(*late), pump(*q_tasks)
    pump(share)
    drain(y_task)
    outy[...] = (yv[x, place.z].astype(F32) + how[...]).astype(BF)
    saves.append(load(outy, out_y))
    pump(share, g_task)
    for task in q_tasks + late:
        drain(task)
    drain(share), drain(g_task)
    gsum[...] = sum(gains16[a, b, c] for a in range(4) for b in range(2) for c in range(2))
    saves += [load(gsum, out_g), load(kvb.at[x, zl], out_kv), load(gq.at[core, y, zh], out_q), load(gqa.at[core, y, zh], out_qa)]
    for grad, swap, out in ((g2v, z2, out_s2), (g3v, z3, out_s3)):
        saves += [load(grad.at[core, y, zh], out.at[zh]), load(swap, out.at[1 - zh])]
    for copy in saves:
        copy.wait()
    mark(None)
    comm.close()


def attend_back(lens, *args):
    outs = [((2, 128, 768), BF), ((2, 128, 768), BF), ((128, 512), BF), ((64, 512), BF), ((192, 128), BF), ((T, 256), F32),
            ((T, 256), BF), ((8, 256), F32)]
    vm = lambda *s: pltpu.VMEM(s, BF)
    vf = lambda *s: pltpu.VMEM(s, F32)
    wide = lambda n, c: (2, 4, 2, n, c)
    back = [(128, 768), (128, 768), (128, 512), (128, 512), (64, 512), (64, 512)]
    scratch = [vm(4, 2, T, 256), vm(4, 2, T, 256), vm(4, 2, T, 256), vf(608, 128), vf(608, 128), vf(4, 2, 8, 256),
               vm(4, 2, 2, 128, 512), vm(4, 2, 2, 64, 512), vm(4, 2, 2, 128, 512), vm(4, 2, 2, 64, 512),
               vm(480, 2048), vm(128, 1024), vm(4, 2, KEYS, 256), vm(T, 256), vf(T, 256), vm(*wide(128, 768)),
               vm(*wide(128, 768)), vm(4, 4, T, 256), vf(T, 256)]
    scratch += [vf(608, 128), vm(480, 2048), vm(128, 1024), vf(8, 128), vm(2, 304, 256), vm(480, 768), vm(128, 768),
                vf(640, 128), vf(4, 2, 8, 640), vf(8, 256), vf(8, 256), vf(4, 2, 2, 8, 256), vf(T, 256), vm(T, 256)]
    scratch += [vm(*wide(n, c)) for n, c in back[2:]]
    scratch += [vm(4, 2, 192, 128), vm(4, 2, T, 256)] + LAND_16 + LAND_8 + [vm(2, 192, 128)] * 3 + [vm(192, 128)]
    scratch += [vm(4, 2, n, c) for n, c in back] + [vm(3, 2, n, c) for n, c in back] + [vm(n, c) for n, c in back]
    return pl.pallas_call(
        attend_back_kernel,
        out_shape=[jax.ShapeDtypeStruct(s, d) for s, d in outs],
        in_specs=[pl.BlockSpec(memory_space=pltpu.SMEM)] + [ANY] * len(args),
        out_specs=[ANY] * len(outs),
        scratch_shapes=scratch + SEM_SCRATCH,
        compiler_params=pltpu.CompilerParams(collective_id=3, has_side_effects=True, vmem_limit_bytes=VMEM_CAP),
        name="attend_back",
    )(lens, *args)
def local(x_pre, x_act, lengths, cot_pre, cot_act, attn_gain_pre, query_pre, key_pre, value_pre, out_pre, ffn_gain_pre,
          gate_pre, up_pre, down_pre, attn_gain_act, query_act, key_act, value_act, out_act, ffn_gain_act, gate_act,
          up_act, down_act):
    wf, wfa = pack_hidden(gate_pre, up_pre, down_pre), pack_hidden(gate_act, up_act, down_act)[:, 0]
    wq, wqa = jnp.concatenate([query_pre, out_pre.T], axis=1), jnp.concatenate([query_act, out_act.T], axis=1)
    kvs = jnp.concatenate([jnp.concatenate([key_pre, value_pre], axis=1), jnp.concatenate([key_act, value_act], axis=1)])
    kvs = jnp.pad(kvs, ((0, 0), (0, 64)))
    xb, cot = pack_tokens(x_pre, x_act), pack_tokens(cot_pre, cot_act)
    gb = jnp.pad(jnp.stack([attn_gain_pre, ffn_gain_pre, jnp.concatenate([attn_gain_act, ffn_gain_act])]), ((0, 5), (0, 0)))
    (f, fa, qo, qoa, kv, kva, c16, g8, n1p, n1a, qkvo, r1, h_own, h16, n2p, n2a, r2) = attend(
        lengths, wf, wfa, wq, wqa, kvs, xb, cot.astype(BF), gb)
    g2, g3, s0, s1, sa, d8, yt = feed_forward(f, fa, n2p, n2a, c16)
    s2, s3, sq, sqa, skv, gx, y, gains = attend_back(
        lengths, d8, h16, c16, r2, r1, g8, qo, qoa, kv, kva, n1p, n1a, qkvo, xb, cot, g2, g3, yt, h_own)
    unact = lambda m: m.reshape(64, 2, 128)[:50].transpose(1, 0, 2)

    def open_hidden(m, n):
        m = m.astype(F32).reshape(2, -1, n, 768).transpose(2, 0, 1, 3)
        gate, up, down = (m[..., 256 * j:256 * j + 256].reshape(n, -1) for j in range(3))
        return gate, up, down.T

    dgate_p, dup_p, ddown_p = open_hidden(jnp.stack([s0, s1, s2, s3], axis=1), 128)
    dgate_a, dup_a, ddown_a = open_hidden(sa, 64)
    sq, sqa, skv = sq.astype(F32), sqa.astype(F32), skv.astype(F32)
    return (y[:480].reshape(2, 240, 256), unact(y[480:]), gx[:480].reshape(2, 240, 256), unact(gx[480:]),
            gains[0], sq[:, :256], skv[:128, :32], skv[:128, 32:64], sq[:, 256:].T, gains[1], dgate_p, dup_p, ddown_p,
            gains[2, :128], sqa[:, :256], skv[128:, :32], skv[128:, 32:64], sqa[:, 256:].T, gains[2, 128:],
            dgate_a, dup_a, ddown_a)


def solution(mesh):
    tok, row, col, vec = P("wide", None, "narrow"), P("wide", "narrow"), P("narrow", "wide"), P("narrow")
    expert = (vec, row, row, row, col, vec, row, row, col)
    return jax.shard_map(
        local, mesh=mesh, in_specs=(tok, tok, P("wide"), tok, tok) + expert + expert,
        out_specs=(tok,) * 4 + expert + expert, check_vma=False)
```

```python
import functools
import jax
import jax.numpy as jnp
from jax import lax
from jax.experimental import pallas as pl
from jax.experimental.pallas import tpu as pltpu
from jax.sharding import PartitionSpec as P

MESH = pl.DeviceIdType.MESH
BF = jnp.bfloat16
F32 = jnp.float32
SEMS = 256
LOCAL_SEMS = 48
VMEM_CAP = 62 * 1024 * 1024


class Place:
    def __init__(self):
        wide, narrow = lax.axis_index("wide"), lax.axis_index("narrow")
        self.core = lax.rem(wide, 2)
        self.zh = lax.rem(lax.div(wide, 2), 2)
        self.y = lax.div(wide, 4)
        self.zl = lax.rem(narrow, 2)
        self.x = lax.div(narrow, 2)
        self.z = self.zh * 2 + self.zl

    def wide_at(self, y, zh, core):
        return (y * 2 + zh) * 2 + core

    def coord(self, axis):
        return {"x": self.x, "y": self.y, "z": self.z}[axis]

    def off(self, axis, step):
        return lax.rem(self.coord(axis) + step + 4, 4)

    def peer(self, name):
        if name == "sib":
            return {"wide": self.wide_at(self.y, self.zh, 1 - self.core)}
        if name == "z2":
            return {"wide": self.wide_at(self.y, 1 - self.zh, self.core)}
        if name == "zl":
            return {"narrow": self.x * 2 + 1 - self.zl}
        if name[0] == "w":
            step, flip = int(name[1]), int(name[2])
            zh = 1 - self.zh if flip else self.zh
            return {"wide": self.wide_at(self.off("y", step), zh, self.core)}
        axis, step = name[0], 1 if name[1] == "+" else -1
        at = self.off(axis, step)
        if axis == "y":
            return {"wide": self.wide_at(at, self.zh, self.core)}
        if axis == "x":
            return {"narrow": at * 2 + self.zl}
        return {"wide": self.wide_at(self.y, lax.div(at, 2), self.core), "narrow": self.x * 2 + lax.rem(at, 2)}


class Link:
    def __init__(self, out, into):
        self.out, self.into = out, into

    def arrive(self):
        self.into.wait_recv()

    def left(self):
        self.out.wait_send()


class Comm:
    def __init__(self, send_sems, recv_sems, local_sems):
        self.place = Place()
        self.send_sems, self.recv_sems, self.local_sems = send_sems, recv_sems, local_sems
        self.count, self.local_count = 0, 0
        self.links = []

    def enter(self, peers):
        barrier = pltpu.get_barrier_semaphore()
        for name in peers:
            pl.semaphore_signal(barrier, inc=1, device_id=self.place.peer(name), device_id_type=MESH)
        pl.semaphore_wait(barrier, len(peers))

    def send(self, src, dst, name, incoming):
        index = self.count
        self.count += 1
        assert index < SEMS
        make = lambda to: pltpu.make_async_remote_copy(
            src_ref=src, dst_ref=to, send_sem=self.send_sems.at[index], recv_sem=self.recv_sems.at[index],
            device_id=self.place.peer(name), device_id_type=MESH)
        out = make(dst)
        out.start()
        link = Link(out, make(incoming))
        self.links.append(link)
        return link

    def local(self, src, dst):
        index = self.local_count
        self.local_count += 1
        assert index < LOCAL_SEMS
        copy = pltpu.make_async_copy(src, dst, self.local_sems.at[index])
        copy.start()
        return copy

    def settle(self):
        for link in self.links:
            link.left()
        self.links = []

    def close(self):
        self.settle()

    def ring_gather(self, axis, view, parts, own=None):
        place = self.place
        at = lambda step: place.off(axis, step)
        src = own if own is not None else (lambda part: view(at(0), part))
        plus = [self.send(src(p), view(at(0), p), axis + "+", view(at(-1), p)) for p, _ in parts]
        minus = [self.send(src(p), view(at(0), p), axis + "-", view(at(1), p)) for p, _ in parts]
        yield
        far = []
        for (p, way), up in zip(parts, plus):
            up.arrive()
            if way > 0:
                far.append(self.send(view(at(-1), p), view(at(-1), p), axis + "+", view(at(-2), p)))
        for (p, way), down in zip(parts, minus):
            down.arrive()
            if way < 0:
                far.append(self.send(view(at(1), p), view(at(1), p), axis + "-", view(at(2), p)))
        yield
        for link in far:
            link.arrive()

    def pair_ring_gather(self, pair, axis, view, parts, own, give, whole):
        place = self.place
        mine = {"z2": place.zh, "zl": place.zl}[pair]
        here = place.coord(axis)
        first = self.ring_gather(axis, lambda k, p: view(k, mine, p), parts, own)
        next(first)
        yield
        swap = self.send(give, view(here, mine, whole), pair, view(here, 1 - mine, whole))
        yield
        next(first)
        yield
        swap.arrive()
        second = self.ring_gather(axis, lambda k, p: view(k, 1 - mine, p), parts)
        next(second)
        yield
        next(second)
        yield
        drain(first)
        drain(second)

    def plane_gather(self, view, parts_x, parts_z, own=None, ready=None):
        place = self.place
        every = slice(None)
        ax = self.ring_gather("x", lambda k, p: view(k, place.z, p), parts_x, own)
        bz = self.ring_gather("z", lambda k, p: view(place.x, k, p), parts_z, own)
        next(ax), next(bz)
        yield
        next(ax), next(bz)
        yield
        if ready is not None:
            ready()
        drain(ax)
        az = self.ring_gather("z", lambda k, p: view(every, k, p), parts_x)
        next(az)
        drain(bz)
        bx = self.ring_gather("x", lambda k, p: view(k, every, p), parts_z)
        next(bx)
        yield
        next(az), next(bx)
        yield
        drain(az), drain(bx)

    def ring_sum(self, axis, view, parts, relay, plus, minus):
        place = self.place
        at = lambda step: place.off(axis, step)
        far = []
        for p, way in parts:
            far.append(self.send(view(at(2), p), relay(p), axis + ("+" if way > 0 else "-"), relay(p)))
        yield
        ups, downs = [], []
        for (p, way), link in zip(parts, far):
            link.arrive()
            add_to(view(at(way), p), relay(p))
            if way > 0:
                ups.append(self.send(view(at(1), p), plus(p), axis + "+", plus(p)))
            else:
                downs.append(self.send(view(at(-1), p), minus(p), axis + "-", minus(p)))
        for p, way in parts:
            if way > 0:
                downs.append(self.send(view(at(-1), p), minus(p), axis + "-", minus(p)))
            else:
                ups.append(self.send(view(at(1), p), plus(p), axis + "+", plus(p)))
        yield
        for link in ups + downs:
            link.arrive()
        for p, _ in parts:
            add_to(view(at(0), p), plus(p), minus(p))


def add_to(ref, *others):
    total = ref[...].astype(F32)
    for other in others:
        total = total + other[...].astype(F32)
    ref[...] = total.astype(ref.dtype)


def drain(task):
    for _ in task:
        pass


def rows(lo, hi):
    return pl.ds(lo, hi - lo)
T = 544
CH = 4


def halves(n):
    return [(rows(0, n // 2), 1), (rows(n // 2, n), -1)]


PARTS_8 = [(rows(0, 272), 1), (rows(272, 544), -1)]
PARTS_A = [(rows(0, 144), 1), (rows(144, 272), -1)]
PARTS_B = [(rows(272, 416), 1), (rows(416, 544), -1)]
PEERS = ("y+", "y-", "z2", "sib", "x+", "x-", "z+", "z-")


def wide_gather(comm, out, own, give, n, parts=None):
    place = comm.place
    core = place.core
    copy = comm.local(own, out.at[place.y, place.zh, core])
    task = comm.pair_ring_gather(
        "z2", "y", lambda k, j, p: out.at[k, j, core, p], parts or halves(n),
        lambda p: own.at[p], give, slice(None))
    yield from task
    copy.wait()
    link = comm.send(out.at[:, :, core], out.at[:, :, core], "sib", out.at[:, :, 1 - core])
    yield
    link.arrive()


def block_gather(comm, out, own, parts):
    place = comm.place
    copy = comm.local(own, out.at[place.x, place.zl])
    yield from comm.pair_ring_gather(
        "zl", "x", lambda k, j, p: out.at[k, j, p], parts, lambda p: own.at[p], own, slice(None))
    copy.wait()


def plane_spread(comm, out, own):
    place = comm.place
    copy = comm.local(own, out.at[place.x, place.z])
    yield from comm.plane_gather(lambda k, j, p: out.at[k, j, p], PARTS_A, PARTS_B, lambda p: own.at[p], copy.wait)


def pack_hidden(gate, up, down):
    n, hidden = gate.shape
    cut = lambda m: m.reshape(n, 2, hidden // 512, 256)
    return jnp.concatenate([cut(gate), cut(up), cut(down.T)], axis=-1).transpose(1, 2, 0, 3)


def pack_tokens(pre, act):
    low = jnp.concatenate([act[0], act[1]], axis=1)
    low = jnp.pad(low, ((0, 14), (0, 0)))
    return jnp.concatenate([pre.reshape(480, 256), low], axis=0)
def block_sum(comm, blocks, lands, swap, parts=PARTS_8):
    place = comm.place
    relay, plus, minus = lands
    yield from comm.ring_sum(
        "x", lambda k, p: blocks.at[k, :, p], parts,
        lambda p: relay.at[:, p], lambda p: plus.at[:, p], lambda p: minus.at[:, p])
    link = comm.send(blocks.at[place.x, 1 - place.zl], swap, "zl", swap)
    yield
    link.arrive()
    add_to(blocks.at[place.x, place.zl], swap)


def plane_sum(comm, blocks, lands_far, lands_near):
    place = comm.place
    az = comm.ring_sum("z", lambda k, p: blocks.at[:, k, p], PARTS_A,
                       lambda p: lands_far.at[0, :, p], lambda p: lands_far.at[1, :, p], lambda p: lands_far.at[2, :, p])
    bx = comm.ring_sum("x", lambda k, p: blocks.at[k, :, p], PARTS_B,
                       lambda p: lands_far.at[0, :, p], lambda p: lands_far.at[1, :, p], lambda p: lands_far.at[2, :, p])
    next(az), next(bx)
    yield
    next(az), next(bx)
    yield
    drain(az)
    ax = comm.ring_sum("x", lambda k, p: blocks.at[k, place.z, p], PARTS_A,
                       lambda p: lands_near.at[0, p], lambda p: lands_near.at[1, p], lambda p: lands_near.at[2, p])
    next(ax)
    drain(bx)
    bz = comm.ring_sum("z", lambda k, p: blocks.at[place.x, k, p], PARTS_B,
                       lambda p: lands_near.at[0, p], lambda p: lands_near.at[1, p], lambda p: lands_near.at[2, p])
    next(bz)
    yield
    next(ax), next(bz)
    yield
    drain(ax), drain(bz)


CHIPS = [(step, flip) for flip in range(2) for step in range(4) if step or flip]


def small_total(comm, slots, pair, own, out):
    place = comm.place
    mine = place.y * 2 + place.zh
    links = []
    for step, flip in CHIPS:
        back = place.off("y", -step) * 2 + (1 - place.zh if flip else place.zh)
        links.append(comm.send(own, slots.at[mine], f"w{step}{flip}", slots.at[back]))
    slots[mine] = own[...]
    yield
    for link in links:
        link.arrive()
    pair[0] = sum(slots[i] for i in range(8))
    link = comm.send(pair.at[0], pair.at[1], "sib", pair.at[1])
    yield
    link.arrive()
    out[...] = pair[0] + pair[1]


def wide_sum(comm, grad, half, relay, plus, minus, swap, n, add):
    place = comm.place
    core, zh = place.core, place.zh
    link = comm.send(grad.at[:, :, 1 - core], half, "sib", half)
    yield
    link.arrive()
    def fold(k, carry):
        add_to(grad.at[k, :, core], half.at[k])
        return carry
    lax.fori_loop(0, 4, fold, 0)
    yield from comm.ring_sum(
        "y", lambda k, p: grad.at[k, :, core, p], halves(n),
        lambda p: relay.at[:, p], lambda p: plus.at[:, p], lambda p: minus.at[:, p])
    link = comm.send(grad.at[place.y, 1 - zh, core], swap, "z2", swap)
    yield
    link.arrive()
    if add:
        add_to(grad.at[place.y, zh, core], swap)


SEM_SCRATCH = [pltpu.SemaphoreType.DMA((SEMS,)), pltpu.SemaphoreType.DMA((SEMS,)), pltpu.SemaphoreType.DMA((LOCAL_SEMS,))]
ANY = pl.BlockSpec(memory_space=pl.ANY)


LAND_8 = [pltpu.VMEM((2, T, 256), BF)] * 3 + [pltpu.VMEM((T, 256), BF)]


LAND_16 = [pltpu.VMEM((3, 4, T, 256), BF), pltpu.VMEM((3, T, 256), BF)]


EPSILON = 1e-06
MASKED = -1000000000.0
KEYS = 384


def dot(a, b, ca, cb):
    return lax.dot_general(a, b, (((ca,), (cb,)), ((), ())), preferred_element_type=F32)


_open = []


def mark(name):
    if _open:
        _open.pop().__exit__(None, None, None)
    if name:
        scope = jax.named_scope(name)
        scope.__enter__()
        _open.append(scope)


def pump(*tasks):
    for task in tasks:
        next(task, None)


def seen(length):
    s = lax.broadcasted_iota(jnp.int32, (304, KEYS), 0)
    t = lax.broadcasted_iota(jnp.int32, (304, KEYS), 1)
    live = (t < 192) | ((t >= 240) & (t < 290)) | ((t < 240) & (t - 192 < length))
    return live & ((t < 240) | (s >= 240))


def soft(q, k, length):
    scores = dot(q, k, 1, 1) * 0.0625
    scores = jnp.where(seen(length), scores, MASKED)
    weights = jnp.exp(scores - jnp.max(scores, axis=1, keepdims=True))
    return weights / jnp.sum(weights, axis=1, keepdims=True)


def pairs8():
    return [(x, zl) for x in range(4) for zl in range(2)]


def norm_block_rows(get, gain, width, put):
    total = sum(jnp.sum(get(n) * get(n), axis=1, keepdims=True) for n in range(8))
    scale = lax.rsqrt(total / (8 * width) + EPSILON)
    for n in range(8):
        put(n, (get(n) * scale * gain(n)).astype(BF))
    return scale


def attend_kernel(lens, wf, wfa, wq, wqa, kvs, xb, gb,
                  out_f, out_fa, out_q, out_qa, out_kv, out_kva, out_g, out_n1p, out_n1a, out_qkvo, out_r1,
                  out_h, out_h16, out_n2p, out_n2a, out_r2,
                  kv8, kvf, qo, qoa, kv, kva, x8, g8, n1p, n1a, qkvo, r1, xv, hv, full, n2p, n2a, r2,
                  blocks, l0, l1, l2, l3, *sems):
    comm = Comm(*sems)
    place = comm.place
    zh = place.zh
    first = comm.local(xb, xv)
    zero = jnp.zeros((KEYS - 304, 256), BF)
    for i in range(2):
        for j in (1, 2):
            qkvo[j, i, 304:KEYS, :] = zero
    comm.enter(PEERS)

    mark('start')
    kv_task = block_gather(comm, kv8, kvs, halves(192))
    g_task = block_gather(comm, g8, gb, [(slice(None), 1)])
    x_task = block_gather(comm, x8, xb, PARTS_8)
    q_tasks = [wide_gather(comm, qo, wq, wq, 128), wide_gather(comm, qoa, wqa, wqa, 64)]
    f_tasks = [wide_gather(comm, out_f.at[i], wf.at[zh, i], wf.at[1 - zh, i], 128) for i in range(CH)]
    f_tasks.append(wide_gather(comm, out_fa, wfa.at[zh], wfa.at[1 - zh], 64))
    pump(kv_task), pump(kv_task)
    pump(x_task), pump(x_task)
    pump(g_task), pump(g_task)
    pump(*q_tasks)
    pump(kv_task), pump(kv_task)
    pump(x_task)
    pump(kv_task)
    pump(x_task)
    pump(*q_tasks), pump(*q_tasks)
    pump(g_task)
    drain(kv_task)
    total = jnp.zeros((192, 512), F32)
    lane = lax.broadcasted_iota(jnp.int32, (128, 512), 0)
    col = lax.broadcasted_iota(jnp.int32, (128, 512), 1)
    for n in range(8):
        pick = ((lane < 32) & (col == 32 * n + lane)) | ((lane >= 32) & (lane < 64) & (col == 224 + 32 * n + lane))
        total = total + dot(kv8[n // 2, n % 2], pick.astype(F32).astype(BF), 1, 0)
    kvf[...] = total.astype(BF)
    kv_a, kv_b = kvf.at[0:128], kvf.at[128:192]
    kv_tasks = [wide_gather(comm, kv, kv_a, kv_a, 128), wide_gather(comm, kva, kv_b, kv_b, 64)]
    pump(*kv_tasks), pump(*kv_tasks)
    pump(*q_tasks)
    pump(g_task), pump(g_task)
    pump(x_task)
    pump(*kv_tasks)
    pump(*q_tasks)
    drain(g_task)
    pump(*kv_tasks)
    drain(x_task)

    mark('norm1')
    for i in range(2):
        here = pl.ds(240 * i, 240)
        get = lambda n: x8[n // 2, n % 2, here, :].astype(F32)
        def put(n, v):
            n1p[here, 256 * n:256 * n + 256] = v
        r1[here, :] = jnp.broadcast_to(norm_block_rows(get, lambda n: g8[n // 2, n % 2, 0:1, :], 256, put), (240, 128))
        low = pl.ds(480, 64)
        get = lambda n: x8[n // 2, n % 2, low, 128 * i:128 * i + 128].astype(F32)
        def put(n, v):
            n1a[64 * i:64 * i + 64, 128 * n:128 * n + 128] = v
        r1[480 + 64 * i:544 + 64 * i, :] = jnp.broadcast_to(
            norm_block_rows(get, lambda n: g8[n // 2, n % 2, 2:3, 0:128], 128, put), (64, 128))
    pump(*q_tasks)
    pump(*kv_tasks)
    for task in f_tasks:
        pump(task), pump(task)
    for task in q_tasks:
        drain(task)
    mark('qkv')
    def queries(i, carry):
        here = pl.ds(pl.multiple_of(240 * i, 16), 240)
        qkvo[0, i, 0:240, :] = dot(n1p[here, :], qo[:, :, :, :, 0:256].reshape(2048, 256), 1, 0).astype(BF)
        return carry
    lax.fori_loop(0, 2, queries, 0)
    pump(*kv_tasks)
    for task in kv_tasks:
        drain(task)
    def keys(i, carry):
        here = pl.ds(pl.multiple_of(240 * i, 16), 240)
        for j in range(2):
            qkvo[1 + j, i, 0:240, :] = dot(
                n1p[here, :], kv[:, :, :, :, 256 * j:256 * j + 256].reshape(2048, 256), 1, 0).astype(BF)
        return carry
    lax.fori_loop(0, 2, keys, 0)
    low = [dot(n1a[...], qoa[:, :, :, :, 0:256].reshape(1024, 256), 1, 0).astype(BF)]
    for j in range(2):
        low.append(dot(n1a[...], kva[:, :, :, :, 256 * j:256 * j + 256].reshape(1024, 256), 1, 0).astype(BF))
    for i in range(2):
        for j in range(3):
            qkvo[j, i, 240:304, :] = low[j][64 * i:64 * i + 64]
    saves = [comm.local(qo, out_q), comm.local(qoa, out_qa), comm.local(kv, out_kv), comm.local(kva, out_kva),
             comm.local(n1p, out_n1p), comm.local(n1a, out_n1a), comm.local(r1, out_r1), comm.local(g8, out_g)]
    mark('attn')
    for i in range(2):
        probs = soft(qkvo[0, i, 0:304, :], qkvo[1, i], lens[i])
        qkvo[3, i, 0:304, :] = dot(probs.astype(BF), qkvo[2, i], 1, 0).astype(BF)
    saves.append(comm.local(qkvo, out_qkvo))
    mark('outproj')
    oa = jnp.concatenate([qkvo[3, 0, 240:304, :], qkvo[3, 1, 240:304, :]], axis=0)

    def terms(step):
        k = place.off("x", step)
        for j in range(2):
            weight = qo[k, j, :, :, 256:512].reshape(256, 256)
            for i in range(2):
                blocks[k, j, 240 * i:240 * i + 240, :] = dot(qkvo[3, i, 0:240, :], weight, 1, 1).astype(BF)
            small = dot(oa, qoa[k, j, :, :, 256:512].reshape(128, 256), 1, 1).astype(BF)
            for i in range(2):
                blocks[k, j, 480:544, 128 * i:128 * i + 128] = small[64 * i:64 * i + 64]

    mark('rs8')
    sum_task = block_sum(comm, blocks, (l0, l1, l2), l3)
    terms(2)
    pump(sum_task)
    terms(1), terms(3)
    pump(f_tasks[0], f_tasks[1])
    pump(sum_task)
    terms(0)
    pump(f_tasks[2], f_tasks[3], f_tasks[4])
    pump(f_tasks[0], f_tasks[1])
    pump(sum_task)
    pump(f_tasks[2], f_tasks[3], f_tasks[4])
    drain(sum_task)
    mark('hmake')
    first.wait()
    hv[...] = xv[...].astype(F32) + blocks[place.x, place.zl].astype(F32)
    full[place.x, place.z] = hv[...].astype(BF)
    saves.append(comm.local(hv, out_h))
    mark('hplane')
    h_task = comm.plane_gather(lambda k, j, p: full.at[k, j, p], PARTS_A, PARTS_B)
    pump(h_task)
    pump(f_tasks[0], f_tasks[1])
    pump(h_task)
    pump(h_task)
    pump(f_tasks[2], f_tasks[3], f_tasks[4])
    pump(f_tasks[0], f_tasks[1])
    pump(h_task)
    pump(f_tasks[2], f_tasks[3])
    drain(h_task)
    saves.append(comm.local(full, out_h16))
    mark('norm2')
    for zhi in range(2):
        def rows_norm(i, carry):
            here = pl.ds(pl.multiple_of(240 * i, 16), 240)
            there = pl.ds(pl.multiple_of(480 * zhi + 240 * i, 16), 240)
            get = lambda n: full[n // 2, 2 * zhi + n % 2, here, :].astype(F32)
            def put(n, v):
                n2p[there, 256 * n:256 * n + 256] = v
            scale = norm_block_rows(get, lambda n: g8[n // 2, n % 2, 1:2, :], 256, put)
            r2[zhi, here, :] = jnp.broadcast_to(scale, (240, 128))
            return carry
        lax.fori_loop(0, 2, rows_norm, 0)
        for i in range(2):
            get = lambda n: full[n // 2, 2 * zhi + n % 2, 480:544, 128 * i:128 * i + 128].astype(F32)
            base = 128 * zhi + 64 * i
            def put(n, v):
                n2a[base:base + 64, 128 * n:128 * n + 128] = v
            scale = norm_block_rows(get, lambda n: g8[n // 2, n % 2, 2:3, 128:256], 128, put)
            r2[zhi, 480 + 64 * i:544 + 64 * i, :] = jnp.broadcast_to(scale, (64, 128))
    mark('tail')
    saves += [comm.local(n2p, out_n2p), comm.local(n2a, out_n2a), comm.local(r2.at[zh], out_r2)]
    for task in f_tasks:
        drain(task)
    for copy in saves:
        copy.wait()
    mark(None)
    comm.close()


def attend(lens, *args):
    wide5 = lambda n, c: (4, 2, 2, n, c)
    outs = [((CH,) + wide5(128, 768), BF), (wide5(64, 768), BF), (wide5(128, 512), BF), (wide5(64, 512), BF),
            (wide5(128, 512), BF), (wide5(64, 512), BF), ((4, 2, 8, 256), F32),
            ((480, 2048), BF), ((128, 1024), BF), ((4, 2, KEYS, 256), BF), ((608, 128), F32), ((T, 256), F32),
            ((4, 4, T, 256), BF), ((960, 2048), BF), ((256, 1024), BF), ((608, 128), F32)]
    vm = pltpu.VMEM
    scratch = [vm((4, 2, 192, 128), BF), vm((192, 512), BF)] + [vm(s, d) for s, d in outs[2:6]] + [
        vm((4, 2, T, 256), BF), vm((4, 2, 8, 256), F32), vm((480, 2048), BF), vm((128, 1024), BF),
        vm((4, 2, KEYS, 256), BF), vm((608, 128), F32), vm((T, 256), BF), vm((T, 256), F32), vm((4, 4, T, 256), BF),
        vm((960, 2048), BF), vm((256, 1024), BF), vm((2, 608, 128), F32), vm((4, 2, T, 256), BF)] + LAND_8
    return pl.pallas_call(
        attend_kernel,
        out_shape=[jax.ShapeDtypeStruct(s, d) for s, d in outs],
        in_specs=[pl.BlockSpec(memory_space=pltpu.SMEM)] + [ANY] * len(args),
        out_specs=[ANY] * len(outs),
        scratch_shapes=scratch + SEM_SCRATCH,
        compiler_params=pltpu.CompilerParams(collective_id=0, has_side_effects=True, vmem_limit_bytes=VMEM_CAP),
        name="attend",
    )(lens, *args)
EARLY = 2
TILE = 240


def gelu_parts(z):
    a, b = 0.7978845608028654, 0.044715
    t = jnp.tanh(a * (z + b * z * z * z))
    half = 0.5 * (1.0 + t)
    return z * half, half + 0.5 * z * (1.0 - t * t) * a * (1.0 + 3.0 * b * z * z)


def side_rows(full, z_low, base, count):
    return jnp.concatenate([full[x, z_low + zl, pl.ds(base, count), :] for x, zl in pairs8()], axis=1)


def feed_forward_kernel(f, fa, n2p, n2a, cb, *refs):
    out_s, out_late, refs = refs[:EARLY + 1], refs[EARLY + 1:CH + 1], refs[CH + 1:]
    out_d8, out_y, out_c, wv, wav, np_, na, gc, ga, dd, aa, dda, aaa, bb, bf, bn, d8, grad_act = refs[:18]
    lands = [refs[18 + 3 * i:21 + 3 * i] for i in range(EARLY + 1)]
    comm = Comm(*refs[-3:])
    place = comm.place
    loads = [comm.local(n2p, np_), comm.local(f.at[0], wv.at[0]), comm.local(n2a, na),
             comm.local(f.at[1], wv.at[1]), comm.local(f.at[2], wv.at[2]), comm.local(f.at[3], wv.at[3]),
             comm.local(fa, wav)]
    c_task = plane_spread(comm, gc, cb)
    comm.enter(PEERS)
    pump(c_task)
    mark("units")
    loads[0].wait()

    def gate_up(left, weight):
        both = dot(left, weight, 1, 0)
        up = both[:, 256:512]
        value, slope = gelu_parts(both[:, 0:256])
        return (value * up).astype(BF), (up * slope).astype(BF), value.astype(BF)

    for i in range(CH):
        loads[(1, 3, 4, 5)[i]].wait()
        def unit(t, carry):
            here = pl.ds(pl.multiple_of(TILE * t, 16), TILE)
            a, b, c = gate_up(np_[here, :], wv[i, :, :, :, :, 0:512].reshape(2048, 512))
            aa[here, 256 * i:256 * i + 256] = a
            dd[here, 512 * i:512 * i + 256] = b
            dd[here, 512 * i + 256:512 * i + 512] = c
            return carry
        lax.fori_loop(0, 4, unit, 0)
        if i in (0, 1):
            pump(c_task)
    loads[2].wait(), loads[6].wait()
    aaa[...], dda[:, 0:256], dda[:, 256:512] = gate_up(na[...], wav[:, :, :, :, 0:512].reshape(1024, 512))

    def product(ref, x, z, left, left_a, lo, hi):
        zh_, zl_ = lax.div(z, 2), lax.rem(z, 2)
        here = pl.ds(pl.multiple_of(480 * zh_, 16), 480)
        rows_w = jnp.concatenate([wv[i, x, zl_, :, :, lo:hi].reshape(256, hi - lo) for i in range(CH)], axis=1)
        ref[0:480, :] = dot(left[here, :], rows_w, 1, 1).astype(BF)
        there = pl.ds(pl.multiple_of(128 * zh_, 16), 128)
        small = dot(left_a[there, :], wav[x, zl_, :, :, lo:hi].reshape(128, hi - lo), 1, 1).astype(BF)
        ref[480:544, 0:128] = small[0:64]
        ref[480:544, 128:256] = small[64:128]

    def down_terms(t, carry):
        x, z = lax.div(t, 4), lax.rem(t, 4)
        product(bb.at[x, z], x, z, aa, aaa, 512, 768)
        return carry

    mark("ydown")
    lax.fori_loop(0, 12, down_terms, 0)
    pump(c_task)
    lax.fori_loop(12, 16, down_terms, 0)
    saves = [comm.local(bb, out_y)]
    mark("cwait")
    drain(c_task)
    saves.append(comm.local(gc.at[:, pl.ds(2 * place.zh, 2)], out_c))
    mark("dact")
    for i in range(CH):
        def dact_unit(t, carry):
            here = pl.ds(pl.multiple_of(TILE * t, 16), TILE)
            rows_c = side_rows(gc, 2 * lax.div(t, 2), pl.multiple_of(TILE * lax.rem(t, 2), 16), TILE)
            dact = dot(rows_c, wv[i, :, :, :, :, 512:768].reshape(2048, 256), 1, 0)
            for j in range(2):
                there = slice(512 * i + 256 * j, 512 * i + 256 * j + 256)
                dd[here, there] = (dact * dd[here, there].astype(F32)).astype(BF)
            return carry
        lax.fori_loop(0, 4, dact_unit, 0)
    for zhi in range(2):
        for i in range(2):
            base = 128 * zhi + 64 * i
            for n in range(8):
                ga[base:base + 64, 128 * n:128 * n + 128] = gc[n // 2, 2 * zhi + n % 2, 480:544, 128 * i:128 * i + 128]
    dact = dot(ga[...], wav[:, :, :, :, 512:768].reshape(1024, 256), 1, 0)
    for j in range(2):
        there = slice(256 * j, 256 * j + 256)
        dda[:, there] = (dact * dda[:, there].astype(F32)).astype(BF)
    saves[0].wait()

    mark("back")
    far_x, far_z = place.off("x", 2), place.off("z", 2)

    def far_terms(t, carry):
        x = jnp.where(t < 4, t, far_x)
        z = jnp.where(t < 4, far_z, lax.rem(far_z + jnp.where(t < 4, 0, t - 3), 4))
        product(bb.at[x, z], x, z, dd, dda, 0, 512)
        return carry

    def near_terms(t, carry):
        x, z = lax.rem(far_x + 1 + lax.div(t, 3), 4), lax.rem(far_z + 1 + lax.rem(t, 3), 4)
        product(bb.at[x, z], x, z, dd, dda, 0, 512)
        return carry

    lax.fori_loop(0, 7, far_terms, 0)
    b_task = plane_sum(comm, bb, bf, bn)
    pump(b_task)
    lax.fori_loop(0, 9, near_terms, 0)
    pump(b_task)

    mark("grads")

    def weight_grads(i):
        def block_rows(y, carry):
            here = pl.ds(pl.multiple_of(512 * y, 512), 512)
            left_n = np_[:, here]
            left_c = jnp.concatenate(
                [jnp.concatenate([gc[y, zl, 0:480, :], gc[y, 2 + zl, 0:480, :]], axis=0) for zl in range(2)], axis=1)
            for j in range(3):
                if j < 2:
                    value = dot(left_n, dd[:, 512 * i + 256 * j:512 * i + 256 * j + 256], 0, 0).astype(BF)
                else:
                    value = dot(left_c, aa[:, 256 * i:256 * i + 256], 0, 0).astype(BF)
                wv[i, y, :, :, :, 256 * j:256 * j + 256] = value.reshape(2, 2, 128, 256)
            return carry
        lax.fori_loop(0, 4, block_rows, 0)

    def act_grads():
        for y in range(4):
            left_n, left_c = na[:, 256 * y:256 * y + 256], ga[:, 256 * y:256 * y + 256]
            for j in range(3):
                value = dot(left_n, dda[:, 256 * j:256 * j + 256], 0, 0) if j < 2 else dot(left_c, aaa[...], 0, 0)
                grad_act[y, :, :, :, 256 * j:256 * j + 256] = value.astype(BF).reshape(2, 2, 64, 256)

    grads = [wv.at[i] for i in range(EARLY)] + [grad_act]
    sums = [wide_sum(comm, grad, s, r.at[0], r.at[1], r.at[2], z, 64 if i == EARLY else 128, False)
            for i, (grad, (s, r, z)) in enumerate(zip(grads, lands))]
    weight_grads(0)
    pump(sums[0])
    weight_grads(1)
    pump(sums[0], sums[1])
    pump(b_task)
    act_grads()
    pump(sums[2])
    pump(sums[1])
    weight_grads(2)
    saves.append(comm.local(wv.at[2], out_late[0]))
    pump(b_task)
    pump(sums[0])
    pump(sums[2])
    drain(b_task)
    mark("dn2")
    d8[place.x, place.zl] = bb[place.x, place.z]
    d_task = comm.pair_ring_gather("zl", "x", lambda k, j, p: d8.at[k, j, p], PARTS_8,
                                   lambda p: d8.at[place.x, place.zl, p], d8.at[place.x, place.zl], slice(None))
    pump(d_task), pump(d_task)
    pump(sums[1])
    weight_grads(3)
    saves.append(comm.local(wv.at[3], out_late[1]))
    pump(d_task), pump(d_task)
    pump(sums[0], sums[2])
    pump(d_task)
    pump(sums[1], sums[2])
    drain(d_task)
    saves.append(comm.local(d8, out_d8))
    mark("sums")
    for task in sums:
        drain(task)
    for grad, (_, _, swap), out in zip(grads, lands, out_s):
        saves.append(comm.local(grad.at[place.y, place.zh, place.core], out.at[place.zh]))
        saves.append(comm.local(swap, out.at[1 - place.zh]))
    for copy in saves[1:]:
        copy.wait()
    mark(None)
    comm.close()


def feed_forward(f, fa, n2p, n2a, cb):
    grad = (4, 2, 2, 128, 768)
    outs = [(2, 128, 768)] * EARLY + [(2, 64, 768)] + [grad] * (CH - EARLY) + [(4, 2, T, 256), (4, 4, T, 256), (4, 2, T, 256)]
    vm = lambda *s: pltpu.VMEM(s, BF)
    scratch = [vm(CH, *grad), vm(4, 2, 2, 64, 768), vm(960, 2048), vm(256, 1024), vm(4, 4, T, 256),
               vm(256, 1024), vm(960, 2048), vm(960, 1024), vm(256, 512), vm(256, 256)]
    scratch += [vm(4, 4, T, 256)] + LAND_16 + [vm(4, 2, T, 256), vm(4, 2, 2, 64, 768)]
    for n in [128] * EARLY + [64]:
        scratch += [vm(4, 2, n, 768), vm(3, 2, n, 768), vm(n, 768)]
    return pl.pallas_call(
        feed_forward_kernel,
        out_shape=[jax.ShapeDtypeStruct(s, BF) for s in outs],
        in_specs=[ANY] * 5,
        out_specs=[ANY] * len(outs),
        scratch_shapes=scratch + SEM_SCRATCH,
        compiler_params=pltpu.CompilerParams(collective_id=2, has_side_effects=True, vmem_limit_bytes=VMEM_CAP),
        name="feed_forward",
    )(f, fa, n2p, n2a, cb)
TS = T + 16
SUM_PARTS = [(rows(0, 272), 1), (rows(272, TS), -1)]
FAR_PEERS = tuple(f"w{step}{flip}" for step, flip in CHIPS if (step, flip) not in ((1, 0), (3, 0), (0, 1)))
KV_PARTS = [(rows(0, 160), 1), (rows(160, 304), -1)]


def attend_back_kernel(lens, d8, h16, c16, r2, r1, g8, qo, qoa, kv, kva, n1p, n1a, qkvo, xb, cotb, g2, g3, yt, h_own,
                       out_s2, out_s3, out_q, out_qa, out_kv, out_kva, out_x, out_y, out_g,
                       dv8, hv, cv, r2v, r1v, g8v, qov, qoav, kvv, kvav, npv, nav, qv, xv, cotv, g2v, g3v, yv, how,
                       mean, ghp, gha, dhb, dov, dqp, dqa, stat, gains, gsum, gains16, gains2, outx, outy,
                       gq, gkv, gqa, gkva, kvb, blocks, yf, yn, l0, l1, l2, l3, k0, k1, k2, k3,
                       s2, s3, sq, skv, sqa, skva, t2, t3, tq, tkv, tqa, tkva, z2, z3, zq, zkv, zqa, zkva, *sems):
    comm = Comm(*sems)
    place = comm.place
    x, y, zh, zl, core = place.x, place.y, place.zh, place.zl, place.core
    side = pl.ds(2 * zh, 2)
    load = comm.local
    la = [load(d8, dv8), load(h16.at[:, side], hv), load(r2, r2v), load(g8, g8v), load(c16, cv), load(cotb, cotv)]
    ly = load(yt, yv)
    lg = [load(g2, g2v), load(g3, g3v)]
    lb = [load(qo, qov), load(qoa, qoav), load(qkvo, qv)]
    lc = [load(kv, kvv), load(kva, kvav), load(n1p, npv), load(n1a, nav), load(xb, xv), load(r1, r1v), load(h_own, how)]
    comm.enter(PEERS + FAR_PEERS)
    late = [wide_sum(comm, g2v, s2, t2.at[0], t2.at[1], t2.at[2], z2, 128, False),
            wide_sum(comm, g3v, s3, t3.at[0], t3.at[1], t3.at[2], z3, 128, False)]
    y_task = plane_sum(comm, yv, yf, yn)
    ly.wait()
    pump(y_task)
    lg[0].wait()
    pump(late[0])
    lg[1].wait()
    pump(late[1])
    mark("dh")
    for copy in la:
        copy.wait()
    for i in range(2):
        here = pl.ds(240 * i, 240)
        scale = r2v[here, 0:1]
        gain = lambda n: g8v[n // 2, n % 2, 1:2, :]
        grad = lambda n: dv8[n // 2, n % 2, here, :].astype(F32) * gain(n)
        unit = lambda n: hv[n // 2, n % 2, here, :].astype(F32) * scale
        m = sum(jnp.sum(grad(n) * unit(n), axis=1, keepdims=True) for n in range(8)) / 2048
        mean[here, :] = jnp.broadcast_to(m, (240, 128))
        for n in range(8):
            value = cv[n // 2, n % 2, here, :].astype(F32) + scale * (grad(n) - unit(n) * m)
            ghp[here, 256 * n:256 * n + 256] = value.astype(BF)
        here, there, lanes = pl.ds(480, 64), pl.ds(480 + 64 * i, 64), pl.ds(128 * i, 128)
        scale_a = r2v[there, 0:1]
        gain_a = lambda n: g8v[n // 2, n % 2, 2:3, 128:256]
        grad_a = lambda n: dv8[n // 2, n % 2, here, lanes].astype(F32) * gain_a(n)
        unit_a = lambda n: hv[n // 2, n % 2, here, lanes].astype(F32) * scale_a
        m = sum(jnp.sum(grad_a(n) * unit_a(n), axis=1, keepdims=True) for n in range(8)) / 1024
        mean[there, :] = jnp.broadcast_to(m, (64, 128))
        for n in range(8):
            value = cv[n // 2, n % 2, here, lanes].astype(F32) + scale_a * (grad_a(n) - unit_a(n) * m)
            gha[64 * i:64 * i + 64, 128 * n:128 * n + 128] = value.astype(BF)
    pump(late[0])
    pump(late[1])
    mark("attnback")
    for copy in lb:
        copy.wait()
    for i in range(2):
        here = pl.ds(240 * i, 240)
        dov[i, 0:240, :] = dot(ghp[here, :], qov[:, :, :, :, 256:512].reshape(2048, 256), 1, 0).astype(BF)
    low = dot(gha[...], qoav[:, :, :, :, 256:512].reshape(1024, 256), 1, 0).astype(BF)
    for i in range(2):
        dov[i, 240:304, :] = low[64 * i:64 * i + 64]
    pump(y_task)
    for i in range(2):
        q, k, v, do = qv[0, i, 0:304, :], qv[1, i], qv[2, i], dov[i]
        probs = soft(q, k, lens[i])
        inner = probs * dot(do, v, 1, 1)
        dscores = (inner - probs * jnp.sum(inner, axis=1, keepdims=True)).astype(BF)
        dq = (dot(dscores, k, 1, 0) * 0.0625).astype(BF)
        dk = (dot(dscores, q, 0, 0) * 0.0625).astype(BF)[0:304]
        dv = dot(probs.astype(BF), do, 0, 0).astype(BF)[0:304]
        for j, value in enumerate((dq, dk, dv)):
            dqp[240 * i:240 * i + 240, 256 * j:256 * j + 256] = value[0:240]
            dqa[64 * i:64 * i + 64, 256 * j:256 * j + 256] = value[240:304]
        total = dq.astype(F32) * q.astype(F32) + dk.astype(F32) * k[0:304].astype(F32) + dv.astype(F32) * v[0:304].astype(F32)
        total = jnp.broadcast_to(jnp.sum(total, axis=1, keepdims=True), (304, 128))
        stat[240 * i:240 * i + 240, :] = total[0:240]
        stat[480 + 64 * i:544 + 64 * i, :] = total[240:304]
    stat[608:640, :] = jnp.zeros((32, 128), F32)
    line = stat[...].T[0:1]
    line = jnp.concatenate([line[:, 0:256], line[:, 256:512], jnp.concatenate([line[:, 512:640], jnp.zeros((1, 128), F32)], axis=1),
                            jnp.zeros((13, 256), F32)], axis=0).astype(BF)
    for n in range(8):
        blocks[n // 2, n % 2, T:TS, :] = line
    lane = lax.broadcasted_iota(jnp.int32, (512, 128), 1)
    col = lax.broadcasted_iota(jnp.int32, (512, 128), 0)
    kv_sum = block_sum(comm, kvb, (k0, k1, k2), k3, KV_PARTS)
    for n in range(8):
        total = []
        for i in range(2):
            at = lane - 64 * i
            pick = ((at >= 0) & (at < 32) & (col == 32 * n + at)) | ((at >= 32) & (at < 64) & (col == 224 + 32 * n + at))
            pick = pick.astype(F32).astype(BF)
            total.append((dot(dqp[240 * i:240 * i + 240, 256:768], pick, 1, 0), dot(dqa[64 * i:64 * i + 64, 256:768], pick, 1, 0)))
        kvb[n // 2, n % 2, 0:240, :] = (total[0][0] + total[1][0]).astype(BF)
        kvb[n // 2, n % 2, 240:304, :] = (total[0][1] + total[1][1]).astype(BF)
    pump(kv_sum)
    for copy in lc:
        copy.wait()
    mark("terms")

    def terms(step):
        k = place.off("x", step)
        for j in range(2):
            weight = jnp.concatenate([qov[k, j, :, :, 0:256].reshape(256, 256), kvv[k, j].reshape(256, 512)], axis=1)
            blocks[k, j, 0:480, :] = dot(dqp[...], weight, 1, 1).astype(BF)
            weight = jnp.concatenate([qoav[k, j, :, :, 0:256].reshape(128, 256), kvav[k, j].reshape(128, 512)], axis=1)
            small = dot(dqa[...], weight, 1, 1).astype(BF)
            for i in range(2):
                blocks[k, j, 480:544, 128 * i:128 * i + 128] = small[64 * i:64 * i + 64]

    def outer(grad, n, left, right, lo, width):
        def block_rows(k, carry):
            here = pl.ds(pl.multiple_of(4 * n * k, 4 * n), 4 * n)
            value = dot(left[:, here], right, 0, 0).astype(BF)
            grad[k, :, :, :, lo:lo + width] = value.reshape(2, 2, n, width)
            return carry
        lax.fori_loop(0, 4, block_rows, 0)

    terms(2)
    sum_task = block_sum(comm, blocks, (l0, l1, l2), l3, SUM_PARTS)
    pump(sum_task)
    terms(1), terms(3)
    mark("attngrads")
    o_act = jnp.concatenate([qv[3, 0, 240:304, :], qv[3, 1, 240:304, :]], axis=0)
    o_pre = jnp.concatenate([qv[3, 0, 0:240, :], qv[3, 1, 0:240, :]], axis=0)
    outer(gq, 128, ghp, o_pre, 256, 256)
    outer(gqa, 64, gha, o_act, 256, 256)
    pump(late[0], late[1])
    terms(0)
    outer(gq, 128, npv, dqp[:, 0:256], 0, 256)
    outer(gqa, 64, nav, dqa[:, 0:256], 0, 256)
    q_tasks = [wide_sum(comm, gq, sq, tq.at[0], tq.at[1], tq.at[2], zq, 128, True),
               wide_sum(comm, gqa, sqa, tqa.at[0], tqa.at[1], tqa.at[2], zqa, 64, True)]
    kv_tasks = [wide_sum(comm, gkv, skv, tkv.at[0], tkv.at[1], tkv.at[2], zkv, 128, True),
                wide_sum(comm, gkva, skva, tkva.at[0], tkva.at[1], tkva.at[2], zkva, 64, True)]
    pump(*q_tasks)
    pump(kv_sum)
    pump(y_task)
    pump(*q_tasks)
    pump(sum_task)
    pump(kv_sum)
    pump(y_task)
    drain(kv_sum)
    own = kvb[x, zl]
    share = []
    for i in range(2):
        lane = lax.broadcasted_iota(jnp.int32, (128, 128), 0)
        col = lax.broadcasted_iota(jnp.int32, (128, 128), 1)
        pick = ((col < 64) & (lane == col + 64 * i)).astype(F32).astype(BF)
        share.append(dot(own, pick, 1, 0).astype(BF))
    outer(gkv, 128, npv, jnp.concatenate([share[0][0:240], share[1][0:240]], axis=0), 0, 128)
    outer(gkva, 64, nav, jnp.concatenate([share[0][240:304], share[1][240:304]], axis=0), 0, 128)
    pump(*kv_tasks)
    mark("late")
    pump(late[0], late[1])
    pump(*kv_tasks)
    pump(*q_tasks)
    pump(sum_task)
    pump(*kv_tasks)
    drain(y_task)
    outy[...] = (yv[x, place.z].astype(F32) + how[...]).astype(BF)
    saves = [load(outy, out_y)]
    pump(*q_tasks)
    drain(sum_task)
    mark("dx")
    g_pre, g_act = g8v[x, zl, 0:1, :], g8v[x, zl, 2:3, 0:128]
    f_pre, f_act = g8v[x, zl, 1:2, :], g8v[x, zl, 2:3, 128:256]
    line = blocks[x, zl, T:TS, :].astype(F32)
    line = jnp.concatenate([line[0:1], line[1:2], line[2:3, 0:128]], axis=1)
    stat[...] = jnp.broadcast_to(line, (128, 640)).T

    def own_norm(here, there, lanes, gain_f, gain_a, width):
        s2_, s1_ = r2v[there, 0:1], r1v[there, 0:1]
        back, unit = dv8[x, zl, here, lanes].astype(F32), hv[x, zl, here, lanes].astype(F32) * s2_
        dh = cotv[here, lanes] + s2_ * (back * gain_f - unit * mean[there, 0:1])
        gain_f_grad = jnp.sum(back * unit, axis=0, keepdims=True)
        back, unit = blocks[x, zl, here, lanes].astype(F32), xv[here, lanes].astype(F32) * s1_
        outx[here, lanes] = dh + s1_ * (back * gain_a - unit * (stat[there, 0:1] / width))
        return jnp.sum(back * unit, axis=0, keepdims=True), gain_f_grad

    pre = [own_norm(pl.ds(240 * i, 240), pl.ds(240 * i, 240), pl.ds(0, 256), f_pre, g_pre, 2048) for i in range(2)]
    act = [own_norm(pl.ds(480, 64), pl.ds(480 + 64 * i, 64), pl.ds(128 * i, 128), f_act, g_act, 1024) for i in range(2)]
    gains[...] = jnp.concatenate(
        [pre[0][0] + pre[1][0], pre[0][1] + pre[1][1],
         jnp.concatenate([act[0][0] + act[1][0], act[0][1] + act[1][1]], axis=1), jnp.zeros((5, 256), F32)], axis=0)
    saves.append(load(outx, out_x))
    g_task = small_total(comm, gains16, gains2, gains, gsum)
    pump(g_task)
    mark("tail")
    pump(g_task)
    pump(*kv_tasks)
    pump(g_task)
    pump(*q_tasks)
    for task in q_tasks + kv_tasks + late:
        drain(task)
    drain(g_task)
    saves += [load(gsum, out_g), load(gkv.at[y, zh, core], out_kv), load(gkva.at[y, zh, core], out_kva), load(gq.at[y, zh, core], out_q), load(gqa.at[y, zh, core], out_qa)]
    saves += [load(g2v.at[y, zh, core], out_s2.at[zh]), load(z2, out_s2.at[1 - zh])]
    saves += [load(g3v.at[y, zh, core], out_s3.at[zh]), load(z3, out_s3.at[1 - zh])]
    for copy in saves:
        copy.wait()
    mark(None)
    comm.close()


def attend_back(lens, *args):
    outs = [((2, 128, 768), BF), ((2, 128, 768), BF), ((128, 512), BF), ((64, 512), BF), ((128, 128), BF), ((64, 128), BF), ((T, 256), F32),
            ((T, 256), BF), ((8, 256), F32)]
    vm = lambda *s: pltpu.VMEM(s, BF)
    vf = lambda *s: pltpu.VMEM(s, F32)
    wide = lambda n, c: (4, 2, 2, n, c)
    back = [(128, 768), (128, 768), (128, 512), (128, 128), (64, 512), (64, 128)]
    scratch = [vm(4, 2, T, 256), vm(4, 2, T, 256), vm(4, 2, T, 256), vf(608, 128), vf(608, 128), vf(4, 2, 8, 256),
               vm(4, 2, 2, 128, 512), vm(4, 2, 2, 64, 512), vm(4, 2, 2, 128, 512), vm(4, 2, 2, 64, 512),
               vm(480, 2048), vm(128, 1024), vm(4, 2, KEYS, 256), vm(T, 256), vf(T, 256), vm(*wide(128, 768)),
               vm(*wide(128, 768)), vm(4, 4, T, 256), vf(T, 256)]
    scratch += [vf(608, 128), vm(480, 2048), vm(128, 1024), vf(8, 128), vm(2, 304, 256), vm(480, 768), vm(128, 768),
                vf(640, 128), vf(8, 256), vf(8, 256), vf(8, 8, 256), vf(2, 8, 256), vf(T, 256), vm(T, 256)]
    scratch += [vm(*wide(n, c)) for n, c in back[2:]]
    scratch += [vm(4, 2, 304, 128), vm(4, 2, TS, 256)] + LAND_16 + [vm(2, TS, 256)] * 3 + [vm(TS, 256)] + [vm(2, 304, 128)] * 3 + [vm(304, 128)]
    scratch += [vm(4, 2, n, c) for n, c in back] + [vm(3, 2, n, c) for n, c in back] + [vm(n, c) for n, c in back]
    return pl.pallas_call(
        attend_back_kernel,
        out_shape=[jax.ShapeDtypeStruct(s, d) for s, d in outs],
        in_specs=[pl.BlockSpec(memory_space=pltpu.SMEM)] + [ANY] * len(args),
        out_specs=[ANY] * len(outs),
        scratch_shapes=scratch + SEM_SCRATCH,
        compiler_params=pltpu.CompilerParams(collective_id=3, has_side_effects=True, vmem_limit_bytes=VMEM_CAP),
        name="attend_back",
    )(lens, *args)
def local(x_pre, x_act, lengths, cot_pre, cot_act, attn_gain_pre, query_pre, key_pre, value_pre, out_pre, ffn_gain_pre,
          gate_pre, up_pre, down_pre, attn_gain_act, query_act, key_act, value_act, out_act, ffn_gain_act, gate_act,
          up_act, down_act):
    wf, wfa = pack_hidden(gate_pre, up_pre, down_pre), pack_hidden(gate_act, up_act, down_act)[:, 0]
    wq, wqa = jnp.concatenate([query_pre, out_pre.T], axis=1), jnp.concatenate([query_act, out_act.T], axis=1)
    kvs = jnp.concatenate([jnp.concatenate([key_pre, value_pre], axis=1), jnp.concatenate([key_act, value_act], axis=1)])
    kvs = jnp.pad(kvs, ((0, 0), (0, 64)))
    xb, cot = pack_tokens(x_pre, x_act), pack_tokens(cot_pre, cot_act)
    gb = jnp.pad(jnp.stack([attn_gain_pre, ffn_gain_pre, jnp.concatenate([attn_gain_act, ffn_gain_act])]), ((0, 5), (0, 0)))
    (f, fa, qo, qoa, kv, kva, g8, n1p, n1a, qkvo, r1, h_own, h16, n2p, n2a, r2) = attend(
        lengths, wf, wfa, wq, wqa, kvs, xb, gb)
    s0, s1, sa, g2, g3, d8, yt, c8 = feed_forward(f, fa, n2p, n2a, cot.astype(BF))
    s2, s3, sq, sqa, skv, skva, gx, y, gains = attend_back(
        lengths, d8, h16, c8, r2, r1, g8, qo, qoa, kv, kva, n1p, n1a, qkvo, xb, cot, g2, g3, yt, h_own)
    unact = lambda m: m.reshape(64, 2, 128)[:50].transpose(1, 0, 2)

    def open_hidden(m, n):
        m = m.astype(F32).reshape(2, -1, n, 768).transpose(2, 0, 1, 3)
        gate, up, down = (m[..., 256 * j:256 * j + 256].reshape(n, -1) for j in range(3))
        return gate, up, down.T

    dgate_p, dup_p, ddown_p = open_hidden(jnp.stack([s0, s1, s2, s3], axis=1), 128)
    dgate_a, dup_a, ddown_a = open_hidden(sa, 64)
    sq, sqa, skv, skva = (m.astype(F32) for m in (sq, sqa, skv, skva))
    return (y[:480].reshape(2, 240, 256), unact(y[480:]), gx[:480].reshape(2, 240, 256), unact(gx[480:]),
            gains[0], sq[:, :256], skv[:, :32], skv[:, 32:64], sq[:, 256:].T, gains[1], dgate_p, dup_p, ddown_p,
            gains[2, :128], sqa[:, :256], skva[:, :32], skva[:, 32:64], sqa[:, 256:].T, gains[2, 128:],
            dgate_a, dup_a, ddown_a)


def solution(mesh):
    tok, row, col, vec = P("wide", None, "narrow"), P("wide", "narrow"), P("narrow", "wide"), P("narrow")
    expert = (vec, row, row, row, col, vec, row, row, col)
    return jax.shard_map(
        local, mesh=mesh, in_specs=(tok, tok, P("wide"), tok, tok) + expert + expert,
        out_specs=(tok,) * 4 + expert + expert, check_vma=False)
```

```python
import functools
import jax
import jax.numpy as jnp
from jax import lax
from jax.experimental import pallas as pl
from jax.experimental.pallas import tpu as pltpu
from jax.sharding import PartitionSpec as P

MESH = pl.DeviceIdType.MESH
BF = jnp.bfloat16
F32 = jnp.float32
SEMS = 256
LOCAL_SEMS = 48
VMEM_CAP = 62 * 1024 * 1024


class Place:
    def __init__(self):
        wide, narrow = lax.axis_index("wide"), lax.axis_index("narrow")
        self.core = lax.rem(wide, 2)
        self.zh = lax.rem(lax.div(wide, 2), 2)
        self.y = lax.div(wide, 4)
        self.zl = lax.rem(narrow, 2)
        self.x = lax.div(narrow, 2)
        self.z = self.zh * 2 + self.zl

    def wide_at(self, y, zh, core):
        return (y * 2 + zh) * 2 + core

    def coord(self, axis):
        return {"x": self.x, "y": self.y, "z": self.z}[axis]

    def off(self, axis, step):
        return lax.rem(self.coord(axis) + step + 4, 4)

    def peer(self, name):
        if name == "sib":
            return {"wide": self.wide_at(self.y, self.zh, 1 - self.core)}
        if name == "z2":
            return {"wide": self.wide_at(self.y, 1 - self.zh, self.core)}
        if name == "zl":
            return {"narrow": self.x * 2 + 1 - self.zl}
        if name[0] == "w":
            step, flip = int(name[1]), int(name[2])
            zh = 1 - self.zh if flip else self.zh
            return {"wide": self.wide_at(self.off("y", step), zh, self.core)}
        axis, step = name[0], 1 if name[1] == "+" else -1
        at = self.off(axis, step)
        if axis == "y":
            return {"wide": self.wide_at(at, self.zh, self.core)}
        if axis == "x":
            return {"narrow": at * 2 + self.zl}
        return {"wide": self.wide_at(self.y, lax.div(at, 2), self.core), "narrow": self.x * 2 + lax.rem(at, 2)}


class Link:
    def __init__(self, out, into):
        self.out, self.into = out, into

    def arrive(self):
        self.into.wait_recv()

    def left(self):
        self.out.wait_send()


class Comm:
    def __init__(self, send_sems, recv_sems, local_sems):
        self.place = Place()
        self.send_sems, self.recv_sems, self.local_sems = send_sems, recv_sems, local_sems
        self.count, self.local_count = 0, 0
        self.links = []

    def enter(self, peers):
        barrier = pltpu.get_barrier_semaphore()
        for name in peers:
            pl.semaphore_signal(barrier, inc=1, device_id=self.place.peer(name), device_id_type=MESH)
        pl.semaphore_wait(barrier, len(peers))

    def send(self, src, dst, name, incoming):
        index = self.count
        self.count += 1
        assert index < SEMS
        make = lambda to: pltpu.make_async_remote_copy(
            src_ref=src, dst_ref=to, send_sem=self.send_sems.at[index], recv_sem=self.recv_sems.at[index],
            device_id=self.place.peer(name), device_id_type=MESH)
        out = make(dst)
        out.start()
        link = Link(out, make(incoming))
        self.links.append(link)
        return link

    def local(self, src, dst):
        index = self.local_count
        self.local_count += 1
        assert index < LOCAL_SEMS
        copy = pltpu.make_async_copy(src, dst, self.local_sems.at[index])
        copy.start()
        return copy

    def settle(self):
        for link in self.links:
            link.left()
        self.links = []

    def close(self):
        self.settle()

    def ring_gather(self, axis, view, parts, own=None):
        place = self.place
        at = lambda step: place.off(axis, step)
        src = own if own is not None else (lambda part: view(at(0), part))
        up_first = sorted(parts, key=lambda part: -part[1])
        plus = [(way, p, self.send(src(p), view(at(0), p), axis + "+", view(at(-1), p))) for p, way in up_first]
        minus = [(way, p, self.send(src(p), view(at(0), p), axis + "-", view(at(1), p))) for p, way in up_first[::-1]]
        yield
        rest = []
        for way, p, link in plus:
            if way > 0:
                link.arrive()
                rest.append(self.send(view(at(-1), p), view(at(-1), p), axis + "+", view(at(-2), p)))
        for way, p, link in minus:
            if way < 0:
                link.arrive()
                rest.append(self.send(view(at(1), p), view(at(1), p), axis + "-", view(at(2), p)))
        yield
        for way, p, link in plus:
            if way < 0:
                link.arrive()
        for way, p, link in minus:
            if way > 0:
                link.arrive()
        for link in rest:
            link.arrive()

    def pair_ring_gather(self, pair, axis, view, parts, own, give, whole, swap_first=False):
        place = self.place
        mine = {"z2": place.zh, "zl": place.zl}[pair]
        here = place.coord(axis)
        first = self.ring_gather(axis, lambda k, p: view(k, mine, p), parts, own)
        if not swap_first:
            next(first)
            yield
        swap = self.send(give, view(here, mine, whole), pair, view(here, 1 - mine, whole))
        yield
        if swap_first:
            next(first)
            yield
        next(first)
        yield
        swap.arrive()
        second = self.ring_gather(axis, lambda k, p: view(k, 1 - mine, p), parts)
        next(second)
        yield
        next(second)
        yield
        drain(first)
        drain(second)

    def plane_gather(self, view, parts_x, parts_z, own=None, ready=None):
        place = self.place
        every = slice(None)
        ax = self.ring_gather("x", lambda k, p: view(k, place.z, p), parts_x, own)
        bz = self.ring_gather("z", lambda k, p: view(place.x, k, p), parts_z, own)
        next(ax), next(bz)
        yield
        next(ax), next(bz)
        yield
        if ready is not None:
            ready()
        drain(ax)
        az = self.ring_gather("z", lambda k, p: view(every, k, p), parts_x)
        next(az)
        drain(bz)
        bx = self.ring_gather("x", lambda k, p: view(k, every, p), parts_z)
        next(bx)
        yield
        next(az), next(bx)
        yield
        drain(az), drain(bx)

    def ring_sum(self, axis, view, parts, relay, plus, minus, split=False):
        place = self.place
        at = lambda step: place.off(axis, step)
        near = {1: lambda p: self.send(view(at(1), p), plus(p), axis + "+", plus(p)),
                -1: lambda p: self.send(view(at(-1), p), minus(p), axis + "-", minus(p))}
        far = [(p, way, self.send(view(at(2), p), relay(p), axis + ("+" if way > 0 else "-"), relay(p))) for p, way in parts]
        if split:
            yield
        links = [near[-way](p) for p, way in parts]
        yield
        for p, way, link in far:
            link.arrive()
            add_to(view(at(way), p), relay(p))
            links.append(near[way](p))
        yield
        for link in links:
            link.arrive()
        for p, _ in parts:
            add_to(view(at(0), p), plus(p), minus(p))


def add_to(ref, *others):
    total = ref[...].astype(F32)
    for other in others:
        total = total + other[...].astype(F32)
    ref[...] = total.astype(ref.dtype)


def drain(task):
    for _ in task:
        pass


def rows(lo, hi):
    return pl.ds(lo, hi - lo)
T = 544
CH = 4


def halves(n):
    return [(rows(0, n // 2), 1), (rows(n // 2, n), -1)]


PARTS_8 = [(rows(0, 272), 1), (rows(272, 544), -1)]
PARTS_A = [(rows(0, 144), 1), (rows(144, 272), -1)]
PARTS_B = [(rows(272, 416), 1), (rows(416, 544), -1)]
PEERS = ("y+", "y-", "z2", "sib", "x+", "x-", "z+", "z-")


def wide_gather(comm, out, own, give, n, parts=None, swap_first=False):
    place = comm.place
    core = place.core
    copy = comm.local(own, out.at[place.y, place.zh, core])
    task = comm.pair_ring_gather(
        "z2", "y", lambda k, j, p: out.at[k, j, core, p], parts or halves(n),
        lambda p: own.at[p], give, slice(None), swap_first)
    yield from task
    copy.wait()
    link = comm.send(out.at[:, :, core], out.at[:, :, core], "sib", out.at[:, :, 1 - core])
    yield
    link.arrive()


def block_gather(comm, out, own, parts):
    place = comm.place
    copy = comm.local(own, out.at[place.x, place.zl])
    yield from comm.pair_ring_gather(
        "zl", "x", lambda k, j, p: out.at[k, j, p], parts, lambda p: own.at[p], own, slice(None))
    copy.wait()


def plane_spread(comm, out, own):
    place = comm.place
    copy = comm.local(own, out.at[place.x, place.z])
    yield from comm.plane_gather(lambda k, j, p: out.at[k, j, p], PARTS_A, PARTS_B, lambda p: own.at[p], copy.wait)


def block_sum(comm, blocks, lands, swap, parts, z=None):
    place = comm.place
    relay, plus, minus = lands
    upto = pl.ds(0, sum(p.size for p, _ in parts))
    xs = comm.ring_sum(
        "x", lambda k, p: blocks.at[k, :, p], parts,
        lambda p: relay.at[:, p], lambda p: plus.at[:, p], lambda p: minus.at[:, p], z is not None)
    next(xs)
    yield
    if z is not None:
        z_rows, z_parts, z_land, z_lands = z
        next(xs)
        link = comm.send(blocks.at[:, 1 - place.zl, z_rows], z_land, "zl", z_land)
        yield
    next(xs)
    yield
    if z is not None:
        link.arrive()
        add_to(blocks.at[:, place.zl, z_rows], z_land)
        zs = comm.ring_sum("x", lambda k, p: blocks.at[k, place.zl, p], z_parts,
                           *[(lambda p, land=land: land.at[pl.ds(p.start - z_rows.start, p.size)]) for land in z_lands])
        next(zs)
        yield
    drain(xs)
    last = comm.send(blocks.at[place.x, 1 - place.zl, upto], swap, "zl", swap)
    if z is not None:
        next(zs)
    yield
    last.arrive()
    add_to(blocks.at[place.x, place.zl, upto], swap)
    if z is not None:
        drain(zs)


def plane_sum(comm, blocks, lands_far, lands_near):
    place = comm.place
    az = comm.ring_sum("z", lambda k, p: blocks.at[:, k, p], PARTS_A,
                       lambda p: lands_far.at[0, :, p], lambda p: lands_far.at[1, :, p], lambda p: lands_far.at[2, :, p], True)
    bx = comm.ring_sum("x", lambda k, p: blocks.at[k, :, p], PARTS_B,
                       lambda p: lands_far.at[0, :, p], lambda p: lands_far.at[1, :, p], lambda p: lands_far.at[2, :, p], True)
    for _ in range(3):
        next(az), next(bx)
        yield
    drain(az)
    ax = comm.ring_sum("x", lambda k, p: blocks.at[k, place.z, p], PARTS_A,
                       lambda p: lands_near.at[0, p], lambda p: lands_near.at[1, p], lambda p: lands_near.at[2, p])
    next(ax)
    drain(bx)
    bz = comm.ring_sum("z", lambda k, p: blocks.at[place.x, k, p], PARTS_B,
                       lambda p: lands_near.at[0, p], lambda p: lands_near.at[1, p], lambda p: lands_near.at[2, p])
    next(bz)
    yield
    next(ax), next(bz)
    yield
    drain(ax), drain(bz)


CHIPS = [(step, flip) for flip in range(2) for step in range(4) if step or flip]


def small_total(comm, slots, pair, own, out):
    place = comm.place
    mine = place.y * 2 + place.zh
    links = []
    for step, flip in CHIPS:
        back = place.off("y", -step) * 2 + (1 - place.zh if flip else place.zh)
        links.append(comm.send(own, slots.at[mine], f"w{step}{flip}", slots.at[back]))
    slots[mine] = own[...]
    yield
    for link in links:
        link.arrive()
    pair[0] = sum(slots[i] for i in range(8))
    link = comm.send(pair.at[0], pair.at[1], "sib", pair.at[1])
    yield
    link.arrive()
    out[...] = pair[0] + pair[1]


def wide_sum(comm, grad, half, relay, plus, minus, swap, n, add):
    place = comm.place
    core, zh = place.core, place.zh
    link = comm.send(grad.at[:, :, 1 - core], half, "sib", half)
    yield
    link.arrive()
    def fold(k, carry):
        add_to(grad.at[k, :, core], half.at[k])
        return carry
    lax.fori_loop(0, 4, fold, 0)
    yield from comm.ring_sum(
        "y", lambda k, p: grad.at[k, :, core, p], halves(n),
        lambda p: relay.at[:, p], lambda p: plus.at[:, p], lambda p: minus.at[:, p])
    link = comm.send(grad.at[place.y, 1 - zh, core], swap, "z2", swap)
    yield
    link.arrive()
    if add:
        add_to(grad.at[place.y, zh, core], swap)


SEM_SCRATCH = [pltpu.SemaphoreType.DMA((SEMS,)), pltpu.SemaphoreType.DMA((SEMS,)), pltpu.SemaphoreType.DMA((LOCAL_SEMS,))]
ANY = pl.BlockSpec(memory_space=pl.ANY)
INSIDE = pl.BlockSpec(memory_space=pltpu.VMEM)


X_ROWS = 400
X_PARTS = [(rows(0, 208), 1), (rows(208, 400), -1)]


def block_lands(count):
    z = count - X_ROWS
    return ([pltpu.VMEM((2, X_ROWS, 256), BF)] * 3 + [pltpu.VMEM((X_ROWS, 256), BF), pltpu.VMEM((4, z, 256), BF)]
            + [pltpu.VMEM((z, 256), BF)] * 3)


def block_sum_both(comm, blocks, lands, count):
    z = (rows(X_ROWS, count), [(rows(X_ROWS, 480), 1), (rows(480, count), -1)], lands[4], lands[5:8])
    return block_sum(comm, blocks, lands[0:3], lands[3], X_PARTS, z)


LAND_16 = [pltpu.VMEM((3, 4, T, 256), BF), pltpu.VMEM((3, T, 256), BF)]


EPSILON = 1e-06
MASKED = -1000000000.0
KEYS = 384


def dot(a, b, ca, cb):
    return lax.dot_general(a, b, (((ca,), (cb,)), ((), ())), preferred_element_type=F32)


_open = []


def mark(name):
    if _open:
        _open.pop().__exit__(None, None, None)
    if name:
        scope = jax.named_scope(name)
        scope.__enter__()
        _open.append(scope)


def pump(*tasks):
    for task in tasks:
        next(task, None)


def seen(length):
    s = lax.broadcasted_iota(jnp.int32, (304, KEYS), 0)
    t = lax.broadcasted_iota(jnp.int32, (304, KEYS), 1)
    live = (t < 192) | ((t >= 240) & (t < 290)) | ((t < 240) & (t - 192 < length))
    return live & ((t < 240) | (s >= 240))


def soft(q, k, length):
    scores = dot(q, k, 1, 1) * 0.0625
    scores = jnp.where(seen(length), scores, MASKED)
    weights = jnp.exp(scores - jnp.max(scores, axis=1, keepdims=True))
    return weights / jnp.sum(weights, axis=1, keepdims=True)


def pairs8():
    return [(x, zl) for x in range(4) for zl in range(2)]


def norm_block_rows(get, gain, width, put):
    total = sum(jnp.sum(get(n) * get(n), axis=1, keepdims=True) for n in range(8))
    scale = lax.rsqrt(total / (8 * width) + EPSILON)
    for n in range(8):
        put(n, (get(n) * scale * gain(n)).astype(BF))
    return scale


def act_rows(act, spare):
    spare[...] = jnp.zeros((64, 256), F32)
    rows_of = act[...].astype(F32)
    for i in range(2):
        spare[0:50, 128 * i:128 * i + 128] = rows_of[:, i, :]
    return spare[...]


def turned(m):
    return m.astype(F32).T.astype(BF)


def attend_kernel(lens, x_pre, x_act, attn_gain_pre, query_pre, key_pre, value_pre, out_pre, ffn_gain_pre, gate_pre, up_pre,
                  down_pre, attn_gain_act, query_act, key_act, value_act, out_act, ffn_gain_act, gate_act, up_act, down_act,
                  out_xb, out_f, out_fa, out_q, out_qa, out_kv, out_kva, out_g, out_n1p, out_n1a, out_qkvo, out_r1,
                  out_h, out_h16, out_n2p, out_n2a, out_r2,
                  kv8, kvf, qo, qoa, kv, kva, x8, g8, n1p, n1a, qkvo, r1, xv, hv, full, n2p, n2a, r2,
                  blocks, l0, l1, l2, l3, l4, l5, l6, l7, wf, wfa, wq, wqa, kvs, gb, spare, *sems):
    comm = Comm(*sems)
    place = comm.place
    zh = place.zh
    for i in range(2):
        xv[240 * i:240 * i + 240, :] = x_pre[i]
    xv[480:544, :] = act_rows(x_act, spare).astype(BF)
    lane = lax.broadcasted_iota(jnp.int32, (32, 128), 1)
    row = lax.broadcasted_iota(jnp.int32, (32, 128), 0)
    spread = [(lane == row + 32 * j).astype(F32).astype(BF) for j in range(2)]
    kvs[0:128, :] = (dot(key_pre[...], spread[0], 0, 0) + dot(value_pre[...], spread[1], 0, 0)).astype(BF)
    kvs[128:192, :] = (dot(key_act[...], spread[0], 0, 0) + dot(value_act[...], spread[1], 0, 0)).astype(BF)
    gb[...] = jnp.concatenate([attn_gain_pre[...], ffn_gain_pre[...],
                               jnp.concatenate([attn_gain_act[...], ffn_gain_act[...]], axis=1), jnp.zeros((5, 256), F32)], axis=0)
    wq[:, 0:256], wqa[:, 0:256] = query_pre[...], query_act[...]
    wq[:, 256:512], wqa[:, 256:512] = turned(out_pre[...]), out_act[...]
    zero = jnp.zeros((KEYS - 304, 256), BF)
    for i in range(2):
        for j in (1, 2):
            qkvo[j, i, 304:KEYS, :] = zero
    comm.enter(PEERS)

    mark('start')
    kv_task = block_gather(comm, kv8, kvs, halves(192))
    g_task = block_gather(comm, g8, gb, [(slice(None), 1)])
    x_task = block_gather(comm, x8, xv, PARTS_8)
    q_tasks = [wide_gather(comm, qo, wq, wq, 128), wide_gather(comm, qoa, wqa, wqa, 64)]
    f_tasks = [wide_gather(comm, out_f.at[i], wf.at[zh, i], wf.at[1 - zh, i], 128, None, True) for i in range(CH)]
    f_tasks.append(wide_gather(comm, out_fa, wfa.at[zh], wfa.at[1 - zh], 64, None, True))
    pump(kv_task), pump(kv_task)
    pump(g_task), pump(g_task)
    pump(x_task), pump(x_task)
    pump(*q_tasks)
    for h in range(2):
        for i in range(CH):
            here = slice(1024 * h + 256 * i, 1024 * h + 256 * i + 256)
            wf[h, i, :, 0:256], wf[h, i, :, 256:512] = gate_pre[:, here], up_pre[:, here]
            wf[h, i, :, 512:768] = turned(down_pre[here, :])
        here = slice(256 * h, 256 * h + 256)
        wfa[h, :, 0:256], wfa[h, :, 256:512] = gate_act[:, here], up_act[:, here]
        wfa[h, :, 512:768] = down_act[:, here]
    pump(kv_task), pump(kv_task)
    pump(g_task), pump(g_task)
    pump(x_task)
    pump(kv_task), pump(g_task)
    pump(x_task)
    pump(*q_tasks), pump(*q_tasks)
    drain(kv_task)
    total = jnp.zeros((192, 512), F32)
    lane = lax.broadcasted_iota(jnp.int32, (128, 512), 0)
    col = lax.broadcasted_iota(jnp.int32, (128, 512), 1)
    for n in range(8):
        pick = ((lane < 32) & (col == 32 * n + lane)) | ((lane >= 32) & (lane < 64) & (col == 224 + 32 * n + lane))
        total = total + dot(kv8[n // 2, n % 2], pick.astype(F32).astype(BF), 1, 0)
    kvf[...] = total.astype(BF)
    kv_a, kv_b = kvf.at[0:128], kvf.at[128:192]
    kv_tasks = [wide_gather(comm, kv, kv_a, kv_a, 128), wide_gather(comm, kva, kv_b, kv_b, 64)]
    pump(*kv_tasks), pump(*kv_tasks)
    pump(*q_tasks)
    pump(*f_tasks)
    pump(x_task)
    drain(g_task)
    pump(*kv_tasks)
    pump(*q_tasks)
    drain(x_task)

    mark('norm1')
    for i in range(2):
        here = pl.ds(240 * i, 240)
        get = lambda n: x8[n // 2, n % 2, here, :].astype(F32)
        def put(n, v):
            n1p[here, 256 * n:256 * n + 256] = v
        r1[here, :] = jnp.broadcast_to(norm_block_rows(get, lambda n: g8[n // 2, n % 2, 0:1, :], 256, put), (240, 128))
        low = pl.ds(480, 64)
        get = lambda n: x8[n // 2, n % 2, low, 128 * i:128 * i + 128].astype(F32)
        def put(n, v):
            n1a[64 * i:64 * i + 64, 128 * n:128 * n + 128] = v
        r1[480 + 64 * i:544 + 64 * i, :] = jnp.broadcast_to(
            norm_block_rows(get, lambda n: g8[n // 2, n % 2, 2:3, 0:128], 128, put), (64, 128))
    pump(*kv_tasks)
    pump(*kv_tasks)
    pump(*q_tasks)
    pump(*f_tasks)
    for task in q_tasks:
        drain(task)
    mark('qkv')
    def queries(i, carry):
        here = pl.ds(pl.multiple_of(240 * i, 16), 240)
        qkvo[0, i, 0:240, :] = dot(n1p[here, :], qo[:, :, :, :, 0:256].reshape(2048, 256), 1, 0).astype(BF)
        return carry
    lax.fori_loop(0, 2, queries, 0)
    pump(*kv_tasks)
    for task in kv_tasks:
        drain(task)
    def keys(i, carry):
        here = pl.ds(pl.multiple_of(240 * i, 16), 240)
        for j in range(2):
            qkvo[1 + j, i, 0:240, :] = dot(
                n1p[here, :], kv[:, :, :, :, 256 * j:256 * j + 256].reshape(2048, 256), 1, 0).astype(BF)
        return carry
    lax.fori_loop(0, 2, keys, 0)
    low = [dot(n1a[...], qoa[:, :, :, :, 0:256].reshape(1024, 256), 1, 0).astype(BF)]
    for j in range(2):
        low.append(dot(n1a[...], kva[:, :, :, :, 256 * j:256 * j + 256].reshape(1024, 256), 1, 0).astype(BF))
    for i in range(2):
        for j in range(3):
            qkvo[j, i, 240:304, :] = low[j][64 * i:64 * i + 64]
    saves = [comm.local(qo, out_q), comm.local(qoa, out_qa), comm.local(kv, out_kv), comm.local(kva, out_kva),
             comm.local(n1p, out_n1p), comm.local(n1a, out_n1a), comm.local(r1, out_r1), comm.local(g8, out_g)]
    mark('attn')
    for i in range(2):
        probs = soft(qkvo[0, i, 0:304, :], qkvo[1, i], lens[i])
        qkvo[3, i, 0:304, :] = dot(probs.astype(BF), qkvo[2, i], 1, 0).astype(BF)
    saves.append(comm.local(qkvo, out_qkvo))
    mark('outproj')
    oa = jnp.concatenate([qkvo[3, 0, 240:304, :], qkvo[3, 1, 240:304, :]], axis=0)

    def terms(step):
        k = place.off("x", step)
        for j in range(2):
            weight = qo[k, j, :, :, 256:512].reshape(256, 256)
            for i in range(2):
                blocks[k, j, 240 * i:240 * i + 240, :] = dot(qkvo[3, i, 0:240, :], weight, 1, 1).astype(BF)
            small = dot(oa, qoa[k, j, :, :, 256:512].reshape(128, 256), 1, 1).astype(BF)
            for i in range(2):
                blocks[k, j, 480:544, 128 * i:128 * i + 128] = small[64 * i:64 * i + 64]

    mark('rs8')
    sum_task = block_sum_both(comm, blocks, (l0, l1, l2, l3, l4, l5, l6, l7), T)
    terms(2)
    pump(sum_task)
    terms(1), terms(3), terms(0)
    pump(sum_task)
    pump(f_tasks[0])
    pump(sum_task)
    pump(sum_task)
    pump(f_tasks[1], f_tasks[2], f_tasks[0])
    pump(sum_task)
    pump(f_tasks[3], f_tasks[4], f_tasks[1])
    drain(sum_task)
    mark('hmake')
    hv[...] = xv[...].astype(F32) + blocks[place.x, place.zl].astype(F32)
    full[place.x, place.z] = hv[...].astype(BF)
    saves += [comm.local(hv, out_h), comm.local(xv, out_xb)]
    mark('hplane')
    h_task = comm.plane_gather(lambda k, j, p: full.at[k, j, p], PARTS_A, PARTS_B)
    pump(h_task)
    pump(f_tasks[2], f_tasks[3])
    pump(h_task)
    pump(h_task)
    pump(f_tasks[4], f_tasks[0])
    pump(f_tasks[1])
    pump(h_task)
    pump(f_tasks[2], f_tasks[3], f_tasks[4])
    pump(f_tasks[0], f_tasks[1])
    drain(h_task)
    saves.append(comm.local(full, out_h16))
    mark('norm2')
    for zhi in range(2):
        def rows_norm(i, carry):
            here = pl.ds(pl.multiple_of(240 * i, 16), 240)
            there = pl.ds(pl.multiple_of(480 * zhi + 240 * i, 16), 240)
            get = lambda n: full[n // 2, 2 * zhi + n % 2, here, :].astype(F32)
            def put(n, v):
                n2p[there, 256 * n:256 * n + 256] = v
            scale = norm_block_rows(get, lambda n: g8[n // 2, n % 2, 1:2, :], 256, put)
            r2[zhi, here, :] = jnp.broadcast_to(scale, (240, 128))
            return carry
        lax.fori_loop(0, 2, rows_norm, 0)
        for i in range(2):
            get = lambda n: full[n // 2, 2 * zhi + n % 2, 480:544, 128 * i:128 * i + 128].astype(F32)
            base = 128 * zhi + 64 * i
            def put(n, v):
                n2a[base:base + 64, 128 * n:128 * n + 128] = v
            scale = norm_block_rows(get, lambda n: g8[n // 2, n % 2, 2:3, 128:256], 128, put)
            r2[zhi, 480 + 64 * i:544 + 64 * i, :] = jnp.broadcast_to(scale, (64, 128))
    mark('tail')
    saves += [comm.local(n2p, out_n2p), comm.local(n2a, out_n2a), comm.local(r2.at[zh], out_r2)]
    for task in f_tasks:
        drain(task)
    for copy in saves:
        copy.wait()
    mark(None)
    comm.close()


def attend(lens, *args):
    wide5 = lambda n, c: (4, 2, 2, n, c)
    outs = [((T, 256), BF), ((CH,) + wide5(128, 768), BF), (wide5(64, 768), BF), (wide5(128, 512), BF), (wide5(64, 512), BF),
            (wide5(128, 512), BF), (wide5(64, 512), BF), ((4, 2, 8, 256), F32),
            ((480, 2048), BF), ((128, 1024), BF), ((4, 2, KEYS, 256), BF), ((608, 128), F32), ((T, 256), F32),
            ((4, 4, T, 256), BF), ((960, 2048), BF), ((256, 1024), BF), ((608, 128), F32)]
    vm = pltpu.VMEM
    scratch = [vm((4, 2, 192, 128), BF), vm((192, 512), BF)] + [vm(s, d) for s, d in outs[3:7]] + [
        vm((4, 2, T, 256), BF), vm((4, 2, 8, 256), F32), vm((480, 2048), BF), vm((128, 1024), BF),
        vm((4, 2, KEYS, 256), BF), vm((608, 128), F32), vm((T, 256), BF), vm((T, 256), F32), vm((4, 4, T, 256), BF),
        vm((960, 2048), BF), vm((256, 1024), BF), vm((2, 608, 128), F32), vm((4, 2, T, 256), BF)] + block_lands(T)
    scratch += [vm((2, CH, 128, 768), BF), vm((2, 64, 768), BF), vm((128, 512), BF), vm((64, 512), BF), vm((192, 128), BF),
                vm((8, 256), F32), vm((64, 256), F32)]
    return pl.pallas_call(
        attend_kernel,
        out_shape=[jax.ShapeDtypeStruct(s, d) for s, d in outs],
        in_specs=[pl.BlockSpec(memory_space=pltpu.SMEM)] + [INSIDE] * len(args),
        out_specs=[ANY] * len(outs),
        scratch_shapes=scratch + SEM_SCRATCH,
        compiler_params=pltpu.CompilerParams(collective_id=0, has_side_effects=True, vmem_limit_bytes=VMEM_CAP),
        name="attend",
    )(lens, *args)
EARLY = 2
TILE = 240


def gelu_parts(z):
    a, b = 0.7978845608028654, 0.044715
    t = jnp.tanh(a * (z + b * z * z * z))
    half = 0.5 * (1.0 + t)
    return z * half, half + 0.5 * z * (1.0 - t * t) * a * (1.0 + 3.0 * b * z * z)


def side_rows(full, z_low, base, count):
    return jnp.concatenate([full[x, z_low + zl, pl.ds(base, count), :] for x, zl in pairs8()], axis=1)


def feed_forward_kernel(f, fa, n2p, n2a, cot_pre, cot_act, *refs):
    out_s, out_late, refs = refs[:EARLY + 1], refs[EARLY + 1:CH + 1], refs[CH + 1:]
    out_d8, out_y, out_c, wv, wav, np_, na, gc, ga, dd, aa, dda, aaa, bb, bf, bn, d8, grad_act, cb, spare = refs[:20]
    lands = [refs[20 + 3 * i:23 + 3 * i] for i in range(EARLY + 1)]
    comm = Comm(*refs[-3:])
    place = comm.place
    loads = [comm.local(n2p, np_), comm.local(f.at[0], wv.at[0]), comm.local(n2a, na),
             comm.local(f.at[1], wv.at[1]), comm.local(f.at[2], wv.at[2]), comm.local(f.at[3], wv.at[3]),
             comm.local(fa, wav)]
    for i in range(2):
        cb[240 * i:240 * i + 240, :] = cot_pre[i].astype(BF)
    cb[480:544, :] = act_rows(cot_act, spare).astype(BF)
    c_task = plane_spread(comm, gc, cb)
    comm.enter(PEERS)
    pump(c_task)
    mark("units")
    loads[0].wait()

    def gate_up(left, weight):
        both = dot(left, weight, 1, 0)
        up = both[:, 256:512]
        value, slope = gelu_parts(both[:, 0:256])
        return (value * up).astype(BF), (up * slope).astype(BF), value.astype(BF)

    for i in range(CH):
        loads[(1, 3, 4, 5)[i]].wait()
        def unit(t, carry):
            here = pl.ds(pl.multiple_of(TILE * t, 16), TILE)
            a, b, c = gate_up(np_[here, :], wv[i, :, :, :, :, 0:512].reshape(2048, 512))
            aa[here, 256 * i:256 * i + 256] = a
            dd[here, 512 * i:512 * i + 256] = b
            dd[here, 512 * i + 256:512 * i + 512] = c
            return carry
        lax.fori_loop(0, 4, unit, 0)
        if i in (0, 1):
            pump(c_task)
    loads[2].wait(), loads[6].wait()
    aaa[...], dda[:, 0:256], dda[:, 256:512] = gate_up(na[...], wav[:, :, :, :, 0:512].reshape(1024, 512))

    def product(ref, x, z, left, left_a, lo, hi):
        zh_, zl_ = lax.div(z, 2), lax.rem(z, 2)
        here = pl.ds(pl.multiple_of(480 * zh_, 16), 480)
        rows_w = jnp.concatenate([wv[i, x, zl_, :, :, lo:hi].reshape(256, hi - lo) for i in range(CH)], axis=1)
        ref[0:480, :] = dot(left[here, :], rows_w, 1, 1).astype(BF)
        there = pl.ds(pl.multiple_of(128 * zh_, 16), 128)
        small = dot(left_a[there, :], wav[x, zl_, :, :, lo:hi].reshape(128, hi - lo), 1, 1).astype(BF)
        ref[480:544, 0:128] = small[0:64]
        ref[480:544, 128:256] = small[64:128]

    def down_terms(t, carry):
        x, z = lax.div(t, 4), lax.rem(t, 4)
        product(bb.at[x, z], x, z, aa, aaa, 512, 768)
        return carry

    mark("ydown")
    lax.fori_loop(0, 4, down_terms, 0)
    pump(c_task)
    lax.fori_loop(4, 16, down_terms, 0)
    saves = [comm.local(bb, out_y)]
    mark("cwait")
    drain(c_task)
    saves.append(comm.local(gc.at[:, pl.ds(2 * place.zh, 2)], out_c))
    mark("dact")
    for i in range(CH):
        def dact_unit(t, carry):
            here = pl.ds(pl.multiple_of(TILE * t, 16), TILE)
            rows_c = side_rows(gc, 2 * lax.div(t, 2), pl.multiple_of(TILE * lax.rem(t, 2), 16), TILE)
            dact = dot(rows_c, wv[i, :, :, :, :, 512:768].reshape(2048, 256), 1, 0)
            for j in range(2):
                there = slice(512 * i + 256 * j, 512 * i + 256 * j + 256)
                dd[here, there] = (dact * dd[here, there].astype(F32)).astype(BF)
            return carry
        lax.fori_loop(0, 4, dact_unit, 0)
    for zhi in range(2):
        for i in range(2):
            base = 128 * zhi + 64 * i
            for n in range(8):
                ga[base:base + 64, 128 * n:128 * n + 128] = gc[n // 2, 2 * zhi + n % 2, 480:544, 128 * i:128 * i + 128]
    dact = dot(ga[...], wav[:, :, :, :, 512:768].reshape(1024, 256), 1, 0)
    for j in range(2):
        there = slice(256 * j, 256 * j + 256)
        dda[:, there] = (dact * dda[:, there].astype(F32)).astype(BF)
    saves[0].wait()

    mark("back")
    far_x, far_z = place.off("x", 2), place.off("z", 2)

    def far_terms(t, carry):
        x = jnp.where(t < 4, t, far_x)
        z = jnp.where(t < 4, far_z, lax.rem(far_z + jnp.where(t < 4, 0, t - 3), 4))
        product(bb.at[x, z], x, z, dd, dda, 0, 512)
        return carry

    def near_terms(t, carry):
        x, z = lax.rem(far_x + 1 + lax.div(t, 3), 4), lax.rem(far_z + 1 + lax.rem(t, 3), 4)
        product(bb.at[x, z], x, z, dd, dda, 0, 512)
        return carry

    lax.fori_loop(0, 7, far_terms, 0)
    b_task = plane_sum(comm, bb, bf, bn)
    pump(b_task)
    lax.fori_loop(0, 9, near_terms, 0)
    pump(b_task)
    pump(b_task)

    mark("grads")

    def weight_grads(i):
        def block_rows(y, carry):
            here = pl.ds(pl.multiple_of(512 * y, 512), 512)
            left_n = np_[:, here]
            left_c = jnp.concatenate(
                [jnp.concatenate([gc[y, zl, 0:480, :], gc[y, 2 + zl, 0:480, :]], axis=0) for zl in range(2)], axis=1)
            for j in range(3):
                if j < 2:
                    value = dot(left_n, dd[:, 512 * i + 256 * j:512 * i + 256 * j + 256], 0, 0).astype(BF)
                else:
                    value = dot(left_c, aa[:, 256 * i:256 * i + 256], 0, 0).astype(BF)
                wv[i, y, :, :, :, 256 * j:256 * j + 256] = value.reshape(2, 2, 128, 256)
            return carry
        lax.fori_loop(0, 4, block_rows, 0)

    def act_grads():
        for y in range(4):
            left_n, left_c = na[:, 256 * y:256 * y + 256], ga[:, 256 * y:256 * y + 256]
            for j in range(3):
                value = dot(left_n, dda[:, 256 * j:256 * j + 256], 0, 0) if j < 2 else dot(left_c, aaa[...], 0, 0)
                grad_act[y, :, :, :, 256 * j:256 * j + 256] = value.astype(BF).reshape(2, 2, 64, 256)

    grads = [wv.at[i] for i in range(EARLY)] + [grad_act]
    sums = [wide_sum(comm, grad, s, r.at[0], r.at[1], r.at[2], z, 64 if i == EARLY else 128, False)
            for i, (grad, (s, r, z)) in enumerate(zip(grads, lands))]
    weight_grads(0)
    pump(sums[0])
    weight_grads(1)
    pump(sums[0], sums[1])
    pump(b_task)
    act_grads()
    pump(sums[2])
    pump(b_task)
    pump(sums[1])
    drain(b_task)
    mark("dn2")
    d8[place.x, place.zl] = bb[place.x, place.z]
    d_task = comm.pair_ring_gather("zl", "x", lambda k, j, p: d8.at[k, j, p], PARTS_8,
                                   lambda p: d8.at[place.x, place.zl, p], d8.at[place.x, place.zl], slice(None))
    pump(d_task), pump(d_task)
    pump(sums[0], sums[2])
    weight_grads(2)
    saves.append(comm.local(wv.at[2], out_late[0]))
    pump(d_task)
    pump(sums[1])
    weight_grads(3)
    saves.append(comm.local(wv.at[3], out_late[1]))
    pump(d_task)
    pump(sums[2], sums[0])
    pump(d_task)
    pump(sums[1], sums[2])
    drain(d_task)
    saves.append(comm.local(d8, out_d8))
    mark("sums")
    for task in sums:
        drain(task)
    for grad, (_, _, swap), out in zip(grads, lands, out_s):
        saves.append(comm.local(grad.at[place.y, place.zh, place.core], out.at[place.zh]))
        saves.append(comm.local(swap, out.at[1 - place.zh]))
    for copy in saves[1:]:
        copy.wait()
    mark(None)
    comm.close()


def feed_forward(f, fa, n2p, n2a, cot_pre, cot_act):
    grad = (4, 2, 2, 128, 768)
    outs = [(2, 128, 768)] * EARLY + [(2, 64, 768)] + [grad] * (CH - EARLY) + [(4, 2, T, 256), (4, 4, T, 256), (4, 2, T, 256)]
    vm = lambda *s: pltpu.VMEM(s, BF)
    scratch = [vm(CH, *grad), vm(4, 2, 2, 64, 768), vm(960, 2048), vm(256, 1024), vm(4, 4, T, 256),
               vm(256, 1024), vm(960, 2048), vm(960, 1024), vm(256, 512), vm(256, 256)]
    scratch += [vm(4, 4, T, 256)] + LAND_16 + [vm(4, 2, T, 256), vm(4, 2, 2, 64, 768), vm(T, 256), pltpu.VMEM((64, 256), F32)]
    for n in [128] * EARLY + [64]:
        scratch += [vm(4, 2, n, 768), vm(3, 2, n, 768), vm(n, 768)]
    return pl.pallas_call(
        feed_forward_kernel,
        out_shape=[jax.ShapeDtypeStruct(s, BF) for s in outs],
        in_specs=[ANY] * 4 + [INSIDE] * 2,
        out_specs=[ANY] * len(outs),
        scratch_shapes=scratch + SEM_SCRATCH,
        compiler_params=pltpu.CompilerParams(collective_id=2, has_side_effects=True, vmem_limit_bytes=VMEM_CAP),
        name="feed_forward",
    )(f, fa, n2p, n2a, cot_pre, cot_act)
TS = T + 16
FAR_PEERS = tuple(f"w{step}{flip}" for step, flip in CHIPS if (step, flip) not in ((1, 0), (3, 0), (0, 1)))
KV_PARTS = [(rows(0, 160), 1), (rows(160, 304), -1)]


def attend_back_kernel(lens, d8, h16, c16, r2, r1, g8, qo, qoa, kv, kva, n1p, n1a, qkvo, xb, cot_pre, cot_act, g2, g3, yt, h_own,
                       out_s2, out_s3, out_q, out_qa, out_kv, out_kva, out_x, out_y, out_g,
                       dv8, hv, cv, r2v, r1v, g8v, qov, qoav, kvv, kvav, npv, nav, qv, xv, cotv, g2v, g3v, yv, how,
                       mean, ghp, gha, dhb, dov, dqp, dqa, stat, gains, gsum, gains16, gains2, spare, outx, outy,
                       gq, gkv, gqa, gkva, kvb, blocks, yf, yn, l0, l1, l2, l3, l4, l5, l6, l7, k0, k1, k2, k3,
                       s2, s3, sq, skv, sqa, skva, t2, t3, tq, tkv, tqa, tkva, z2, z3, zq, zkv, zqa, zkva, *sems):
    comm = Comm(*sems)
    place = comm.place
    x, y, zh, zl, core = place.x, place.y, place.zh, place.zl, place.core
    side = pl.ds(2 * zh, 2)
    load = comm.local
    la = [load(d8, dv8), load(h16.at[:, side], hv), load(r2, r2v), load(g8, g8v), load(c16, cv)]
    ly = load(yt, yv)
    lg = [load(g2, g2v), load(g3, g3v)]
    lb = [load(qo, qov), load(qoa, qoav), load(qkvo, qv)]
    lc = [load(kv, kvv), load(kva, kvav), load(n1p, npv), load(n1a, nav), load(xb, xv), load(r1, r1v), load(h_own, how)]
    comm.enter(PEERS + FAR_PEERS)
    late = [wide_sum(comm, g2v, s2, t2.at[0], t2.at[1], t2.at[2], z2, 128, False),
            wide_sum(comm, g3v, s3, t3.at[0], t3.at[1], t3.at[2], z3, 128, False)]
    y_task = plane_sum(comm, yv, yf, yn)
    ly.wait()
    pump(y_task), pump(y_task)
    lg[0].wait()
    pump(late[0])
    lg[1].wait()
    pump(late[1])
    for i in range(2):
        cotv[240 * i:240 * i + 240, :] = cot_pre[i]
    cotv[480:544, :] = act_rows(cot_act, spare)
    mark("dh")
    for copy in la:
        copy.wait()
    for i in range(2):
        here = pl.ds(240 * i, 240)
        scale = r2v[here, 0:1]
        gain = lambda n: g8v[n // 2, n % 2, 1:2, :]
        grad = lambda n: dv8[n // 2, n % 2, here, :].astype(F32) * gain(n)
        unit = lambda n: hv[n // 2, n % 2, here, :].astype(F32) * scale
        m = sum(jnp.sum(grad(n) * unit(n), axis=1, keepdims=True) for n in range(8)) / 2048
        mean[here, :] = jnp.broadcast_to(m, (240, 128))
        for n in range(8):
            value = cv[n // 2, n % 2, here, :].astype(F32) + scale * (grad(n) - unit(n) * m)
            ghp[here, 256 * n:256 * n + 256] = value.astype(BF)
        here, there, lanes = pl.ds(480, 64), pl.ds(480 + 64 * i, 64), pl.ds(128 * i, 128)
        scale_a = r2v[there, 0:1]
        gain_a = lambda n: g8v[n // 2, n % 2, 2:3, 128:256]
        grad_a = lambda n: dv8[n // 2, n % 2, here, lanes].astype(F32) * gain_a(n)
        unit_a = lambda n: hv[n // 2, n % 2, here, lanes].astype(F32) * scale_a
        m = sum(jnp.sum(grad_a(n) * unit_a(n), axis=1, keepdims=True) for n in range(8)) / 1024
        mean[there, :] = jnp.broadcast_to(m, (64, 128))
        for n in range(8):
            value = cv[n // 2, n % 2, here, lanes].astype(F32) + scale_a * (grad_a(n) - unit_a(n) * m)
            gha[64 * i:64 * i + 64, 128 * n:128 * n + 128] = value.astype(BF)
    pump(late[0])
    pump(late[1])
    mark("attnback")
    for copy in lb:
        copy.wait()
    for i in range(2):
        here = pl.ds(240 * i, 240)
        dov[i, 0:240, :] = dot(ghp[here, :], qov[:, :, :, :, 256:512].reshape(2048, 256), 1, 0).astype(BF)
    low = dot(gha[...], qoav[:, :, :, :, 256:512].reshape(1024, 256), 1, 0).astype(BF)
    for i in range(2):
        dov[i, 240:304, :] = low[64 * i:64 * i + 64]
    for i in range(2):
        q, k, v, do = qv[0, i, 0:304, :], qv[1, i], qv[2, i], dov[i]
        probs = soft(q, k, lens[i])
        inner = probs * dot(do, v, 1, 1)
        dscores = (inner - probs * jnp.sum(inner, axis=1, keepdims=True)).astype(BF)
        dq = (dot(dscores, k, 1, 0) * 0.0625).astype(BF)
        dk = (dot(dscores, q, 0, 0) * 0.0625).astype(BF)[0:304]
        dv = dot(probs.astype(BF), do, 0, 0).astype(BF)[0:304]
        for j, value in enumerate((dq, dk, dv)):
            dqp[240 * i:240 * i + 240, 256 * j:256 * j + 256] = value[0:240]
            dqa[64 * i:64 * i + 64, 256 * j:256 * j + 256] = value[240:304]
        total = dq.astype(F32) * q.astype(F32) + dk.astype(F32) * k[0:304].astype(F32) + dv.astype(F32) * v[0:304].astype(F32)
        total = jnp.broadcast_to(jnp.sum(total, axis=1, keepdims=True), (304, 128))
        stat[240 * i:240 * i + 240, :] = total[0:240]
        stat[480 + 64 * i:544 + 64 * i, :] = total[240:304]
    stat[608:640, :] = jnp.zeros((32, 128), F32)
    line = stat[...].T[0:1]
    line = jnp.concatenate([line[:, 0:256], line[:, 256:512], jnp.concatenate([line[:, 512:640], jnp.zeros((1, 128), F32)], axis=1),
                            jnp.zeros((13, 256), F32)], axis=0).astype(BF)
    for n in range(8):
        blocks[n // 2, n % 2, T:TS, :] = line
    lane = lax.broadcasted_iota(jnp.int32, (512, 128), 1)
    col = lax.broadcasted_iota(jnp.int32, (512, 128), 0)
    kv_sum = block_sum(comm, kvb, (k0, k1, k2), k3, KV_PARTS)
    for n in range(8):
        total = []
        for i in range(2):
            at = lane - 64 * i
            pick = ((at >= 0) & (at < 32) & (col == 32 * n + at)) | ((at >= 32) & (at < 64) & (col == 224 + 32 * n + at))
            pick = pick.astype(F32).astype(BF)
            total.append((dot(dqp[240 * i:240 * i + 240, 256:768], pick, 1, 0), dot(dqa[64 * i:64 * i + 64, 256:768], pick, 1, 0)))
        kvb[n // 2, n % 2, 0:240, :] = (total[0][0] + total[1][0]).astype(BF)
        kvb[n // 2, n % 2, 240:304, :] = (total[0][1] + total[1][1]).astype(BF)
    pump(kv_sum)
    for copy in lc:
        copy.wait()
    mark("terms")

    def terms(step):
        k = place.off("x", step)
        for j in range(2):
            weight = jnp.concatenate([qov[k, j, :, :, 0:256].reshape(256, 256), kvv[k, j].reshape(256, 512)], axis=1)
            blocks[k, j, 0:480, :] = dot(dqp[...], weight, 1, 1).astype(BF)
            weight = jnp.concatenate([qoav[k, j, :, :, 0:256].reshape(128, 256), kvav[k, j].reshape(128, 512)], axis=1)
            small = dot(dqa[...], weight, 1, 1).astype(BF)
            for i in range(2):
                blocks[k, j, 480:544, 128 * i:128 * i + 128] = small[64 * i:64 * i + 64]

    def outer(grad, n, left, right, lo, width):
        def block_rows(k, carry):
            here = pl.ds(pl.multiple_of(4 * n * k, 4 * n), 4 * n)
            value = dot(left[:, here], right, 0, 0).astype(BF)
            grad[k, :, :, :, lo:lo + width] = value.reshape(2, 2, n, width)
            return carry
        lax.fori_loop(0, 4, block_rows, 0)

    terms(2)
    sum_task = block_sum_both(comm, blocks, (l0, l1, l2, l3, l4, l5, l6, l7), TS)
    pump(sum_task)
    terms(1), terms(3), terms(0)
    pump(sum_task)
    mark("attngrads")
    o_act = jnp.concatenate([qv[3, 0, 240:304, :], qv[3, 1, 240:304, :]], axis=0)
    o_pre = jnp.concatenate([qv[3, 0, 0:240, :], qv[3, 1, 0:240, :]], axis=0)
    outer(gq, 128, ghp, o_pre, 256, 256)
    outer(gqa, 64, gha, o_act, 256, 256)
    outer(gq, 128, npv, dqp[:, 0:256], 0, 256)
    outer(gqa, 64, nav, dqa[:, 0:256], 0, 256)
    q_tasks = [wide_sum(comm, gq, sq, tq.at[0], tq.at[1], tq.at[2], zq, 128, True),
               wide_sum(comm, gqa, sqa, tqa.at[0], tqa.at[1], tqa.at[2], zqa, 64, True)]
    kv_tasks = [wide_sum(comm, gkv, skv, tkv.at[0], tkv.at[1], tkv.at[2], zkv, 128, True),
                wide_sum(comm, gkva, skva, tkva.at[0], tkva.at[1], tkva.at[2], zkva, 64, True)]
    pump(*q_tasks)
    pump(late[0])
    pump(kv_sum)
    pump(*q_tasks)
    pump(late[1])
    pump(sum_task)
    pump(kv_sum)
    pump(sum_task)
    pump(y_task)
    drain(kv_sum)
    own = kvb[x, zl]
    share = []
    for i in range(2):
        lane = lax.broadcasted_iota(jnp.int32, (128, 128), 0)
        col = lax.broadcasted_iota(jnp.int32, (128, 128), 1)
        pick = ((col < 64) & (lane == col + 64 * i)).astype(F32).astype(BF)
        share.append(dot(own, pick, 1, 0).astype(BF))
    outer(gkv, 128, npv, jnp.concatenate([share[0][0:240], share[1][0:240]], axis=0), 0, 128)
    outer(gkva, 64, nav, jnp.concatenate([share[0][240:304], share[1][240:304]], axis=0), 0, 128)
    pump(*kv_tasks)
    mark("late")
    pump(sum_task)
    pump(late[0])
    pump(y_task)
    pump(*kv_tasks)
    pump(*q_tasks)
    drain(sum_task)
    mark("dx")
    g_pre, g_act = g8v[x, zl, 0:1, :], g8v[x, zl, 2:3, 0:128]
    f_pre, f_act = g8v[x, zl, 1:2, :], g8v[x, zl, 2:3, 128:256]
    line = blocks[x, zl, T:TS, :].astype(F32)
    line = jnp.concatenate([line[0:1], line[1:2], line[2:3, 0:128]], axis=1)
    stat[...] = jnp.broadcast_to(line, (128, 640)).T

    def own_norm(here, there, lanes, gain_f, gain_a, width):
        s2_, s1_ = r2v[there, 0:1], r1v[there, 0:1]
        back, unit = dv8[x, zl, here, lanes].astype(F32), hv[x, zl, here, lanes].astype(F32) * s2_
        dh = cotv[here, lanes] + s2_ * (back * gain_f - unit * mean[there, 0:1])
        gain_f_grad = jnp.sum(back * unit, axis=0, keepdims=True)
        back, unit = blocks[x, zl, here, lanes].astype(F32), xv[here, lanes].astype(F32) * s1_
        outx[here, lanes] = dh + s1_ * (back * gain_a - unit * (stat[there, 0:1] / width))
        return jnp.sum(back * unit, axis=0, keepdims=True), gain_f_grad

    pre = [own_norm(pl.ds(240 * i, 240), pl.ds(240 * i, 240), pl.ds(0, 256), f_pre, g_pre, 2048) for i in range(2)]
    act = [own_norm(pl.ds(480, 64), pl.ds(480 + 64 * i, 64), pl.ds(128 * i, 128), f_act, g_act, 1024) for i in range(2)]
    gains[...] = jnp.concatenate(
        [pre[0][0] + pre[1][0], pre[0][1] + pre[1][1],
         jnp.concatenate([act[0][0] + act[1][0], act[0][1] + act[1][1]], axis=1), jnp.zeros((5, 256), F32)], axis=0)
    saves = [load(outx, out_x)]
    g_task = small_total(comm, gains16, gains2, gains, gsum)
    pump(g_task)
    mark("tail")
    pump(y_task)
    pump(*kv_tasks)
    pump(*q_tasks)
    pump(late[1])
    drain(y_task)
    outy[...] = (yv[x, place.z].astype(F32) + how[...]).astype(BF)
    saves.append(load(outy, out_y))
    pump(g_task)
    pump(*kv_tasks)
    pump(*q_tasks)
    for task in q_tasks + kv_tasks + late:
        drain(task)
    drain(g_task)
    saves += [load(gsum, out_g), load(gkv.at[y, zh, core], out_kv), load(gkva.at[y, zh, core], out_kva), load(gq.at[y, zh, core], out_q), load(gqa.at[y, zh, core], out_qa)]
    saves += [load(g2v.at[y, zh, core], out_s2.at[zh]), load(z2, out_s2.at[1 - zh])]
    saves += [load(g3v.at[y, zh, core], out_s3.at[zh]), load(z3, out_s3.at[1 - zh])]
    for copy in saves:
        copy.wait()
    mark(None)
    comm.close()


def attend_back(lens, *args):
    outs = [((2, 128, 768), BF), ((2, 128, 768), BF), ((128, 512), BF), ((64, 512), BF), ((128, 128), BF), ((64, 128), BF), ((T, 256), F32),
            ((T, 256), BF), ((8, 256), F32)]
    vm = lambda *s: pltpu.VMEM(s, BF)
    vf = lambda *s: pltpu.VMEM(s, F32)
    wide = lambda n, c: (4, 2, 2, n, c)
    back = [(128, 768), (128, 768), (128, 512), (128, 128), (64, 512), (64, 128)]
    scratch = [vm(4, 2, T, 256), vm(4, 2, T, 256), vm(4, 2, T, 256), vf(608, 128), vf(608, 128), vf(4, 2, 8, 256),
               vm(4, 2, 2, 128, 512), vm(4, 2, 2, 64, 512), vm(4, 2, 2, 128, 512), vm(4, 2, 2, 64, 512),
               vm(480, 2048), vm(128, 1024), vm(4, 2, KEYS, 256), vm(T, 256), vf(T, 256), vm(*wide(128, 768)),
               vm(*wide(128, 768)), vm(4, 4, T, 256), vf(T, 256)]
    scratch += [vf(608, 128), vm(480, 2048), vm(128, 1024), vf(8, 128), vm(2, 304, 256), vm(480, 768), vm(128, 768),
                vf(640, 128), vf(8, 256), vf(8, 256), vf(8, 8, 256), vf(2, 8, 256), vf(64, 256), vf(T, 256), vm(T, 256)]
    scratch += [vm(*wide(n, c)) for n, c in back[2:]]
    scratch += [vm(4, 2, 304, 128), vm(4, 2, TS, 256)] + LAND_16 + block_lands(TS) + [vm(2, 304, 128)] * 3 + [vm(304, 128)]
    scratch += [vm(4, 2, n, c) for n, c in back] + [vm(3, 2, n, c) for n, c in back] + [vm(n, c) for n, c in back]
    return pl.pallas_call(
        attend_back_kernel,
        out_shape=[jax.ShapeDtypeStruct(s, d) for s, d in outs],
        in_specs=[pl.BlockSpec(memory_space=pltpu.SMEM)] + [ANY] * 14 + [INSIDE] * 2 + [ANY] * (len(args) - 16),
        out_specs=[ANY] * len(outs),
        scratch_shapes=scratch + SEM_SCRATCH,
        compiler_params=pltpu.CompilerParams(collective_id=3, has_side_effects=True, vmem_limit_bytes=VMEM_CAP),
        name="attend_back",
    )(lens, *args)
def result_kernel(s0, s1, s2, s3, sa, sq, sqa, skv, skva, y, gx, gains,
                  y_pre, y_act, x_pre, x_act, attn_gain_pre, query_pre, key_pre, value_pre, out_pre, ffn_gain_pre, gate_pre,
                  up_pre, down_pre, attn_gain_act, query_act, key_act, value_act, out_act, ffn_gain_act, gate_act, up_act,
                  down_act):
    for i in range(2):
        here, lanes = slice(240 * i, 240 * i + 240), slice(128 * i, 128 * i + 128)
        y_pre[i], x_pre[i] = y[here, :], gx[here, :]
        x_act[:, i, :] = gx[480:530, lanes]
    low = y[480:544, :].astype(F32)[0:50]
    y_act[...] = jnp.stack([low[:, 0:128], low[:, 128:256]], axis=1).astype(BF)
    attn_gain_pre[...], ffn_gain_pre[...] = gains[0:1, :], gains[1:2, :]
    attn_gain_act[...], ffn_gain_act[...] = gains[2:3, 0:128], gains[2:3, 128:256]
    for q, kv, query, key, value in ((sq, skv, query_pre, key_pre, value_pre),
                                     (sqa, skva, query_act, key_act, value_act)):
        query[...] = q[:, 0:256].astype(F32)
        both = kv[...].astype(F32).T
        key[...], value[...] = both[0:32], both[32:64]
    out_pre[...], out_act[...] = sq[:, 256:512].astype(F32).T, sqa[:, 256:512].astype(F32)
    for h in range(2):
        for i, s in enumerate((s0, s1, s2, s3)):
            here = slice(1024 * h + 256 * i, 1024 * h + 256 * i + 256)
            gate_pre[:, here], up_pre[:, here] = s[h, :, 0:256].astype(F32), s[h, :, 256:512].astype(F32)
            down_pre[here, :] = s[h, :, 512:768].astype(F32).T
        here = slice(256 * h, 256 * h + 256)
        gate_act[:, here], up_act[:, here] = sa[h, :, 0:256].astype(F32), sa[h, :, 256:512].astype(F32)
        down_act[:, here] = sa[h, :, 512:768].astype(F32)


def results(*args):
    tokens = lambda d: [((2, 240, 256), d), ((50, 2, 128), d)]
    expert = lambda n, h, out, down: [((1, n * 2), F32), ((n, 256), F32), ((32, n), F32), ((32, n), F32), (out, F32),
                                      ((1, n * 2), F32), ((n, h), F32), ((n, h), F32), (down, F32)]
    shapes = tokens(BF) + tokens(F32) + expert(128, 2048, (256, 128), (2048, 128)) + expert(64, 512, (64, 256), (64, 512))
    return pl.pallas_call(
        result_kernel,
        out_shape=[jax.ShapeDtypeStruct(s, d) for s, d in shapes],
        in_specs=[INSIDE] * len(args),
        out_specs=[INSIDE] * len(shapes),
        compiler_params=pltpu.CompilerParams(vmem_limit_bytes=VMEM_CAP),
        name="results",
    )(*args)


def local(x_pre, x_act, lengths, cot_pre, cot_act, attn_gain_pre, query_pre, key_pre, value_pre, out_pre, ffn_gain_pre,
          gate_pre, up_pre, down_pre, attn_gain_act, query_act, key_act, value_act, out_act, ffn_gain_act, gate_act,
          up_act, down_act):
    line = lambda gain: gain.reshape(1, -1)
    x_act, cot_act = x_act.transpose(1, 0, 2), cot_act.transpose(1, 0, 2)
    key_pre, value_pre, key_act, value_act, out_act, down_act = (
        m.T for m in (key_pre, value_pre, key_act, value_act, out_act, down_act))
    (xb, f, fa, qo, qoa, kv, kva, g8, n1p, n1a, qkvo, r1, h_own, h16, n2p, n2a, r2) = attend(
        lengths, x_pre, x_act, line(attn_gain_pre), query_pre, key_pre, value_pre, out_pre, line(ffn_gain_pre), gate_pre,
        up_pre, down_pre, line(attn_gain_act), query_act, key_act, value_act, out_act, line(ffn_gain_act), gate_act, up_act,
        down_act)
    s0, s1, sa, g2, g3, d8, yt, c8 = feed_forward(f, fa, n2p, n2a, cot_pre, cot_act)
    s2, s3, sq, sqa, skv, skva, gx, y, gains = attend_back(
        lengths, d8, h16, c8, r2, r1, g8, qo, qoa, kv, kva, n1p, n1a, qkvo, xb, cot_pre, cot_act, g2, g3, yt, h_own)
    outs = results(s0, s1, s2, s3, sa, sq, sqa, skv, skva, y, gx, gains)
    turn = lambda i, o: o.transpose(1, 0, 2) if i in (1, 3) else o.T if i in (6, 7, 15, 16, 17, 21) else o
    return tuple(o.reshape(-1) if o.shape[0] == 1 else turn(i, o) for i, o in enumerate(outs))


def solution(mesh):
    tok, row, col, vec = P("wide", None, "narrow"), P("wide", "narrow"), P("narrow", "wide"), P("narrow")
    expert = (vec, row, row, row, col, vec, row, row, col)
    return jax.shard_map(
        local, mesh=mesh, in_specs=(tok, tok, P("wide"), tok, tok) + expert + expert,
        out_specs=(tok,) * 4 + expert + expert, check_vma=False)
```

```python
import functools
import jax
import jax.numpy as jnp
from jax import lax
from jax.experimental import pallas as pl
from jax.experimental.pallas import tpu as pltpu
from jax.sharding import PartitionSpec as P

MESH = pl.DeviceIdType.MESH
BF = jnp.bfloat16
F32 = jnp.float32
SEMS = 256
LOCAL_SEMS = 48
VMEM_CAP = 62 * 1024 * 1024


class Place:
    def __init__(self):
        wide, narrow = lax.axis_index("wide"), lax.axis_index("narrow")
        self.core = lax.rem(wide, 2)
        self.zh = lax.rem(lax.div(wide, 2), 2)
        self.y = lax.div(wide, 4)
        self.zl = lax.rem(narrow, 2)
        self.x = lax.div(narrow, 2)
        self.z = self.zh * 2 + self.zl

    def wide_at(self, y, zh, core):
        return (y * 2 + zh) * 2 + core

    def coord(self, axis):
        return {"x": self.x, "y": self.y, "z": self.z}[axis]

    def off(self, axis, step):
        return lax.rem(self.coord(axis) + step + 4, 4)

    def peer(self, name):
        if name == "sib":
            return {"wide": self.wide_at(self.y, self.zh, 1 - self.core)}
        if name == "z2":
            return {"wide": self.wide_at(self.y, 1 - self.zh, self.core)}
        if name == "zl":
            return {"narrow": self.x * 2 + 1 - self.zl}
        if name[0] == "w":
            step, flip = int(name[1]), int(name[2])
            zh = 1 - self.zh if flip else self.zh
            return {"wide": self.wide_at(self.off("y", step), zh, self.core)}
        if name[0] == "n":
            zl = 1 - self.zl if int(name[2]) else self.zl
            return {"narrow": self.off("x", int(name[1])) * 2 + zl}
        axis, step = name[0], 1 if name[1] == "+" else -1
        at = self.off(axis, step)
        if axis == "y":
            return {"wide": self.wide_at(at, self.zh, self.core)}
        if axis == "x":
            return {"narrow": at * 2 + self.zl}
        return {"wide": self.wide_at(self.y, lax.div(at, 2), self.core), "narrow": self.x * 2 + lax.rem(at, 2)}


class Link:
    def __init__(self, out, into):
        self.out, self.into = out, into

    def arrive(self):
        self.into.wait_recv()

    def left(self):
        self.out.wait_send()


class Comm:
    def __init__(self, send_sems, recv_sems, local_sems):
        self.place = Place()
        self.send_sems, self.recv_sems, self.local_sems = send_sems, recv_sems, local_sems
        self.count, self.local_count = 0, 0
        self.links = []

    def enter(self, peers):
        barrier = pltpu.get_barrier_semaphore()
        for name in peers:
            pl.semaphore_signal(barrier, inc=1, device_id=self.place.peer(name), device_id_type=MESH)
        pl.semaphore_wait(barrier, len(peers))

    def send(self, src, dst, name, incoming):
        index = self.count
        self.count += 1
        assert index < SEMS
        make = lambda to: pltpu.make_async_remote_copy(
            src_ref=src, dst_ref=to, send_sem=self.send_sems.at[index], recv_sem=self.recv_sems.at[index],
            device_id=self.place.peer(name), device_id_type=MESH)
        out = make(dst)
        out.start()
        link = Link(out, make(incoming))
        self.links.append(link)
        return link

    def local(self, src, dst):
        index = self.local_count
        self.local_count += 1
        assert index < LOCAL_SEMS
        copy = pltpu.make_async_copy(src, dst, self.local_sems.at[index])
        copy.start()
        return copy

    def settle(self):
        for link in self.links:
            link.left()
        self.links = []

    def close(self):
        self.settle()

    def ring_gather(self, axis, view, parts, own=None, staged=False):
        place = self.place
        at = lambda step: place.off(axis, step)
        src = own if own is not None else (lambda part: view(at(0), part))
        up_first = sorted(parts, key=lambda part: -part[1])
        plus = [(way, p, self.send(src(p), view(at(0), p), axis + "+", view(at(-1), p))) for p, way in up_first]
        minus = [(way, p, self.send(src(p), view(at(0), p), axis + "-", view(at(1), p))) for p, way in up_first[::-1]]
        yield
        rest = []
        for way, p, link in plus:
            if way > 0:
                link.arrive()
                rest.append(self.send(view(at(-1), p), view(at(-1), p), axis + "+", view(at(-2), p)))
        for way, p, link in minus:
            if way < 0:
                link.arrive()
                rest.append(self.send(view(at(1), p), view(at(1), p), axis + "-", view(at(2), p)))
        yield
        for way, p, link in plus:
            if way < 0:
                link.arrive()
        for way, p, link in minus:
            if way > 0:
                link.arrive()
        if staged:
            yield
        for link in rest:
            link.arrive()

    def pair_ring_gather(self, pair, axis, view, parts, own, give, whole, swap_first=False):
        place = self.place
        mine = {"z2": place.zh, "zl": place.zl}[pair]
        here = place.coord(axis)
        first = self.ring_gather(axis, lambda k, p: view(k, mine, p), parts, own)
        if not swap_first:
            next(first)
            yield
        swap = self.send(give, view(here, mine, whole), pair, view(here, 1 - mine, whole))
        yield
        if swap_first:
            next(first)
            yield
        next(first)
        yield
        swap.arrive()
        second = self.ring_gather(axis, lambda k, p: view(k, 1 - mine, p), parts)
        next(second)
        yield
        next(second)
        yield
        drain(first)
        drain(second)

    def plane_gather(self, view, parts_x, parts_z, own=None, ready=None):
        place = self.place
        ax = self.ring_gather("x", lambda k, p: view(k, place.z, p), parts_x, own, True)
        bz = self.ring_gather("z", lambda k, p: view(place.x, k, p), parts_z, own, True)
        onward = lambda step: [
            self.ring_gather("z", lambda k, p: view(place.off("x", step), k, p), parts_x),
            self.ring_gather("x", lambda k, p: view(k, place.off("z", step), p), parts_z)]
        next(ax), next(bz)
        yield
        next(ax), next(bz)
        next(ax)
        if ready is not None:
            ready()
        close = [onward(step) for step in (0, 1, -1)]
        for az, _ in close:
            next(az)
        next(bz)
        for _, bx in close:
            next(bx)
        yield
        drain(ax)
        last = onward(2)
        next(last[0])
        drain(bz)
        next(last[1])
        yield
        for az, bx in close:
            next(az), next(bx)
        yield
        next(last[0]), next(last[1])
        yield
        for az, bx in close + [last]:
            drain(az), drain(bx)

    def ring_sum(self, axis, view, parts, relay, plus, minus, split=False):
        place = self.place
        at = lambda step: place.off(axis, step)
        near = {1: lambda p: self.send(view(at(1), p), plus(p), axis + "+", plus(p)),
                -1: lambda p: self.send(view(at(-1), p), minus(p), axis + "-", minus(p))}
        far = [(p, way, self.send(view(at(2), p), relay(p), axis + ("+" if way > 0 else "-"), relay(p))) for p, way in parts]
        if split:
            yield
        links = [near[-way](p) for p, way in parts]
        yield
        for p, way, link in far:
            link.arrive()
            add_to(view(at(way), p), relay(p))
            links.append(near[way](p))
        yield
        for link in links:
            link.arrive()
        for p, _ in parts:
            add_to(view(at(0), p), plus(p), minus(p))


def add_to(ref, *others):
    total = ref[...].astype(F32)
    for other in others:
        total = total + other[...].astype(F32)
    ref[...] = total.astype(ref.dtype)


def drain(task):
    for _ in task:
        pass


def rows(lo, hi):
    return pl.ds(lo, hi - lo)
T = 544
CH = 4


def halves(n):
    return [(rows(0, n // 2), 1), (rows(n // 2, n), -1)]


PARTS_8 = [(rows(0, 272), 1), (rows(272, 544), -1)]
PARTS_A = [(rows(0, 144), 1), (rows(144, 272), -1)]
PARTS_B = [(rows(272, 416), 1), (rows(416, 544), -1)]
PEERS = ("y+", "y-", "z2", "sib", "x+", "x-", "z+", "z-")


def wide_gather(comm, out, own, give, n, parts=None, swap_first=False):
    place = comm.place
    core = place.core
    copy = comm.local(own, out.at[place.y, place.zh, core])
    task = comm.pair_ring_gather(
        "z2", "y", lambda k, j, p: out.at[k, j, core, p], parts or halves(n),
        lambda p: own.at[p], give, slice(None), swap_first)
    yield from task
    copy.wait()
    link = comm.send(out.at[:, :, core], out.at[:, :, core], "sib", out.at[:, :, 1 - core])
    yield
    link.arrive()


def block_gather(comm, out, own, parts):
    place = comm.place
    copy = comm.local(own, out.at[place.x, place.zl])
    yield from comm.pair_ring_gather(
        "zl", "x", lambda k, j, p: out.at[k, j, p], parts, lambda p: own.at[p], own, slice(None))
    copy.wait()


STEPS = [(step, flip) for flip in range(2) for step in range(4) if step or flip]


def small_gather(comm, out, own):
    place = comm.place
    copy = comm.local(own, out.at[place.x, place.zl])
    links = []
    for step, flip in STEPS:
        back = out.at[place.off("x", -step), 1 - place.zl if flip else place.zl]
        links.append(comm.send(own, out.at[place.x, place.zl], f"n{step}{flip}", back))
    yield
    copy.wait()
    for link in links:
        link.arrive()


def plane_spread(comm, out, own):
    place = comm.place
    copy = comm.local(own, out.at[place.x, place.z])
    yield from comm.plane_gather(lambda k, j, p: out.at[k, j, p], PARTS_A, PARTS_B, lambda p: own.at[p], copy.wait)


def block_sum(comm, blocks, lands, swap, parts, z=None):
    place = comm.place
    relay, plus, minus = lands
    upto = pl.ds(0, sum(p.size for p, _ in parts))
    xs = comm.ring_sum(
        "x", lambda k, p: blocks.at[k, :, p], parts,
        lambda p: relay.at[:, p], lambda p: plus.at[:, p], lambda p: minus.at[:, p], z is not None)
    next(xs)
    yield
    if z is not None:
        z_rows, z_parts, z_land, z_lands = z
        next(xs)
        link = comm.send(blocks.at[:, 1 - place.zl, z_rows], z_land, "zl", z_land)
        yield
    next(xs)
    yield
    if z is not None:
        link.arrive()
        add_to(blocks.at[:, place.zl, z_rows], z_land)
        zs = comm.ring_sum("x", lambda k, p: blocks.at[k, place.zl, p], z_parts,
                           *[(lambda p, land=land: land.at[pl.ds(p.start - z_rows.start, p.size)]) for land in z_lands])
        next(zs)
        yield
    drain(xs)
    last = comm.send(blocks.at[place.x, 1 - place.zl, upto], swap, "zl", swap)
    if z is not None:
        next(zs)
    yield
    last.arrive()
    add_to(blocks.at[place.x, place.zl, upto], swap)
    if z is not None:
        drain(zs)


def plane_sum(comm, blocks, lands_far, lands_near):
    place = comm.place
    az = comm.ring_sum("z", lambda k, p: blocks.at[:, k, p], PARTS_A,
                       lambda p: lands_far.at[0, :, p], lambda p: lands_far.at[1, :, p], lambda p: lands_far.at[2, :, p], True)
    bx = comm.ring_sum("x", lambda k, p: blocks.at[k, :, p], PARTS_B,
                       lambda p: lands_far.at[0, :, p], lambda p: lands_far.at[1, :, p], lambda p: lands_far.at[2, :, p], True)
    for _ in range(3):
        next(az), next(bx)
        yield
    drain(az)
    ax = comm.ring_sum("x", lambda k, p: blocks.at[k, place.z, p], PARTS_A,
                       lambda p: lands_near.at[0, p], lambda p: lands_near.at[1, p], lambda p: lands_near.at[2, p])
    next(ax)
    drain(bx)
    bz = comm.ring_sum("z", lambda k, p: blocks.at[place.x, k, p], PARTS_B,
                       lambda p: lands_near.at[0, p], lambda p: lands_near.at[1, p], lambda p: lands_near.at[2, p])
    next(bz)
    yield
    next(ax), next(bz)
    yield
    drain(ax), drain(bz)


CHIPS = [(step, flip) for flip in range(2) for step in range(4) if step or flip]


def small_total(comm, slots, pair, own, out):
    place = comm.place
    mine = place.y * 2 + place.zh
    links = []
    for step, flip in CHIPS:
        back = place.off("y", -step) * 2 + (1 - place.zh if flip else place.zh)
        links.append(comm.send(own, slots.at[mine], f"w{step}{flip}", slots.at[back]))
    slots[mine] = own[...]
    yield
    for link in links:
        link.arrive()
    pair[0] = sum(slots[i] for i in range(8))
    link = comm.send(pair.at[0], pair.at[1], "sib", pair.at[1])
    yield
    link.arrive()
    out[...] = pair[0] + pair[1]


def wide_sum(comm, grad, half, relay, plus, minus, swap, n, add):
    place = comm.place
    core, zh = place.core, place.zh
    link = comm.send(grad.at[:, :, 1 - core], half, "sib", half)
    yield
    link.arrive()
    def fold(k, carry):
        add_to(grad.at[k, :, core], half.at[k])
        return carry
    lax.fori_loop(0, 4, fold, 0)
    yield from comm.ring_sum(
        "y", lambda k, p: grad.at[k, :, core, p], halves(n),
        lambda p: relay.at[:, p], lambda p: plus.at[:, p], lambda p: minus.at[:, p])
    link = comm.send(grad.at[place.y, 1 - zh, core], swap, "z2", swap)
    yield
    link.arrive()
    if add:
        add_to(grad.at[place.y, zh, core], swap)


SEM_SCRATCH = [pltpu.SemaphoreType.DMA((SEMS,)), pltpu.SemaphoreType.DMA((SEMS,)), pltpu.SemaphoreType.DMA((LOCAL_SEMS,))]
ANY = pl.BlockSpec(memory_space=pl.ANY)
INSIDE = pl.BlockSpec(memory_space=pltpu.VMEM)


X_ROWS = 400
X_PARTS = [(rows(0, 208), 1), (rows(208, 400), -1)]


def block_lands(count):
    z = count - X_ROWS
    return ([pltpu.VMEM((2, X_ROWS, 256), BF)] * 3 + [pltpu.VMEM((X_ROWS, 256), BF), pltpu.VMEM((4, z, 256), BF)]
            + [pltpu.VMEM((z, 256), BF)] * 3)


def block_sum_both(comm, blocks, lands, count):
    z = (rows(X_ROWS, count), [(rows(X_ROWS, 480), 1), (rows(480, count), -1)], lands[4], lands[5:8])
    return block_sum(comm, blocks, lands[0:3], lands[3], X_PARTS, z)


LAND_16 = [pltpu.VMEM((3, 4, T, 256), BF), pltpu.VMEM((3, T, 256), BF)]


EPSILON = 1e-06
MASKED = -1000000000.0
KEYS = 384


def dot(a, b, ca, cb):
    return lax.dot_general(a, b, (((ca,), (cb,)), ((), ())), preferred_element_type=F32)


_open = []


def mark(name):
    if _open:
        _open.pop().__exit__(None, None, None)
    if name:
        scope = jax.named_scope(name)
        scope.__enter__()
        _open.append(scope)


def pump(*tasks):
    for task in tasks:
        next(task, None)


def seen(length):
    s = lax.broadcasted_iota(jnp.int32, (304, KEYS), 0)
    t = lax.broadcasted_iota(jnp.int32, (304, KEYS), 1)
    live = (t < 192) | ((t >= 240) & (t < 290)) | ((t < 240) & (t - 192 < length))
    return live & ((t < 240) | (s >= 240))


def soft(q, k, length):
    scores = dot(q, k, 1, 1) * 0.0625
    scores = jnp.where(seen(length), scores, MASKED)
    weights = jnp.exp(scores - jnp.max(scores, axis=1, keepdims=True))
    return weights / jnp.sum(weights, axis=1, keepdims=True)


def pairs8():
    return [(x, zl) for x in range(4) for zl in range(2)]


def norm_block_rows(get, gain, width, put):
    total = sum(jnp.sum(get(n) * get(n), axis=1, keepdims=True) for n in range(8))
    scale = lax.rsqrt(total / (8 * width) + EPSILON)
    for n in range(8):
        put(n, (get(n) * scale * gain(n)).astype(BF))
    return scale


def act_rows(act, spare):
    spare[...] = jnp.zeros((64, 256), F32)
    rows_of = act[...].astype(F32)
    for i in range(2):
        spare[0:50, 128 * i:128 * i + 128] = rows_of[:, i, :]
    return spare[...]


def turned(m):
    return m.astype(F32).T.astype(BF)


def attend_kernel(lens, x_pre, x_act, attn_gain_pre, query_pre, key_pre, value_pre, out_pre, ffn_gain_pre, gate_pre, up_pre,
                  down_pre, attn_gain_act, query_act, key_act, value_act, out_act, ffn_gain_act, gate_act, up_act, down_act,
                  out_xb, out_f, out_fa, out_q, out_qa, out_kv, out_kva, out_g, out_n1p, out_n1a, out_qkvo, out_r1,
                  out_h, out_h16, out_n2p, out_n2a, out_r2,
                  kv8, kvf, qo, qoa, kv, kva, x8, g8, n1p, n1a, qkvo, r1, xv, hv, full, n2p, n2a, r2,
                  blocks, l0, l1, l2, l3, l4, l5, l6, l7, wf, wfa, wq, wqa, kvs, gb, spare, *sems):
    comm = Comm(*sems)
    place = comm.place
    zh = place.zh
    for i in range(2):
        xv[240 * i:240 * i + 240, :] = x_pre[i]
    xv[480:544, :] = act_rows(x_act, spare).astype(BF)
    lane = lax.broadcasted_iota(jnp.int32, (32, 128), 1)
    row = lax.broadcasted_iota(jnp.int32, (32, 128), 0)
    spread = [(lane == row + 32 * j).astype(F32).astype(BF) for j in range(4)]
    for base, half, key, value in ((0, 64, key_pre, value_pre), (64, 32, key_act, value_act)):
        kvs[base:base + half, :] = (
            dot(key[:, 0:half], spread[0], 0, 0) + dot(value[:, 0:half], spread[1], 0, 0)
            + dot(key[:, half:2 * half], spread[2], 0, 0) + dot(value[:, half:2 * half], spread[3], 0, 0)).astype(BF)
    gb[...] = jnp.concatenate([attn_gain_pre[...], ffn_gain_pre[...],
                               jnp.concatenate([attn_gain_act[...], ffn_gain_act[...]], axis=1), jnp.zeros((5, 256), F32)], axis=0)
    wq[:, 0:256], wqa[:, 0:256] = query_pre[...], query_act[...]
    wq[:, 256:512], wqa[:, 256:512] = turned(out_pre[...]), out_act[...]
    zero = jnp.zeros((KEYS - 304, 256), BF)
    for i in range(2):
        for j in (1, 2):
            qkvo[j, i, 304:KEYS, :] = zero
    comm.enter(PEERS + ("n20", "n11", "n21", "n31"))

    mark('start')
    kv_task = small_gather(comm, kv8, kvs)
    g_task = small_gather(comm, g8, gb)
    x_task = block_gather(comm, x8, xv, PARTS_8)
    q_tasks = [wide_gather(comm, qo, wq, wq, 128), wide_gather(comm, qoa, wqa, wqa, 64)]
    f_tasks = [wide_gather(comm, out_f.at[i], wf.at[zh, i], wf.at[1 - zh, i], 128, None, True) for i in range(CH)]
    f_tasks.append(wide_gather(comm, out_fa, wfa.at[zh], wfa.at[1 - zh], 64, None, True))
    pump(kv_task)
    pump(g_task)
    pump(x_task), pump(x_task)
    pump(*q_tasks), pump(*q_tasks)
    for h in range(2):
        for i in range(CH):
            here = slice(1024 * h + 256 * i, 1024 * h + 256 * i + 256)
            wf[h, i, :, 0:256], wf[h, i, :, 256:512] = gate_pre[:, here], up_pre[:, here]
            wf[h, i, :, 512:768] = turned(down_pre[here, :])
        here = slice(256 * h, 256 * h + 256)
        wfa[h, :, 0:256], wfa[h, :, 256:512] = gate_act[:, here], up_act[:, here]
        wfa[h, :, 512:768] = down_act[:, here]
    drain(kv_task)
    lane = lax.broadcasted_iota(jnp.int32, (128, 512), 0)
    col = lax.broadcasted_iota(jnp.int32, (128, 512), 1)
    for side in range(2):
        total = jnp.zeros((96, 512), F32)
        at = lane - 64 * side
        for n in range(8):
            pick = ((at >= 0) & (at < 32) & (col == 32 * n + at)) | ((at >= 32) & (at < 64) & (col == 224 + 32 * n + at))
            total = total + dot(kv8[n // 2, n % 2], pick.astype(F32).astype(BF), 1, 0)
        kvf[64 * side:64 * side + 64, :] = total[0:64].astype(BF)
        kvf[128 + 32 * side:160 + 32 * side, :] = total[64:96].astype(BF)
    kv_a, kv_b = kvf.at[0:128], kvf.at[128:192]
    kv_tasks = [wide_gather(comm, kv, kv_a, kv_a, 128), wide_gather(comm, kva, kv_b, kv_b, 64)]
    pump(*kv_tasks), pump(*kv_tasks)
    pump(x_task)
    pump(x_task)
    pump(*q_tasks)
    pump(*kv_tasks)
    pump(*f_tasks)
    pump(*q_tasks)
    pump(*kv_tasks)
    pump(x_task)
    pump(*q_tasks)
    pump(*kv_tasks)
    pump(*f_tasks)
    drain(g_task)
    drain(x_task)

    mark('norm1')
    for i in range(2):
        here = pl.ds(240 * i, 240)
        get = lambda n: x8[n // 2, n % 2, here, :].astype(F32)
        def put(n, v):
            n1p[here, 256 * n:256 * n + 256] = v
        r1[here, :] = jnp.broadcast_to(norm_block_rows(get, lambda n: g8[n // 2, n % 2, 0:1, :], 256, put), (240, 128))
        low = pl.ds(480, 64)
        get = lambda n: x8[n // 2, n % 2, low, 128 * i:128 * i + 128].astype(F32)
        def put(n, v):
            n1a[64 * i:64 * i + 64, 128 * n:128 * n + 128] = v
        r1[480 + 64 * i:544 + 64 * i, :] = jnp.broadcast_to(
            norm_block_rows(get, lambda n: g8[n // 2, n % 2, 2:3, 0:128], 128, put), (64, 128))
    pump(*q_tasks)
    pump(*kv_tasks)
    for task in q_tasks:
        drain(task)
    mark('qkv')
    def queries(i, carry):
        here = pl.ds(pl.multiple_of(240 * i, 16), 240)
        qkvo[0, i, 0:240, :] = dot(n1p[here, :], qo[:, :, :, :, 0:256].reshape(2048, 256), 1, 0).astype(BF)
        return carry
    lax.fori_loop(0, 2, queries, 0)
    for task in kv_tasks:
        drain(task)
    def keys(i, carry):
        here = pl.ds(pl.multiple_of(240 * i, 16), 240)
        for j in range(2):
            qkvo[1 + j, i, 0:240, :] = dot(
                n1p[here, :], kv[:, :, :, :, 256 * j:256 * j + 256].reshape(2048, 256), 1, 0).astype(BF)
        return carry
    lax.fori_loop(0, 2, keys, 0)
    low = [dot(n1a[...], qoa[:, :, :, :, 0:256].reshape(1024, 256), 1, 0).astype(BF)]
    for j in range(2):
        low.append(dot(n1a[...], kva[:, :, :, :, 256 * j:256 * j + 256].reshape(1024, 256), 1, 0).astype(BF))
    for i in range(2):
        for j in range(3):
            qkvo[j, i, 240:304, :] = low[j][64 * i:64 * i + 64]
    saves = [comm.local(qo, out_q), comm.local(qoa, out_qa), comm.local(kv, out_kv), comm.local(kva, out_kva),
             comm.local(n1p, out_n1p), comm.local(n1a, out_n1a), comm.local(r1, out_r1), comm.local(g8, out_g)]
    mark('attn')
    for i in range(2):
        probs = soft(qkvo[0, i, 0:304, :], qkvo[1, i], lens[i])
        qkvo[3, i, 0:304, :] = dot(probs.astype(BF), qkvo[2, i], 1, 0).astype(BF)
    saves.append(comm.local(qkvo, out_qkvo))
    mark('outproj')
    oa = jnp.concatenate([qkvo[3, 0, 240:304, :], qkvo[3, 1, 240:304, :]], axis=0)

    def terms(step):
        k = place.off("x", step)
        for j in range(2):
            weight = qo[k, j, :, :, 256:512].reshape(256, 256)
            for i in range(2):
                blocks[k, j, 240 * i:240 * i + 240, :] = dot(qkvo[3, i, 0:240, :], weight, 1, 1).astype(BF)
            small = dot(oa, qoa[k, j, :, :, 256:512].reshape(128, 256), 1, 1).astype(BF)
            for i in range(2):
                blocks[k, j, 480:544, 128 * i:128 * i + 128] = small[64 * i:64 * i + 64]

    mark('rs8')
    sum_task = block_sum_both(comm, blocks, (l0, l1, l2, l3, l4, l5, l6, l7), T)
    terms(2)
    pump(sum_task)
    terms(1), terms(3), terms(0)
    pump(sum_task)
    pump(f_tasks[0], f_tasks[1])
    pump(f_tasks[0], f_tasks[1])
    pump(sum_task)
    pump(f_tasks[2])
    pump(f_tasks[2])
    pump(sum_task)
    pump(f_tasks[3], f_tasks[4])
    pump(f_tasks[3], f_tasks[4])
    pump(sum_task)
    drain(sum_task)
    mark('hmake')
    hv[...] = xv[...].astype(F32) + blocks[place.x, place.zl].astype(F32)
    full[place.x, place.z] = hv[...].astype(BF)
    saves += [comm.local(hv, out_h), comm.local(xv, out_xb)]
    mark('hplane')
    h_task = comm.plane_gather(lambda k, j, p: full.at[k, j, p], PARTS_A, PARTS_B)
    pump(h_task)
    pump(h_task)
    pump(f_tasks[0])
    pump(h_task)
    pump(f_tasks[1])
    pump(h_task)
    pump(f_tasks[2])
    pump(h_task)
    pump(f_tasks[3], f_tasks[4])
    pump(f_tasks[0], f_tasks[1])
    drain(h_task)
    saves.append(comm.local(full, out_h16))
    mark('norm2')
    for zhi in range(2):
        def rows_norm(i, carry):
            here = pl.ds(pl.multiple_of(240 * i, 16), 240)
            there = pl.ds(pl.multiple_of(480 * zhi + 240 * i, 16), 240)
            get = lambda n: full[n // 2, 2 * zhi + n % 2, here, :].astype(F32)
            def put(n, v):
                n2p[there, 256 * n:256 * n + 256] = v
            scale = norm_block_rows(get, lambda n: g8[n // 2, n % 2, 1:2, :], 256, put)
            r2[zhi, here, :] = jnp.broadcast_to(scale, (240, 128))
            return carry
        lax.fori_loop(0, 2, rows_norm, 0)
        for i in range(2):
            get = lambda n: full[n // 2, 2 * zhi + n % 2, 480:544, 128 * i:128 * i + 128].astype(F32)
            base = 128 * zhi + 64 * i
            def put(n, v):
                n2a[base:base + 64, 128 * n:128 * n + 128] = v
            scale = norm_block_rows(get, lambda n: g8[n // 2, n % 2, 2:3, 128:256], 128, put)
            r2[zhi, 480 + 64 * i:544 + 64 * i, :] = jnp.broadcast_to(scale, (64, 128))
    mark('tail')
    saves += [comm.local(n2p, out_n2p), comm.local(n2a, out_n2a), comm.local(r2.at[zh], out_r2)]
    pump(*f_tasks[2:])
    for task in f_tasks:
        drain(task)
    for copy in saves:
        copy.wait()
    mark(None)
    comm.close()


def attend(lens, *args):
    wide5 = lambda n, c: (4, 2, 2, n, c)
    outs = [((T, 256), BF), ((CH,) + wide5(128, 768), BF), (wide5(64, 768), BF), (wide5(128, 512), BF), (wide5(64, 512), BF),
            (wide5(128, 512), BF), (wide5(64, 512), BF), ((4, 2, 8, 256), F32),
            ((480, 2048), BF), ((128, 1024), BF), ((4, 2, KEYS, 256), BF), ((608, 128), F32), ((T, 256), F32),
            ((4, 4, T, 256), BF), ((960, 2048), BF), ((256, 1024), BF), ((608, 128), F32)]
    vm = pltpu.VMEM
    scratch = [vm((4, 2, 96, 128), BF), vm((192, 512), BF)] + [vm(s, d) for s, d in outs[3:7]] + [
        vm((4, 2, T, 256), BF), vm((4, 2, 8, 256), F32), vm((480, 2048), BF), vm((128, 1024), BF),
        vm((4, 2, KEYS, 256), BF), vm((608, 128), F32), vm((T, 256), BF), vm((T, 256), F32), vm((4, 4, T, 256), BF),
        vm((960, 2048), BF), vm((256, 1024), BF), vm((2, 608, 128), F32), vm((4, 2, T, 256), BF)] + block_lands(T)
    scratch += [vm((2, CH, 128, 768), BF), vm((2, 64, 768), BF), vm((128, 512), BF), vm((64, 512), BF), vm((96, 128), BF),
                vm((8, 256), F32), vm((64, 256), F32)]
    return pl.pallas_call(
        attend_kernel,
        out_shape=[jax.ShapeDtypeStruct(s, d) for s, d in outs],
        in_specs=[pl.BlockSpec(memory_space=pltpu.SMEM)] + [INSIDE] * len(args),
        out_specs=[ANY] * len(outs),
        scratch_shapes=scratch + SEM_SCRATCH,
        compiler_params=pltpu.CompilerParams(collective_id=0, has_side_effects=True, vmem_limit_bytes=VMEM_CAP),
        name="attend",
    )(lens, *args)
EARLY = 2
TILE = 240


def gelu_parts(z):
    a, b = 0.7978845608028654, 0.044715
    t = jnp.tanh(a * (z + b * z * z * z))
    half = 0.5 * (1.0 + t)
    return z * half, half + 0.5 * z * (1.0 - t * t) * a * (1.0 + 3.0 * b * z * z)


def side_rows(full, z_low, base, count):
    return jnp.concatenate([full[x, z_low + zl, pl.ds(base, count), :] for x, zl in pairs8()], axis=1)


def feed_forward_kernel(f, fa, n2p, n2a, cot_pre, cot_act, *refs):
    out_s, out_late, refs = refs[:EARLY + 1], refs[EARLY + 1:CH + 1], refs[CH + 1:]
    out_d8, out_y, out_c, wv, wav, np_, na, gc, ga, dd, aa, dda, aaa, bb, bf, bn, d8, grad_act, cb, spare = refs[:20]
    lands = [refs[20 + 3 * i:23 + 3 * i] for i in range(EARLY + 1)]
    comm = Comm(*refs[-3:])
    place = comm.place
    loads = [comm.local(n2p, np_), comm.local(f.at[0], wv.at[0]), comm.local(n2a, na),
             comm.local(f.at[1], wv.at[1]), comm.local(f.at[2], wv.at[2]), comm.local(f.at[3], wv.at[3]),
             comm.local(fa, wav)]
    for i in range(2):
        cb[240 * i:240 * i + 240, :] = cot_pre[i].astype(BF)
    cb[480:544, :] = act_rows(cot_act, spare).astype(BF)
    c_task = plane_spread(comm, gc, cb)
    comm.enter(PEERS)
    pump(c_task)
    mark("units")
    loads[0].wait()

    def gate_up(left, weight):
        both = dot(left, weight, 1, 0)
        up = both[:, 256:512]
        value, slope = gelu_parts(both[:, 0:256])
        return (value * up).astype(BF), (up * slope).astype(BF), value.astype(BF)

    for i in range(CH):
        loads[(1, 3, 4, 5)[i]].wait()
        def unit(t, carry):
            here = pl.ds(pl.multiple_of(TILE * t, 16), TILE)
            a, b, c = gate_up(np_[here, :], wv[i, :, :, :, :, 0:512].reshape(2048, 512))
            aa[here, 256 * i:256 * i + 256] = a
            dd[here, 512 * i:512 * i + 256] = b
            dd[here, 512 * i + 256:512 * i + 512] = c
            return carry
        lax.fori_loop(0, 4, unit, 0)
        if i in (0, 1):
            pump(c_task)
    loads[2].wait(), loads[6].wait()
    aaa[...], dda[:, 0:256], dda[:, 256:512] = gate_up(na[...], wav[:, :, :, :, 0:512].reshape(1024, 512))

    def product(ref, x, z, left, left_a, lo, hi):
        zh_, zl_ = lax.div(z, 2), lax.rem(z, 2)
        here = pl.ds(pl.multiple_of(480 * zh_, 16), 480)
        rows_w = jnp.concatenate([wv[i, x, zl_, :, :, lo:hi].reshape(256, hi - lo) for i in range(CH)], axis=1)
        ref[0:480, :] = dot(left[here, :], rows_w, 1, 1).astype(BF)
        there = pl.ds(pl.multiple_of(128 * zh_, 16), 128)
        small = dot(left_a[there, :], wav[x, zl_, :, :, lo:hi].reshape(128, hi - lo), 1, 1).astype(BF)
        ref[480:544, 0:128] = small[0:64]
        ref[480:544, 128:256] = small[64:128]

    def down_terms(t, carry):
        x, z = lax.div(t, 4), lax.rem(t, 4)
        product(bb.at[x, z], x, z, aa, aaa, 512, 768)
        return carry

    mark("ydown")
    pump(c_task)
    lax.fori_loop(0, 8, down_terms, 0)
    pump(c_task)
    lax.fori_loop(8, 16, down_terms, 0)
    saves = [comm.local(bb, out_y)]
    mark("cwait")
    drain(c_task)
    saves.append(comm.local(gc.at[:, pl.ds(2 * place.zh, 2)], out_c))
    mark("dact")
    for i in range(CH):
        def dact_unit(t, carry):
            here = pl.ds(pl.multiple_of(TILE * t, 16), TILE)
            rows_c = side_rows(gc, 2 * lax.div(t, 2), pl.multiple_of(TILE * lax.rem(t, 2), 16), TILE)
            dact = dot(rows_c, wv[i, :, :, :, :, 512:768].reshape(2048, 256), 1, 0)
            for j in range(2):
                there = slice(512 * i + 256 * j, 512 * i + 256 * j + 256)
                dd[here, there] = (dact * dd[here, there].astype(F32)).astype(BF)
            return carry
        lax.fori_loop(0, 4, dact_unit, 0)
    for zhi in range(2):
        for i in range(2):
            base = 128 * zhi + 64 * i
            for n in range(8):
                ga[base:base + 64, 128 * n:128 * n + 128] = gc[n // 2, 2 * zhi + n % 2, 480:544, 128 * i:128 * i + 128]
    dact = dot(ga[...], wav[:, :, :, :, 512:768].reshape(1024, 256), 1, 0)
    for j in range(2):
        there = slice(256 * j, 256 * j + 256)
        dda[:, there] = (dact * dda[:, there].astype(F32)).astype(BF)
    saves[0].wait()

    mark("back")
    far_x, far_z = place.off("x", 2), place.off("z", 2)

    def far_terms(t, carry):
        x = jnp.where(t < 4, t, far_x)
        z = jnp.where(t < 4, far_z, lax.rem(far_z + jnp.where(t < 4, 0, t - 3), 4))
        product(bb.at[x, z], x, z, dd, dda, 0, 512)
        return carry

    def near_terms(t, carry):
        x, z = lax.rem(far_x + 1 + lax.div(t, 3), 4), lax.rem(far_z + 1 + lax.rem(t, 3), 4)
        product(bb.at[x, z], x, z, dd, dda, 0, 512)
        return carry

    lax.fori_loop(0, 7, far_terms, 0)
    b_task = plane_sum(comm, bb, bf, bn)
    pump(b_task)
    lax.fori_loop(0, 9, near_terms, 0)
    pump(b_task)
    pump(b_task)

    mark("grads")

    def weight_grads(i):
        def block_rows(y, carry):
            here = pl.ds(pl.multiple_of(512 * y, 512), 512)
            left_n = np_[:, here]
            left_c = jnp.concatenate(
                [jnp.concatenate([gc[y, zl, 0:480, :], gc[y, 2 + zl, 0:480, :]], axis=0) for zl in range(2)], axis=1)
            for j in range(3):
                if j < 2:
                    value = dot(left_n, dd[:, 512 * i + 256 * j:512 * i + 256 * j + 256], 0, 0).astype(BF)
                else:
                    value = dot(left_c, aa[:, 256 * i:256 * i + 256], 0, 0).astype(BF)
                wv[i, y, :, :, :, 256 * j:256 * j + 256] = value.reshape(2, 2, 128, 256)
            return carry
        lax.fori_loop(0, 4, block_rows, 0)

    def act_grads():
        for y in range(4):
            left_n, left_c = na[:, 256 * y:256 * y + 256], ga[:, 256 * y:256 * y + 256]
            for j in range(3):
                value = dot(left_n, dda[:, 256 * j:256 * j + 256], 0, 0) if j < 2 else dot(left_c, aaa[...], 0, 0)
                grad_act[y, :, :, :, 256 * j:256 * j + 256] = value.astype(BF).reshape(2, 2, 64, 256)

    grads = [wv.at[i] for i in range(EARLY)] + [grad_act]
    sums = [wide_sum(comm, grad, s, r.at[0], r.at[1], r.at[2], z, 64 if i == EARLY else 128, False)
            for i, (grad, (s, r, z)) in enumerate(zip(grads, lands))]
    weight_grads(0)
    pump(sums[0])
    weight_grads(1)
    pump(sums[0], sums[1])
    pump(b_task)
    act_grads()
    pump(sums[2])
    pump(b_task)
    pump(sums[1])
    drain(b_task)
    mark("dn2")
    d8[place.x, place.zl] = bb[place.x, place.z]
    d_task = comm.pair_ring_gather("zl", "x", lambda k, j, p: d8.at[k, j, p], PARTS_8,
                                   lambda p: d8.at[place.x, place.zl, p], d8.at[place.x, place.zl], slice(None))
    pump(d_task), pump(d_task)
    pump(sums[0], sums[2])
    weight_grads(2)
    saves.append(comm.local(wv.at[2], out_late[0]))
    pump(d_task)
    pump(sums[1])
    weight_grads(3)
    saves.append(comm.local(wv.at[3], out_late[1]))
    pump(d_task)
    pump(sums[2], sums[0])
    pump(d_task)
    pump(sums[1], sums[2])
    drain(d_task)
    saves.append(comm.local(d8, out_d8))
    mark("sums")
    for task in sums:
        drain(task)
    for grad, (_, _, swap), out in zip(grads, lands, out_s):
        saves.append(comm.local(grad.at[place.y, place.zh, place.core], out.at[place.zh]))
        saves.append(comm.local(swap, out.at[1 - place.zh]))
    for copy in saves[1:]:
        copy.wait()
    mark(None)
    comm.close()


def feed_forward(f, fa, n2p, n2a, cot_pre, cot_act):
    grad = (4, 2, 2, 128, 768)
    outs = [(2, 128, 768)] * EARLY + [(2, 64, 768)] + [grad] * (CH - EARLY) + [(4, 2, T, 256), (4, 4, T, 256), (4, 2, T, 256)]
    vm = lambda *s: pltpu.VMEM(s, BF)
    scratch = [vm(CH, *grad), vm(4, 2, 2, 64, 768), vm(960, 2048), vm(256, 1024), vm(4, 4, T, 256),
               vm(256, 1024), vm(960, 2048), vm(960, 1024), vm(256, 512), vm(256, 256)]
    scratch += [vm(4, 4, T, 256)] + LAND_16 + [vm(4, 2, T, 256), vm(4, 2, 2, 64, 768), vm(T, 256), pltpu.VMEM((64, 256), F32)]
    for n in [128] * EARLY + [64]:
        scratch += [vm(4, 2, n, 768), vm(3, 2, n, 768), vm(n, 768)]
    return pl.pallas_call(
        feed_forward_kernel,
        out_shape=[jax.ShapeDtypeStruct(s, BF) for s in outs],
        in_specs=[ANY] * 4 + [INSIDE] * 2,
        out_specs=[ANY] * len(outs),
        scratch_shapes=scratch + SEM_SCRATCH,
        compiler_params=pltpu.CompilerParams(collective_id=2, has_side_effects=True, vmem_limit_bytes=VMEM_CAP),
        name="feed_forward",
    )(f, fa, n2p, n2a, cot_pre, cot_act)
TS = T + 16
FAR_PEERS = tuple(f"w{step}{flip}" for step, flip in CHIPS if (step, flip) not in ((1, 0), (3, 0), (0, 1)))
KV_PARTS = [(rows(0, 160), 1), (rows(160, 304), -1)]


def attend_back_kernel(lens, d8, h16, c16, r2, r1, g8, qo, qoa, kv, kva, n1p, n1a, qkvo, xb, cot_pre, cot_act, g2, g3, yt, h_own,
                       out_s2, out_s3, out_q, out_qa, out_kv, out_kva, out_x, out_y, out_g,
                       dv8, hv, cv, r2v, r1v, g8v, qov, qoav, kvv, kvav, npv, nav, qv, xv, cotv, g2v, g3v, yv, how,
                       mean, ghp, gha, dhb, dov, dqp, dqa, stat, gains, gsum, gains16, gains2, spare, outx, outy,
                       gq, gkv, gqa, gkva, kvb, blocks, yf, yn, l0, l1, l2, l3, l4, l5, l6, l7, k0, k1, k2, k3,
                       s2, s3, sq, skv, sqa, skva, t2, t3, tq, tkv, tqa, tkva, z2, z3, zq, zkv, zqa, zkva, *sems):
    comm = Comm(*sems)
    place = comm.place
    x, y, zh, zl, core = place.x, place.y, place.zh, place.zl, place.core
    side = pl.ds(2 * zh, 2)
    load = comm.local
    la = [load(d8, dv8), load(h16.at[:, side], hv), load(r2, r2v), load(g8, g8v), load(c16, cv)]
    ly = load(yt, yv)
    lg = [load(g2, g2v), load(g3, g3v)]
    lb = [load(qo, qov), load(qoa, qoav), load(qkvo, qv)]
    lc = [load(kv, kvv), load(kva, kvav), load(n1p, npv), load(n1a, nav), load(xb, xv), load(r1, r1v), load(h_own, how)]
    comm.enter(PEERS + FAR_PEERS)
    late = [wide_sum(comm, g2v, s2, t2.at[0], t2.at[1], t2.at[2], z2, 128, False),
            wide_sum(comm, g3v, s3, t3.at[0], t3.at[1], t3.at[2], z3, 128, False)]
    y_task = plane_sum(comm, yv, yf, yn)
    ly.wait()
    pump(y_task), pump(y_task)
    lg[0].wait()
    pump(late[0])
    lg[1].wait()
    pump(late[1])
    for i in range(2):
        cotv[240 * i:240 * i + 240, :] = cot_pre[i]
    cotv[480:544, :] = act_rows(cot_act, spare)
    mark("dh")
    for copy in la:
        copy.wait()
    for i in range(2):
        here = pl.ds(240 * i, 240)
        scale = r2v[here, 0:1]
        gain = lambda n: g8v[n // 2, n % 2, 1:2, :]
        grad = lambda n: dv8[n // 2, n % 2, here, :].astype(F32) * gain(n)
        unit = lambda n: hv[n // 2, n % 2, here, :].astype(F32) * scale
        m = sum(jnp.sum(grad(n) * unit(n), axis=1, keepdims=True) for n in range(8)) / 2048
        mean[here, :] = jnp.broadcast_to(m, (240, 128))
        for n in range(8):
            value = cv[n // 2, n % 2, here, :].astype(F32) + scale * (grad(n) - unit(n) * m)
            ghp[here, 256 * n:256 * n + 256] = value.astype(BF)
        here, there, lanes = pl.ds(480, 64), pl.ds(480 + 64 * i, 64), pl.ds(128 * i, 128)
        scale_a = r2v[there, 0:1]
        gain_a = lambda n: g8v[n // 2, n % 2, 2:3, 128:256]
        grad_a = lambda n: dv8[n // 2, n % 2, here, lanes].astype(F32) * gain_a(n)
        unit_a = lambda n: hv[n // 2, n % 2, here, lanes].astype(F32) * scale_a
        m = sum(jnp.sum(grad_a(n) * unit_a(n), axis=1, keepdims=True) for n in range(8)) / 1024
        mean[there, :] = jnp.broadcast_to(m, (64, 128))
        for n in range(8):
            value = cv[n // 2, n % 2, here, lanes].astype(F32) + scale_a * (grad_a(n) - unit_a(n) * m)
            gha[64 * i:64 * i + 64, 128 * n:128 * n + 128] = value.astype(BF)
    pump(late[0])
    pump(late[1])
    mark("attnback")
    for copy in lb:
        copy.wait()
    for i in range(2):
        here = pl.ds(240 * i, 240)
        dov[i, 0:240, :] = dot(ghp[here, :], qov[:, :, :, :, 256:512].reshape(2048, 256), 1, 0).astype(BF)
    low = dot(gha[...], qoav[:, :, :, :, 256:512].reshape(1024, 256), 1, 0).astype(BF)
    for i in range(2):
        dov[i, 240:304, :] = low[64 * i:64 * i + 64]
    for i in range(2):
        q, k, v, do = qv[0, i, 0:304, :], qv[1, i], qv[2, i], dov[i]
        probs = soft(q, k, lens[i])
        inner = probs * dot(do, v, 1, 1)
        dscores = (inner - probs * jnp.sum(inner, axis=1, keepdims=True)).astype(BF)
        dq = (dot(dscores, k, 1, 0) * 0.0625).astype(BF)
        dk = (dot(dscores, q, 0, 0) * 0.0625).astype(BF)[0:304]
        dv = dot(probs.astype(BF), do, 0, 0).astype(BF)[0:304]
        for j, value in enumerate((dq, dk, dv)):
            dqp[240 * i:240 * i + 240, 256 * j:256 * j + 256] = value[0:240]
            dqa[64 * i:64 * i + 64, 256 * j:256 * j + 256] = value[240:304]
        total = dq.astype(F32) * q.astype(F32) + dk.astype(F32) * k[0:304].astype(F32) + dv.astype(F32) * v[0:304].astype(F32)
        total = jnp.broadcast_to(jnp.sum(total, axis=1, keepdims=True), (304, 128))
        stat[240 * i:240 * i + 240, :] = total[0:240]
        stat[480 + 64 * i:544 + 64 * i, :] = total[240:304]
    stat[608:640, :] = jnp.zeros((32, 128), F32)
    line = stat[...].T[0:1]
    line = jnp.concatenate([line[:, 0:256], line[:, 256:512], jnp.concatenate([line[:, 512:640], jnp.zeros((1, 128), F32)], axis=1),
                            jnp.zeros((13, 256), F32)], axis=0).astype(BF)
    for n in range(8):
        blocks[n // 2, n % 2, T:TS, :] = line
    lane = lax.broadcasted_iota(jnp.int32, (512, 128), 1)
    col = lax.broadcasted_iota(jnp.int32, (512, 128), 0)
    kv_sum = block_sum(comm, kvb, (k0, k1, k2), k3, KV_PARTS)
    for n in range(8):
        total = []
        for i in range(2):
            at = lane - 64 * i
            pick = ((at >= 0) & (at < 32) & (col == 32 * n + at)) | ((at >= 32) & (at < 64) & (col == 224 + 32 * n + at))
            pick = pick.astype(F32).astype(BF)
            total.append((dot(dqp[240 * i:240 * i + 240, 256:768], pick, 1, 0), dot(dqa[64 * i:64 * i + 64, 256:768], pick, 1, 0)))
        kvb[n // 2, n % 2, 0:240, :] = (total[0][0] + total[1][0]).astype(BF)
        kvb[n // 2, n % 2, 240:304, :] = (total[0][1] + total[1][1]).astype(BF)
    pump(y_task)
    pump(kv_sum)
    for copy in lc:
        copy.wait()
    mark("terms")

    def terms(step):
        k = place.off("x", step)
        for j in range(2):
            weight = jnp.concatenate([qov[k, j, :, :, 0:256].reshape(256, 256), kvv[k, j].reshape(256, 512)], axis=1)
            blocks[k, j, 0:480, :] = dot(dqp[...], weight, 1, 1).astype(BF)
            weight = jnp.concatenate([qoav[k, j, :, :, 0:256].reshape(128, 256), kvav[k, j].reshape(128, 512)], axis=1)
            small = dot(dqa[...], weight, 1, 1).astype(BF)
            for i in range(2):
                blocks[k, j, 480:544, 128 * i:128 * i + 128] = small[64 * i:64 * i + 64]

    def outer(grad, n, left, right, lo, width):
        def block_rows(k, carry):
            here = pl.ds(pl.multiple_of(4 * n * k, 4 * n), 4 * n)
            value = dot(left[:, here], right, 0, 0).astype(BF)
            grad[k, :, :, :, lo:lo + width] = value.reshape(2, 2, n, width)
            return carry
        lax.fori_loop(0, 4, block_rows, 0)

    terms(2)
    sum_task = block_sum_both(comm, blocks, (l0, l1, l2, l3, l4, l5, l6, l7), TS)
    pump(sum_task)
    terms(1), terms(3), terms(0)
    pump(sum_task)
    mark("attngrads")
    o_act = jnp.concatenate([qv[3, 0, 240:304, :], qv[3, 1, 240:304, :]], axis=0)
    o_pre = jnp.concatenate([qv[3, 0, 0:240, :], qv[3, 1, 0:240, :]], axis=0)
    outer(gq, 128, ghp, o_pre, 256, 256)
    outer(gqa, 64, gha, o_act, 256, 256)
    outer(gq, 128, npv, dqp[:, 0:256], 0, 256)
    outer(gqa, 64, nav, dqa[:, 0:256], 0, 256)
    q_tasks = [wide_sum(comm, gq, sq, tq.at[0], tq.at[1], tq.at[2], zq, 128, True),
               wide_sum(comm, gqa, sqa, tqa.at[0], tqa.at[1], tqa.at[2], zqa, 64, True)]
    kv_tasks = [wide_sum(comm, gkv, skv, tkv.at[0], tkv.at[1], tkv.at[2], zkv, 128, True),
                wide_sum(comm, gkva, skva, tkva.at[0], tkva.at[1], tkva.at[2], zkva, 64, True)]
    pump(*q_tasks)
    pump(late[0])
    pump(kv_sum)
    pump(*q_tasks)
    pump(late[1])
    pump(sum_task)
    pump(kv_sum)
    pump(sum_task)
    pump(y_task)
    drain(kv_sum)
    own = kvb[x, zl]
    share = []
    for i in range(2):
        lane = lax.broadcasted_iota(jnp.int32, (128, 128), 0)
        col = lax.broadcasted_iota(jnp.int32, (128, 128), 1)
        pick = ((col < 64) & (lane == col + 64 * i)).astype(F32).astype(BF)
        share.append(dot(own, pick, 1, 0).astype(BF))
    outer(gkv, 128, npv, jnp.concatenate([share[0][0:240], share[1][0:240]], axis=0), 0, 128)
    outer(gkva, 64, nav, jnp.concatenate([share[0][240:304], share[1][240:304]], axis=0), 0, 128)
    pump(*kv_tasks)
    mark("late")
    pump(sum_task)
    pump(*q_tasks)
    pump(late[0])
    pump(*kv_tasks)
    pump(y_task)
    drain(sum_task)
    mark("dx")
    g_pre, g_act = g8v[x, zl, 0:1, :], g8v[x, zl, 2:3, 0:128]
    f_pre, f_act = g8v[x, zl, 1:2, :], g8v[x, zl, 2:3, 128:256]
    line = blocks[x, zl, T:TS, :].astype(F32)
    line = jnp.concatenate([line[0:1], line[1:2], line[2:3, 0:128]], axis=1)
    stat[...] = jnp.broadcast_to(line, (128, 640)).T

    def own_norm(here, there, lanes, gain_f, gain_a, width):
        s2_, s1_ = r2v[there, 0:1], r1v[there, 0:1]
        back, unit = dv8[x, zl, here, lanes].astype(F32), hv[x, zl, here, lanes].astype(F32) * s2_
        dh = cotv[here, lanes] + s2_ * (back * gain_f - unit * mean[there, 0:1])
        gain_f_grad = jnp.sum(back * unit, axis=0, keepdims=True)
        back, unit = blocks[x, zl, here, lanes].astype(F32), xv[here, lanes].astype(F32) * s1_
        outx[here, lanes] = dh + s1_ * (back * gain_a - unit * (stat[there, 0:1] / width))
        return jnp.sum(back * unit, axis=0, keepdims=True), gain_f_grad

    pre = [own_norm(pl.ds(240 * i, 240), pl.ds(240 * i, 240), pl.ds(0, 256), f_pre, g_pre, 2048) for i in range(2)]
    act = [own_norm(pl.ds(480, 64), pl.ds(480 + 64 * i, 64), pl.ds(128 * i, 128), f_act, g_act, 1024) for i in range(2)]
    gains[...] = jnp.concatenate(
        [pre[0][0] + pre[1][0], pre[0][1] + pre[1][1],
         jnp.concatenate([act[0][0] + act[1][0], act[0][1] + act[1][1]], axis=1), jnp.zeros((5, 256), F32)], axis=0)
    saves = [load(outx, out_x)]
    g_task = small_total(comm, gains16, gains2, gains, gsum)
    pump(g_task)
    mark("tail")
    pump(*q_tasks)
    pump(*kv_tasks)
    pump(late[1])
    drain(y_task)
    outy[...] = (yv[x, place.z].astype(F32) + how[...]).astype(BF)
    saves.append(load(outy, out_y))
    pump(*q_tasks)
    pump(*kv_tasks)
    pump(g_task)
    for task in q_tasks + kv_tasks + late:
        drain(task)
    drain(g_task)
    saves += [load(gsum, out_g), load(gkv.at[y, zh, core], out_kv), load(gkva.at[y, zh, core], out_kva), load(gq.at[y, zh, core], out_q), load(gqa.at[y, zh, core], out_qa)]
    saves += [load(g2v.at[y, zh, core], out_s2.at[zh]), load(z2, out_s2.at[1 - zh])]
    saves += [load(g3v.at[y, zh, core], out_s3.at[zh]), load(z3, out_s3.at[1 - zh])]
    for copy in saves:
        copy.wait()
    mark(None)
    comm.close()


def attend_back(lens, *args):
    outs = [((2, 128, 768), BF), ((2, 128, 768), BF), ((128, 512), BF), ((64, 512), BF), ((128, 128), BF), ((64, 128), BF), ((T, 256), F32),
            ((T, 256), BF), ((8, 256), F32)]
    vm = lambda *s: pltpu.VMEM(s, BF)
    vf = lambda *s: pltpu.VMEM(s, F32)
    wide = lambda n, c: (4, 2, 2, n, c)
    back = [(128, 768), (128, 768), (128, 512), (128, 128), (64, 512), (64, 128)]
    scratch = [vm(4, 2, T, 256), vm(4, 2, T, 256), vm(4, 2, T, 256), vf(608, 128), vf(608, 128), vf(4, 2, 8, 256),
               vm(4, 2, 2, 128, 512), vm(4, 2, 2, 64, 512), vm(4, 2, 2, 128, 512), vm(4, 2, 2, 64, 512),
               vm(480, 2048), vm(128, 1024), vm(4, 2, KEYS, 256), vm(T, 256), vf(T, 256), vm(*wide(128, 768)),
               vm(*wide(128, 768)), vm(4, 4, T, 256), vf(T, 256)]
    scratch += [vf(608, 128), vm(480, 2048), vm(128, 1024), vf(8, 128), vm(2, 304, 256), vm(480, 768), vm(128, 768),
                vf(640, 128), vf(8, 256), vf(8, 256), vf(8, 8, 256), vf(2, 8, 256), vf(64, 256), vf(T, 256), vm(T, 256)]
    scratch += [vm(*wide(n, c)) for n, c in back[2:]]
    scratch += [vm(4, 2, 304, 128), vm(4, 2, TS, 256)] + LAND_16 + block_lands(TS) + [vm(2, 304, 128)] * 3 + [vm(304, 128)]
    scratch += [vm(4, 2, n, c) for n, c in back] + [vm(3, 2, n, c) for n, c in back] + [vm(n, c) for n, c in back]
    return pl.pallas_call(
        attend_back_kernel,
        out_shape=[jax.ShapeDtypeStruct(s, d) for s, d in outs],
        in_specs=[pl.BlockSpec(memory_space=pltpu.SMEM)] + [ANY] * 14 + [INSIDE] * 2 + [ANY] * (len(args) - 16),
        out_specs=[ANY] * len(outs),
        scratch_shapes=scratch + SEM_SCRATCH,
        compiler_params=pltpu.CompilerParams(collective_id=3, has_side_effects=True, vmem_limit_bytes=VMEM_CAP),
        name="attend_back",
    )(lens, *args)
def result_kernel(s0, s1, s2, s3, sa, sq, sqa, skv, skva, y, gx, gains,
                  y_pre, y_act, x_pre, x_act, attn_gain_pre, query_pre, key_pre, value_pre, out_pre, ffn_gain_pre, gate_pre,
                  up_pre, down_pre, attn_gain_act, query_act, key_act, value_act, out_act, ffn_gain_act, gate_act, up_act,
                  down_act):
    for i in range(2):
        here, lanes = slice(240 * i, 240 * i + 240), slice(128 * i, 128 * i + 128)
        y_pre[i], x_pre[i] = y[here, :], gx[here, :]
        x_act[:, i, :] = gx[480:530, lanes]
    low = y[480:544, :].astype(F32)[0:50]
    y_act[...] = jnp.stack([low[:, 0:128], low[:, 128:256]], axis=1).astype(BF)
    attn_gain_pre[...], ffn_gain_pre[...] = gains[0:1, :], gains[1:2, :]
    attn_gain_act[...], ffn_gain_act[...] = gains[2:3, 0:128], gains[2:3, 128:256]
    for q, kv, query, key, value in ((sq, skv, query_pre, key_pre, value_pre),
                                     (sqa, skva, query_act, key_act, value_act)):
        query[...] = q[:, 0:256].astype(F32)
        both = kv[...].astype(F32).T
        key[...], value[...] = both[0:32], both[32:64]
    out_pre[...], out_act[...] = sq[:, 256:512].astype(F32).T, sqa[:, 256:512].astype(F32)
    for h in range(2):
        for i, s in enumerate((s0, s1, s2, s3)):
            here = slice(1024 * h + 256 * i, 1024 * h + 256 * i + 256)
            gate_pre[:, here], up_pre[:, here] = s[h, :, 0:256].astype(F32), s[h, :, 256:512].astype(F32)
            down_pre[here, :] = s[h, :, 512:768].astype(F32).T
        here = slice(256 * h, 256 * h + 256)
        gate_act[:, here], up_act[:, here] = sa[h, :, 0:256].astype(F32), sa[h, :, 256:512].astype(F32)
        down_act[:, here] = sa[h, :, 512:768].astype(F32)


def results(*args):
    tokens = lambda d: [((2, 240, 256), d), ((50, 2, 128), d)]
    expert = lambda n, h, out, down: [((1, n * 2), F32), ((n, 256), F32), ((32, n), F32), ((32, n), F32), (out, F32),
                                      ((1, n * 2), F32), ((n, h), F32), ((n, h), F32), (down, F32)]
    shapes = tokens(BF) + tokens(F32) + expert(128, 2048, (256, 128), (2048, 128)) + expert(64, 512, (64, 256), (64, 512))
    return pl.pallas_call(
        result_kernel,
        out_shape=[jax.ShapeDtypeStruct(s, d) for s, d in shapes],
        in_specs=[INSIDE] * len(args),
        out_specs=[INSIDE] * len(shapes),
        compiler_params=pltpu.CompilerParams(vmem_limit_bytes=VMEM_CAP),
        name="results",
    )(*args)


def local(x_pre, x_act, lengths, cot_pre, cot_act, attn_gain_pre, query_pre, key_pre, value_pre, out_pre, ffn_gain_pre,
          gate_pre, up_pre, down_pre, attn_gain_act, query_act, key_act, value_act, out_act, ffn_gain_act, gate_act,
          up_act, down_act):
    line = lambda gain: gain.reshape(1, -1)
    x_act, cot_act = x_act.transpose(1, 0, 2), cot_act.transpose(1, 0, 2)
    key_pre, value_pre, key_act, value_act, out_act, down_act = (
        m.T for m in (key_pre, value_pre, key_act, value_act, out_act, down_act))
    (xb, f, fa, qo, qoa, kv, kva, g8, n1p, n1a, qkvo, r1, h_own, h16, n2p, n2a, r2) = attend(
        lengths, x_pre, x_act, line(attn_gain_pre), query_pre, key_pre, value_pre, out_pre, line(ffn_gain_pre), gate_pre,
        up_pre, down_pre, line(attn_gain_act), query_act, key_act, value_act, out_act, line(ffn_gain_act), gate_act, up_act,
        down_act)
    s0, s1, sa, g2, g3, d8, yt, c8 = feed_forward(f, fa, n2p, n2a, cot_pre, cot_act)
    s2, s3, sq, sqa, skv, skva, gx, y, gains = attend_back(
        lengths, d8, h16, c8, r2, r1, g8, qo, qoa, kv, kva, n1p, n1a, qkvo, xb, cot_pre, cot_act, g2, g3, yt, h_own)
    outs = results(s0, s1, s2, s3, sa, sq, sqa, skv, skva, y, gx, gains)
    turn = lambda i, o: o.transpose(1, 0, 2) if i in (1, 3) else o.T if i in (6, 7, 15, 16, 17, 21) else o
    return tuple(o.reshape(-1) if o.shape[0] == 1 else turn(i, o) for i, o in enumerate(outs))


def solution(mesh):
    tok, row, col, vec = P("wide", None, "narrow"), P("wide", "narrow"), P("narrow", "wide"), P("narrow")
    expert = (vec, row, row, row, col, vec, row, row, col)
    return jax.shard_map(
        local, mesh=mesh, in_specs=(tok, tok, P("wide"), tok, tok) + expert + expert,
        out_specs=(tok,) * 4 + expert + expert, check_vma=False)
```

```python
import functools
import jax
import jax.numpy as jnp
from jax import lax
from jax.experimental import pallas as pl
from jax.experimental.pallas import tpu as pltpu
from jax.sharding import PartitionSpec as P

MESH = pl.DeviceIdType.MESH
BF = jnp.bfloat16
F32 = jnp.float32
SEMS = 256
LOCAL_SEMS = 48
VMEM_CAP = 62 * 1024 * 1024


class Place:
    def __init__(self):
        wide, narrow = lax.axis_index("wide"), lax.axis_index("narrow")
        self.core = lax.rem(wide, 2)
        self.zh = lax.rem(lax.div(wide, 2), 2)
        self.y = lax.div(wide, 4)
        self.zl = lax.rem(narrow, 2)
        self.x = lax.div(narrow, 2)
        self.z = self.zh * 2 + self.zl

    def wide_at(self, y, zh, core):
        return (y * 2 + zh) * 2 + core

    def coord(self, axis):
        return {"x": self.x, "y": self.y, "z": self.z}[axis]

    def off(self, axis, step):
        return lax.rem(self.coord(axis) + step + 4, 4)

    def peer(self, name):
        if name == "sib":
            return {"wide": self.wide_at(self.y, self.zh, 1 - self.core)}
        if name == "z2":
            return {"wide": self.wide_at(self.y, 1 - self.zh, self.core)}
        if name == "zl":
            return {"narrow": self.x * 2 + 1 - self.zl}
        if name[0] == "w":
            step, flip = int(name[1]), int(name[2])
            zh = 1 - self.zh if flip else self.zh
            return {"wide": self.wide_at(self.off("y", step), zh, self.core)}
        if name[0] == "n":
            zl = 1 - self.zl if int(name[2]) else self.zl
            return {"narrow": self.off("x", int(name[1])) * 2 + zl}
        axis, step = name[0], 1 if name[1] == "+" else -1
        at = self.off(axis, step)
        if axis == "y":
            return {"wide": self.wide_at(at, self.zh, self.core)}
        if axis == "x":
            return {"narrow": at * 2 + self.zl}
        return {"wide": self.wide_at(self.y, lax.div(at, 2), self.core), "narrow": self.x * 2 + lax.rem(at, 2)}


class Link:
    def __init__(self, out, into):
        self.out, self.into = out, into

    def arrive(self):
        self.into.wait_recv()

    def left(self):
        self.out.wait_send()


class Comm:
    def __init__(self, send_sems, recv_sems, local_sems):
        self.place = Place()
        self.send_sems, self.recv_sems, self.local_sems = send_sems, recv_sems, local_sems
        self.count, self.local_count = 0, 0
        self.links = []

    def enter(self, peers):
        barrier = pltpu.get_barrier_semaphore()
        for name in peers:
            pl.semaphore_signal(barrier, inc=1, device_id=self.place.peer(name), device_id_type=MESH)
        pl.semaphore_wait(barrier, len(peers))

    def send(self, src, dst, name, incoming):
        index = self.count
        self.count += 1
        assert index < SEMS
        make = lambda to: pltpu.make_async_remote_copy(
            src_ref=src, dst_ref=to, send_sem=self.send_sems.at[index], recv_sem=self.recv_sems.at[index],
            device_id=self.place.peer(name), device_id_type=MESH)
        out = make(dst)
        out.start()
        link = Link(out, make(incoming))
        self.links.append(link)
        return link

    def local(self, src, dst):
        index = self.local_count
        self.local_count += 1
        assert index < LOCAL_SEMS
        copy = pltpu.make_async_copy(src, dst, self.local_sems.at[index])
        copy.start()
        return copy

    def settle(self):
        for link in self.links:
            link.left()
        self.links = []

    def close(self):
        self.settle()

    def ring_gather(self, axis, view, parts, own=None, staged=False):
        place = self.place
        at = lambda step: place.off(axis, step)
        src = own if own is not None else (lambda part: view(at(0), part))
        up_first = sorted(parts, key=lambda part: -part[1])
        plus = [(way, p, self.send(src(p), view(at(0), p), axis + "+", view(at(-1), p))) for p, way in up_first]
        minus = [(way, p, self.send(src(p), view(at(0), p), axis + "-", view(at(1), p))) for p, way in up_first[::-1]]
        yield
        rest = []
        for way, p, link in plus:
            if way > 0:
                link.arrive()
                rest.append(self.send(view(at(-1), p), view(at(-1), p), axis + "+", view(at(-2), p)))
        for way, p, link in minus:
            if way < 0:
                link.arrive()
                rest.append(self.send(view(at(1), p), view(at(1), p), axis + "-", view(at(2), p)))
        yield
        for way, p, link in plus:
            if way < 0:
                link.arrive()
        for way, p, link in minus:
            if way > 0:
                link.arrive()
        if staged:
            yield
        for link in rest:
            link.arrive()

    def pair_ring_gather(self, pair, axis, view, parts, own, give, whole, swap_first=False):
        place = self.place
        mine = {"z2": place.zh, "zl": place.zl}[pair]
        here = place.coord(axis)
        first = self.ring_gather(axis, lambda k, p: view(k, mine, p), parts, own)
        if not swap_first:
            next(first)
            yield
        swap = self.send(give, view(here, mine, whole), pair, view(here, 1 - mine, whole))
        yield
        if swap_first:
            next(first)
            yield
        next(first)
        yield
        swap.arrive()
        second = self.ring_gather(axis, lambda k, p: view(k, 1 - mine, p), parts)
        next(second)
        yield
        next(second)
        yield
        drain(first)
        drain(second)

    def plane_gather(self, view, parts_x, parts_z, own=None, ready=None):
        place = self.place
        ax = self.ring_gather("x", lambda k, p: view(k, place.z, p), parts_x, own, True)
        bz = self.ring_gather("z", lambda k, p: view(place.x, k, p), parts_z, own, True)
        onward = lambda step: [
            self.ring_gather("z", lambda k, p: view(place.off("x", step), k, p), parts_x),
            self.ring_gather("x", lambda k, p: view(k, place.off("z", step), p), parts_z)]
        next(ax), next(bz)
        yield
        next(ax), next(bz)
        next(ax)
        if ready is not None:
            ready()
        close = [onward(step) for step in (0, 1, -1)]
        for az, _ in close:
            next(az)
        next(bz)
        for _, bx in close:
            next(bx)
        yield
        drain(ax)
        last = onward(2)
        next(last[0])
        drain(bz)
        next(last[1])
        yield
        for az, bx in close:
            next(az), next(bx)
        yield
        next(last[0]), next(last[1])
        yield
        for az, bx in close + [last]:
            drain(az), drain(bx)

    def ring_sum(self, axis, view, parts, relay, plus, minus, split=False):
        place = self.place
        at = lambda step: place.off(axis, step)
        near = {1: lambda p: self.send(view(at(1), p), plus(p), axis + "+", plus(p)),
                -1: lambda p: self.send(view(at(-1), p), minus(p), axis + "-", minus(p))}
        far = [(p, way, self.send(view(at(2), p), relay(p), axis + ("+" if way > 0 else "-"), relay(p))) for p, way in parts]
        if split:
            yield
        links = [near[-way](p) for p, way in parts]
        yield
        for p, way, link in far:
            link.arrive()
            add_to(view(at(way), p), relay(p))
            links.append(near[way](p))
        yield
        for link in links:
            link.arrive()
        for p, _ in parts:
            add_to(view(at(0), p), plus(p), minus(p))


def add_to(ref, *others):
    total = ref[...].astype(F32)
    for other in others:
        total = total + other[...].astype(F32)
    ref[...] = total.astype(ref.dtype)


def drain(task):
    for _ in task:
        pass


def rows(lo, hi):
    return pl.ds(lo, hi - lo)
T = 544
CH = 4


def halves(n):
    return [(rows(0, n // 2), 1), (rows(n // 2, n), -1)]


PARTS_8 = [(rows(0, 272), 1), (rows(272, 544), -1)]
PARTS_A = [(rows(0, 144), 1), (rows(144, 272), -1)]
PARTS_B = [(rows(272, 416), 1), (rows(416, 544), -1)]
PEERS = ("y+", "y-", "z2", "sib", "x+", "x-", "z+", "z-")


def wide_gather(comm, out, own, give, n, parts=None, swap_first=False):
    place = comm.place
    core = place.core
    copy = comm.local(own, out.at[place.y, place.zh, core])
    task = comm.pair_ring_gather(
        "z2", "y", lambda k, j, p: out.at[k, j, core, p], parts or halves(n),
        lambda p: own.at[p], give, slice(None), swap_first)
    yield from task
    copy.wait()
    link = comm.send(out.at[:, :, core], out.at[:, :, core], "sib", out.at[:, :, 1 - core])
    yield
    link.arrive()


def block_gather(comm, out, own, parts):
    place = comm.place
    copy = comm.local(own, out.at[place.x, place.zl])
    yield from comm.pair_ring_gather(
        "zl", "x", lambda k, j, p: out.at[k, j, p], parts, lambda p: own.at[p], own, slice(None))
    copy.wait()


STEPS = [(step, flip) for flip in range(2) for step in range(4) if step or flip]


def small_gather(comm, out, own):
    place = comm.place
    copy = comm.local(own, out.at[place.x, place.zl])
    links = []
    for step, flip in STEPS:
        back = out.at[place.off("x", -step), 1 - place.zl if flip else place.zl]
        links.append(comm.send(own, out.at[place.x, place.zl], f"n{step}{flip}", back))
    yield
    copy.wait()
    for link in links:
        link.arrive()


def plane_spread(comm, out, own):
    place = comm.place
    copy = comm.local(own, out.at[place.x, place.z])
    yield from comm.plane_gather(lambda k, j, p: out.at[k, j, p], PARTS_A, PARTS_B, lambda p: own.at[p], copy.wait)


def block_sum(comm, blocks, lands, swap, parts, z=None):
    place = comm.place
    relay, plus, minus = lands
    upto = pl.ds(0, sum(p.size for p, _ in parts))
    xs = comm.ring_sum(
        "x", lambda k, p: blocks.at[k, :, p], parts,
        lambda p: relay.at[:, p], lambda p: plus.at[:, p], lambda p: minus.at[:, p], z is not None)
    next(xs)
    yield
    if z is not None:
        z_rows, z_parts, z_land, z_lands = z
        next(xs)
        link = comm.send(blocks.at[:, 1 - place.zl, z_rows], z_land, "zl", z_land)
        yield
    next(xs)
    yield
    if z is not None:
        link.arrive()
        add_to(blocks.at[:, place.zl, z_rows], z_land)
        zs = comm.ring_sum("x", lambda k, p: blocks.at[k, place.zl, p], z_parts,
                           *[(lambda p, land=land: land.at[pl.ds(p.start - z_rows.start, p.size)]) for land in z_lands])
        next(zs)
        yield
    drain(xs)
    last = comm.send(blocks.at[place.x, 1 - place.zl, upto], swap, "zl", swap)
    if z is not None:
        next(zs)
    yield
    last.arrive()
    add_to(blocks.at[place.x, place.zl, upto], swap)
    if z is not None:
        drain(zs)


def plane_sum(comm, blocks, lands_far, lands_near):
    place = comm.place
    az = comm.ring_sum("z", lambda k, p: blocks.at[:, k, p], PARTS_A,
                       lambda p: lands_far.at[0, :, p], lambda p: lands_far.at[1, :, p], lambda p: lands_far.at[2, :, p], True)
    bx = comm.ring_sum("x", lambda k, p: blocks.at[k, :, p], PARTS_B,
                       lambda p: lands_far.at[0, :, p], lambda p: lands_far.at[1, :, p], lambda p: lands_far.at[2, :, p], True)
    for _ in range(3):
        next(az), next(bx)
        yield
    drain(az)
    ax = comm.ring_sum("x", lambda k, p: blocks.at[k, place.z, p], PARTS_A,
                       lambda p: lands_near.at[0, p], lambda p: lands_near.at[1, p], lambda p: lands_near.at[2, p])
    next(ax)
    drain(bx)
    bz = comm.ring_sum("z", lambda k, p: blocks.at[place.x, k, p], PARTS_B,
                       lambda p: lands_near.at[0, p], lambda p: lands_near.at[1, p], lambda p: lands_near.at[2, p])
    next(bz)
    yield
    next(ax), next(bz)
    yield
    drain(ax), drain(bz)


CHIPS = [(step, flip) for flip in range(2) for step in range(4) if step or flip]


def small_total(comm, slots, pair, own, out):
    place = comm.place
    mine = place.y * 2 + place.zh
    links = []
    for step, flip in CHIPS:
        back = place.off("y", -step) * 2 + (1 - place.zh if flip else place.zh)
        links.append(comm.send(own, slots.at[mine], f"w{step}{flip}", slots.at[back]))
    slots[mine] = own[...]
    yield
    for link in links:
        link.arrive()
    pair[0] = sum(slots[i] for i in range(8))
    link = comm.send(pair.at[0], pair.at[1], "sib", pair.at[1])
    yield
    link.arrive()
    out[...] = pair[0] + pair[1]


def wide_sum(comm, grad, half, relay, plus, minus, swap, n, add):
    place = comm.place
    core, zh = place.core, place.zh
    link = comm.send(grad.at[:, :, 1 - core], half, "sib", half)
    yield
    link.arrive()
    def fold(k, carry):
        add_to(grad.at[k, :, core], half.at[k])
        return carry
    lax.fori_loop(0, 4, fold, 0)
    yield from comm.ring_sum(
        "y", lambda k, p: grad.at[k, :, core, p], halves(n),
        lambda p: relay.at[:, p], lambda p: plus.at[:, p], lambda p: minus.at[:, p])
    link = comm.send(grad.at[place.y, 1 - zh, core], swap, "z2", swap)
    yield
    link.arrive()
    if add:
        add_to(grad.at[place.y, zh, core], swap)


SEM_SCRATCH = [pltpu.SemaphoreType.DMA((SEMS,)), pltpu.SemaphoreType.DMA((SEMS,)), pltpu.SemaphoreType.DMA((LOCAL_SEMS,))]
ANY = pl.BlockSpec(memory_space=pl.ANY)
INSIDE = pl.BlockSpec(memory_space=pltpu.VMEM)


X_ROWS = 400
X_PARTS = [(rows(0, 208), 1), (rows(208, 400), -1)]


def block_lands(count):
    z = count - X_ROWS
    return ([pltpu.VMEM((2, X_ROWS, 256), BF)] * 3 + [pltpu.VMEM((X_ROWS, 256), BF), pltpu.VMEM((4, z, 256), BF)]
            + [pltpu.VMEM((z, 256), BF)] * 3)


def block_sum_both(comm, blocks, lands, count):
    z = (rows(X_ROWS, count), [(rows(X_ROWS, 480), 1), (rows(480, count), -1)], lands[4], lands[5:8])
    return block_sum(comm, blocks, lands[0:3], lands[3], X_PARTS, z)


LAND_16 = [pltpu.VMEM((3, 4, T, 256), BF), pltpu.VMEM((3, T, 256), BF)]


EPSILON = 1e-06
MASKED = -1000000000.0
KEYS = 384


def dot(a, b, ca, cb):
    return lax.dot_general(a, b, (((ca,), (cb,)), ((), ())), preferred_element_type=F32)


_open = []


def mark(name):
    if _open:
        _open.pop().__exit__(None, None, None)
    if name:
        scope = jax.named_scope(name)
        scope.__enter__()
        _open.append(scope)


def pump(*tasks):
    for task in tasks:
        next(task, None)


def seen(length):
    s = lax.broadcasted_iota(jnp.int32, (304, KEYS), 0)
    t = lax.broadcasted_iota(jnp.int32, (304, KEYS), 1)
    live = (t < 192) | ((t >= 240) & (t < 290)) | ((t < 240) & (t - 192 < length))
    return live & ((t < 240) | (s >= 240))


def soft(q, k, length):
    scores = dot(q, k, 1, 1) * 0.0625
    scores = jnp.where(seen(length), scores, MASKED)
    weights = jnp.exp(scores - jnp.max(scores, axis=1, keepdims=True))
    return weights / jnp.sum(weights, axis=1, keepdims=True)


def pairs8():
    return [(x, zl) for x in range(4) for zl in range(2)]


def norm_block_rows(get, gain, width, put):
    total = sum(jnp.sum(get(n) * get(n), axis=1, keepdims=True) for n in range(8))
    scale = lax.rsqrt(total / (8 * width) + EPSILON)
    for n in range(8):
        put(n, (get(n) * scale * gain(n)).astype(BF))
    return scale


def act_rows(act, spare):
    spare[...] = jnp.zeros((64, 256), F32)
    rows_of = act[...].astype(F32)
    for i in range(2):
        spare[0:50, 128 * i:128 * i + 128] = rows_of[:, i, :]
    return spare[...]


def turned(m):
    return m.astype(F32).T.astype(BF)


def attend_kernel(lens, x_pre, x_act, attn_gain_pre, query_pre, key_pre, value_pre, out_pre, ffn_gain_pre, gate_pre, up_pre,
                  down_pre, attn_gain_act, query_act, key_act, value_act, out_act, ffn_gain_act, gate_act, up_act, down_act,
                  out_xb, out_f, out_fa, out_q, out_qa, out_kv, out_kva, out_g, out_n1p, out_n1a, out_qkvo, out_r1,
                  out_h, out_h16, out_n2p, out_n2a, out_r2,
                  kv8, kvf, qo, qoa, kv, kva, x8, g8, n1p, n1a, qkvo, r1, xv, hv, full, n2p, n2a, r2,
                  blocks, l0, l1, l2, l3, l4, l5, l6, l7, wf, wfa, wq, wqa, kvs, gb, spare, *sems):
    comm = Comm(*sems)
    place = comm.place
    zh = place.zh
    for i in range(2):
        xv[240 * i:240 * i + 240, :] = x_pre[i]
    xv[480:544, :] = act_rows(x_act, spare).astype(BF)
    lane = lax.broadcasted_iota(jnp.int32, (32, 128), 1)
    row = lax.broadcasted_iota(jnp.int32, (32, 128), 0)
    spread = [(lane == row + 32 * j).astype(F32).astype(BF) for j in range(4)]
    for base, half, key, value in ((0, 64, key_pre, value_pre), (64, 32, key_act, value_act)):
        kvs[base:base + half, :] = (
            dot(key[:, 0:half], spread[0], 0, 0) + dot(value[:, 0:half], spread[1], 0, 0)
            + dot(key[:, half:2 * half], spread[2], 0, 0) + dot(value[:, half:2 * half], spread[3], 0, 0)).astype(BF)
    gb[...] = jnp.concatenate([attn_gain_pre[...], ffn_gain_pre[...],
                               jnp.concatenate([attn_gain_act[...], ffn_gain_act[...]], axis=1), jnp.zeros((5, 256), F32)], axis=0)
    wq[:, 0:256], wqa[:, 0:256] = query_pre[...], query_act[...]
    wq[:, 256:512], wqa[:, 256:512] = turned(out_pre[...]), out_act[...]
    zero = jnp.zeros((KEYS - 304, 256), BF)
    for i in range(2):
        for j in (1, 2):
            qkvo[j, i, 304:KEYS, :] = zero
    comm.enter(PEERS + ("n20", "n11", "n21", "n31"))

    mark('start')
    kv_task = small_gather(comm, kv8, kvs)
    g_task = small_gather(comm, g8, gb)
    x_task = block_gather(comm, x8, xv, PARTS_8)
    q_tasks = [wide_gather(comm, qo, wq, wq, 128), wide_gather(comm, qoa, wqa, wqa, 64)]
    f_tasks = [wide_gather(comm, out_f.at[i], wf.at[zh, i], wf.at[1 - zh, i], 128, None, True) for i in range(CH)]
    f_tasks.append(wide_gather(comm, out_fa, wfa.at[zh], wfa.at[1 - zh], 64, None, True))
    pump(kv_task)
    pump(g_task)
    pump(x_task), pump(x_task)
    pump(*q_tasks), pump(*q_tasks)
    for h in range(2):
        for i in range(CH):
            here = slice(1024 * h + 256 * i, 1024 * h + 256 * i + 256)
            wf[h, i, :, 0:256], wf[h, i, :, 256:512] = gate_pre[:, here], up_pre[:, here]
            wf[h, i, :, 512:768] = turned(down_pre[here, :])
        here = slice(256 * h, 256 * h + 256)
        wfa[h, :, 0:256], wfa[h, :, 256:512] = gate_act[:, here], up_act[:, here]
        wfa[h, :, 512:768] = down_act[:, here]
    drain(kv_task)
    lane = lax.broadcasted_iota(jnp.int32, (128, 512), 0)
    col = lax.broadcasted_iota(jnp.int32, (128, 512), 1)
    for side in range(2):
        total = jnp.zeros((96, 512), F32)
        at = lane - 64 * side
        for n in range(8):
            pick = ((at >= 0) & (at < 32) & (col == 32 * n + at)) | ((at >= 32) & (at < 64) & (col == 224 + 32 * n + at))
            total = total + dot(kv8[n // 2, n % 2], pick.astype(F32).astype(BF), 1, 0)
        kvf[64 * side:64 * side + 64, :] = total[0:64].astype(BF)
        kvf[128 + 32 * side:160 + 32 * side, :] = total[64:96].astype(BF)
    kv_a, kv_b = kvf.at[0:128], kvf.at[128:192]
    kv_tasks = [wide_gather(comm, kv, kv_a, kv_a, 128), wide_gather(comm, kva, kv_b, kv_b, 64)]
    pump(*kv_tasks), pump(*kv_tasks)
    pump(x_task)
    pump(x_task)
    pump(*q_tasks)
    pump(*kv_tasks)
    pump(*f_tasks)
    pump(*q_tasks)
    pump(*kv_tasks)
    pump(x_task)
    pump(*q_tasks)
    pump(*kv_tasks)
    pump(*f_tasks)
    drain(g_task)
    drain(x_task)

    mark('norm1')
    for i in range(2):
        here = pl.ds(240 * i, 240)
        get = lambda n: x8[n // 2, n % 2, here, :].astype(F32)
        def put(n, v):
            n1p[here, 256 * n:256 * n + 256] = v
        r1[here, :] = jnp.broadcast_to(norm_block_rows(get, lambda n: g8[n // 2, n % 2, 0:1, :], 256, put), (240, 128))
        low = pl.ds(480, 64)
        get = lambda n: x8[n // 2, n % 2, low, 128 * i:128 * i + 128].astype(F32)
        def put(n, v):
            n1a[64 * i:64 * i + 64, 128 * n:128 * n + 128] = v
        r1[480 + 64 * i:544 + 64 * i, :] = jnp.broadcast_to(
            norm_block_rows(get, lambda n: g8[n // 2, n % 2, 2:3, 0:128], 128, put), (64, 128))
    pump(*q_tasks)
    pump(*kv_tasks)
    for task in q_tasks:
        drain(task)
    mark('qkv')
    def queries(i, carry):
        here = pl.ds(pl.multiple_of(240 * i, 16), 240)
        qkvo[0, i, 0:240, :] = dot(n1p[here, :], qo[:, :, :, :, 0:256].reshape(2048, 256), 1, 0).astype(BF)
        return carry
    lax.fori_loop(0, 2, queries, 0)
    for task in kv_tasks:
        drain(task)
    def keys(i, carry):
        here = pl.ds(pl.multiple_of(240 * i, 16), 240)
        for j in range(2):
            qkvo[1 + j, i, 0:240, :] = dot(
                n1p[here, :], kv[:, :, :, :, 256 * j:256 * j + 256].reshape(2048, 256), 1, 0).astype(BF)
        return carry
    lax.fori_loop(0, 2, keys, 0)
    low = [dot(n1a[...], qoa[:, :, :, :, 0:256].reshape(1024, 256), 1, 0).astype(BF)]
    for j in range(2):
        low.append(dot(n1a[...], kva[:, :, :, :, 256 * j:256 * j + 256].reshape(1024, 256), 1, 0).astype(BF))
    for i in range(2):
        for j in range(3):
            qkvo[j, i, 240:304, :] = low[j][64 * i:64 * i + 64]
    saves = [comm.local(qo, out_q), comm.local(qoa, out_qa), comm.local(kv, out_kv), comm.local(kva, out_kva),
             comm.local(n1p, out_n1p), comm.local(n1a, out_n1a), comm.local(r1, out_r1), comm.local(g8, out_g)]
    mark('attn')
    for i in range(2):
        probs = soft(qkvo[0, i, 0:304, :], qkvo[1, i], lens[i])
        qkvo[3, i, 0:304, :] = dot(probs.astype(BF), qkvo[2, i], 1, 0).astype(BF)
    saves.append(comm.local(qkvo, out_qkvo))
    mark('outproj')
    oa = jnp.concatenate([qkvo[3, 0, 240:304, :], qkvo[3, 1, 240:304, :]], axis=0)

    def terms(step):
        k = place.off("x", step)
        for j in range(2):
            weight = qo[k, j, :, :, 256:512].reshape(256, 256)
            for i in range(2):
                blocks[k, j, 240 * i:240 * i + 240, :] = dot(qkvo[3, i, 0:240, :], weight, 1, 1).astype(BF)
            small = dot(oa, qoa[k, j, :, :, 256:512].reshape(128, 256), 1, 1).astype(BF)
            for i in range(2):
                blocks[k, j, 480:544, 128 * i:128 * i + 128] = small[64 * i:64 * i + 64]

    mark('rs8')
    sum_task = block_sum_both(comm, blocks, (l0, l1, l2, l3, l4, l5, l6, l7), T)
    terms(2)
    pump(sum_task)
    terms(1), terms(3), terms(0)
    pump(sum_task)
    pump(f_tasks[0], f_tasks[1])
    pump(f_tasks[0], f_tasks[1])
    pump(sum_task)
    pump(f_tasks[2])
    pump(f_tasks[2])
    pump(sum_task)
    pump(f_tasks[3], f_tasks[4])
    pump(f_tasks[3], f_tasks[4])
    pump(sum_task)
    drain(sum_task)
    mark('hmake')
    hv[...] = xv[...].astype(F32) + blocks[place.x, place.zl].astype(F32)
    full[place.x, place.z] = hv[...].astype(BF)
    saves += [comm.local(hv, out_h), comm.local(xv, out_xb)]
    mark('hplane')
    h_task = comm.plane_gather(lambda k, j, p: full.at[k, j, p], PARTS_A, PARTS_B)
    pump(h_task)
    pump(h_task)
    pump(f_tasks[0])
    pump(h_task)
    pump(f_tasks[1])
    pump(h_task)
    pump(f_tasks[2])
    pump(h_task)
    pump(f_tasks[3], f_tasks[4])
    pump(f_tasks[0], f_tasks[1])
    drain(h_task)
    saves.append(comm.local(full, out_h16))
    mark('norm2')
    for zhi in range(2):
        def rows_norm(i, carry):
            here = pl.ds(pl.multiple_of(240 * i, 16), 240)
            there = pl.ds(pl.multiple_of(480 * zhi + 240 * i, 16), 240)
            get = lambda n: full[n // 2, 2 * zhi + n % 2, here, :].astype(F32)
            def put(n, v):
                n2p[there, 256 * n:256 * n + 256] = v
            scale = norm_block_rows(get, lambda n: g8[n // 2, n % 2, 1:2, :], 256, put)
            r2[zhi, here, :] = jnp.broadcast_to(scale, (240, 128))
            return carry
        lax.fori_loop(0, 2, rows_norm, 0)
        for i in range(2):
            get = lambda n: full[n // 2, 2 * zhi + n % 2, 480:544, 128 * i:128 * i + 128].astype(F32)
            base = 128 * zhi + 64 * i
            def put(n, v):
                n2a[base:base + 64, 128 * n:128 * n + 128] = v
            scale = norm_block_rows(get, lambda n: g8[n // 2, n % 2, 2:3, 128:256], 128, put)
            r2[zhi, 480 + 64 * i:544 + 64 * i, :] = jnp.broadcast_to(scale, (64, 128))
    mark('tail')
    saves += [comm.local(n2p, out_n2p), comm.local(n2a, out_n2a), comm.local(r2.at[zh], out_r2)]
    pump(*f_tasks[2:])
    for task in f_tasks:
        drain(task)
    for copy in saves:
        copy.wait()
    mark(None)
    comm.close()


def attend(lens, *args):
    wide5 = lambda n, c: (4, 2, 2, n, c)
    outs = [((T, 256), BF), ((CH,) + wide5(128, 768), BF), (wide5(64, 768), BF), (wide5(128, 512), BF), (wide5(64, 512), BF),
            (wide5(128, 512), BF), (wide5(64, 512), BF), ((4, 2, 8, 256), F32),
            ((480, 2048), BF), ((128, 1024), BF), ((4, 2, KEYS, 256), BF), ((608, 128), F32), ((T, 256), F32),
            ((4, 4, T, 256), BF), ((960, 2048), BF), ((256, 1024), BF), ((608, 128), F32)]
    vm = pltpu.VMEM
    scratch = [vm((4, 2, 96, 128), BF), vm((192, 512), BF)] + [vm(s, d) for s, d in outs[3:7]] + [
        vm((4, 2, T, 256), BF), vm((4, 2, 8, 256), F32), vm((480, 2048), BF), vm((128, 1024), BF),
        vm((4, 2, KEYS, 256), BF), vm((608, 128), F32), vm((T, 256), BF), vm((T, 256), F32), vm((4, 4, T, 256), BF),
        vm((960, 2048), BF), vm((256, 1024), BF), vm((2, 608, 128), F32), vm((4, 2, T, 256), BF)] + block_lands(T)
    scratch += [vm((2, CH, 128, 768), BF), vm((2, 64, 768), BF), vm((128, 512), BF), vm((64, 512), BF), vm((96, 128), BF),
                vm((8, 256), F32), vm((64, 256), F32)]
    return pl.pallas_call(
        attend_kernel,
        out_shape=[jax.ShapeDtypeStruct(s, d) for s, d in outs],
        in_specs=[pl.BlockSpec(memory_space=pltpu.SMEM)] + [INSIDE] * len(args),
        out_specs=[ANY] * len(outs),
        scratch_shapes=scratch + SEM_SCRATCH,
        compiler_params=pltpu.CompilerParams(collective_id=0, has_side_effects=True, vmem_limit_bytes=VMEM_CAP),
        name="attend",
    )(lens, *args)
EARLY = 2
TILE = 240


def gelu_parts(z):
    a, b = 0.7978845608028654, 0.044715
    t = jnp.tanh(a * (z + b * z * z * z))
    half = 0.5 * (1.0 + t)
    return z * half, half + 0.5 * z * (1.0 - t * t) * a * (1.0 + 3.0 * b * z * z)


def side_rows(full, z_low, base, count):
    return jnp.concatenate([full[x, z_low + zl, pl.ds(base, count), :] for x, zl in pairs8()], axis=1)


def feed_forward_kernel(f, fa, n2p, n2a, cot_pre, cot_act, *refs):
    out_s, out_late, refs = refs[:EARLY + 1], refs[EARLY + 1:CH + 1], refs[CH + 1:]
    out_d8, out_y, out_c, wv, wav, np_, na, gc, ga, dd, aa, dda, aaa, bb, bf, bn, d8, grad_act, cb, spare = refs[:20]
    lands = [refs[20 + 3 * i:23 + 3 * i] for i in range(EARLY + 1)]
    comm = Comm(*refs[-3:])
    place = comm.place
    loads = [comm.local(n2p, np_), comm.local(f.at[0], wv.at[0]), comm.local(n2a, na),
             comm.local(f.at[1], wv.at[1]), comm.local(f.at[2], wv.at[2]), comm.local(f.at[3], wv.at[3]),
             comm.local(fa, wav)]
    for i in range(2):
        cb[240 * i:240 * i + 240, :] = cot_pre[i].astype(BF)
    cb[480:544, :] = act_rows(cot_act, spare).astype(BF)
    c_task = plane_spread(comm, gc, cb)
    comm.enter(PEERS)
    pump(c_task)
    mark("units")
    loads[0].wait()

    def gate_up(left, weight):
        both = dot(left, weight, 1, 0)
        up = both[:, 256:512]
        value, slope = gelu_parts(both[:, 0:256])
        return (value * up).astype(BF), (up * slope).astype(BF), value.astype(BF)

    for i in range(CH):
        loads[(1, 3, 4, 5)[i]].wait()
        def unit(t, carry):
            here = pl.ds(pl.multiple_of(TILE * t, 16), TILE)
            a, b, c = gate_up(np_[here, :], wv[i, :, :, :, :, 0:512].reshape(2048, 512))
            aa[here, 256 * i:256 * i + 256] = a
            dd[here, 512 * i:512 * i + 256] = b
            dd[here, 512 * i + 256:512 * i + 512] = c
            return carry
        lax.fori_loop(0, 4, unit, 0)
        if i in (0, 1):
            pump(c_task)
    loads[2].wait(), loads[6].wait()
    aaa[...], dda[:, 0:256], dda[:, 256:512] = gate_up(na[...], wav[:, :, :, :, 0:512].reshape(1024, 512))

    def product(ref, x, z, left, left_a, lo, hi):
        zh_, zl_ = lax.div(z, 2), lax.rem(z, 2)
        here = pl.ds(pl.multiple_of(480 * zh_, 16), 480)
        rows_w = jnp.concatenate([wv[i, x, zl_, :, :, lo:hi].reshape(256, hi - lo) for i in range(CH)], axis=1)
        ref[0:480, :] = dot(left[here, :], rows_w, 1, 1).astype(BF)
        there = pl.ds(pl.multiple_of(128 * zh_, 16), 128)
        small = dot(left_a[there, :], wav[x, zl_, :, :, lo:hi].reshape(128, hi - lo), 1, 1).astype(BF)
        ref[480:544, 0:128] = small[0:64]
        ref[480:544, 128:256] = small[64:128]

    def down_terms(t, carry):
        x, z = lax.div(t, 4), lax.rem(t, 4)
        product(bb.at[x, z], x, z, aa, aaa, 512, 768)
        return carry

    mark("ydown")
    pump(c_task)
    lax.fori_loop(0, 8, down_terms, 0)
    pump(c_task)
    lax.fori_loop(8, 16, down_terms, 0)
    saves = [comm.local(bb, out_y)]
    mark("cwait")
    drain(c_task)
    saves.append(comm.local(gc.at[:, pl.ds(2 * place.zh, 2)], out_c))
    mark("dact")
    for i in range(CH):
        def dact_unit(t, carry):
            here = pl.ds(pl.multiple_of(TILE * t, 16), TILE)
            rows_c = side_rows(gc, 2 * lax.div(t, 2), pl.multiple_of(TILE * lax.rem(t, 2), 16), TILE)
            dact = dot(rows_c, wv[i, :, :, :, :, 512:768].reshape(2048, 256), 1, 0)
            for j in range(2):
                there = slice(512 * i + 256 * j, 512 * i + 256 * j + 256)
                dd[here, there] = (dact * dd[here, there].astype(F32)).astype(BF)
            return carry
        lax.fori_loop(0, 4, dact_unit, 0)
    for zhi in range(2):
        for i in range(2):
            base = 128 * zhi + 64 * i
            for n in range(8):
                ga[base:base + 64, 128 * n:128 * n + 128] = gc[n // 2, 2 * zhi + n % 2, 480:544, 128 * i:128 * i + 128]
    dact = dot(ga[...], wav[:, :, :, :, 512:768].reshape(1024, 256), 1, 0)
    for j in range(2):
        there = slice(256 * j, 256 * j + 256)
        dda[:, there] = (dact * dda[:, there].astype(F32)).astype(BF)
    saves[0].wait()

    mark("back")
    far_x, far_z = place.off("x", 2), place.off("z", 2)

    def far_terms(t, carry):
        x = jnp.where(t < 4, t, far_x)
        z = jnp.where(t < 4, far_z, lax.rem(far_z + jnp.where(t < 4, 0, t - 3), 4))
        product(bb.at[x, z], x, z, dd, dda, 0, 512)
        return carry

    def near_terms(t, carry):
        x, z = lax.rem(far_x + 1 + lax.div(t, 3), 4), lax.rem(far_z + 1 + lax.rem(t, 3), 4)
        product(bb.at[x, z], x, z, dd, dda, 0, 512)
        return carry

    lax.fori_loop(0, 7, far_terms, 0)
    b_task = plane_sum(comm, bb, bf, bn)
    pump(b_task)
    lax.fori_loop(0, 9, near_terms, 0)
    pump(b_task)
    pump(b_task)

    mark("grads")

    def weight_grads(i):
        def block_rows(y, carry):
            here = pl.ds(pl.multiple_of(512 * y, 512), 512)
            left_n = np_[:, here]
            left_c = jnp.concatenate(
                [jnp.concatenate([gc[y, zl, 0:480, :], gc[y, 2 + zl, 0:480, :]], axis=0) for zl in range(2)], axis=1)
            for j in range(3):
                if j < 2:
                    value = dot(left_n, dd[:, 512 * i + 256 * j:512 * i + 256 * j + 256], 0, 0).astype(BF)
                else:
                    value = dot(left_c, aa[:, 256 * i:256 * i + 256], 0, 0).astype(BF)
                wv[i, y, :, :, :, 256 * j:256 * j + 256] = value.reshape(2, 2, 128, 256)
            return carry
        lax.fori_loop(0, 4, block_rows, 0)

    def act_grads():
        for y in range(4):
            left_n, left_c = na[:, 256 * y:256 * y + 256], ga[:, 256 * y:256 * y + 256]
            for j in range(3):
                value = dot(left_n, dda[:, 256 * j:256 * j + 256], 0, 0) if j < 2 else dot(left_c, aaa[...], 0, 0)
                grad_act[y, :, :, :, 256 * j:256 * j + 256] = value.astype(BF).reshape(2, 2, 64, 256)

    grads = [wv.at[i] for i in range(EARLY)] + [grad_act]
    sums = [wide_sum(comm, grad, s, r.at[0], r.at[1], r.at[2], z, 64 if i == EARLY else 128, False)
            for i, (grad, (s, r, z)) in enumerate(zip(grads, lands))]
    weight_grads(0)
    pump(sums[0])
    weight_grads(1)
    pump(sums[0], sums[1])
    pump(b_task)
    act_grads()
    pump(sums[2])
    pump(b_task)
    pump(sums[1])
    drain(b_task)
    mark("dn2")
    d8[place.x, place.zl] = bb[place.x, place.z]
    d_task = comm.pair_ring_gather("zl", "x", lambda k, j, p: d8.at[k, j, p], PARTS_8,
                                   lambda p: d8.at[place.x, place.zl, p], d8.at[place.x, place.zl], slice(None))
    pump(d_task), pump(d_task)
    pump(sums[0], sums[2])
    weight_grads(2)
    saves.append(comm.local(wv.at[2], out_late[0]))
    pump(d_task)
    pump(sums[1])
    weight_grads(3)
    saves.append(comm.local(wv.at[3], out_late[1]))
    pump(d_task)
    pump(sums[2], sums[0])
    pump(d_task)
    pump(sums[1], sums[2])
    drain(d_task)
    saves.append(comm.local(d8, out_d8))
    mark("sums")
    for task in sums:
        drain(task)
    for grad, (_, _, swap), out in zip(grads, lands, out_s):
        saves.append(comm.local(grad.at[place.y, place.zh, place.core], out.at[place.zh]))
        saves.append(comm.local(swap, out.at[1 - place.zh]))
    for copy in saves[1:]:
        copy.wait()
    mark(None)
    comm.close()


def feed_forward(f, fa, n2p, n2a, cot_pre, cot_act):
    grad = (4, 2, 2, 128, 768)
    outs = [(2, 128, 768)] * EARLY + [(2, 64, 768)] + [grad] * (CH - EARLY) + [(4, 2, T, 256), (4, 4, T, 256), (4, 2, T, 256)]
    vm = lambda *s: pltpu.VMEM(s, BF)
    scratch = [vm(CH, *grad), vm(4, 2, 2, 64, 768), vm(960, 2048), vm(256, 1024), vm(4, 4, T, 256),
               vm(256, 1024), vm(960, 2048), vm(960, 1024), vm(256, 512), vm(256, 256)]
    scratch += [vm(4, 4, T, 256)] + LAND_16 + [vm(4, 2, T, 256), vm(4, 2, 2, 64, 768), vm(T, 256), pltpu.VMEM((64, 256), F32)]
    for n in [128] * EARLY + [64]:
        scratch += [vm(4, 2, n, 768), vm(3, 2, n, 768), vm(n, 768)]
    return pl.pallas_call(
        feed_forward_kernel,
        out_shape=[jax.ShapeDtypeStruct(s, BF) for s in outs],
        in_specs=[ANY] * 4 + [INSIDE] * 2,
        out_specs=[ANY] * len(outs),
        scratch_shapes=scratch + SEM_SCRATCH,
        compiler_params=pltpu.CompilerParams(collective_id=2, has_side_effects=True, vmem_limit_bytes=VMEM_CAP),
        name="feed_forward",
    )(f, fa, n2p, n2a, cot_pre, cot_act)
TS = T + 16
FAR_PEERS = tuple(f"w{step}{flip}" for step, flip in CHIPS if (step, flip) not in ((1, 0), (3, 0), (0, 1)))
KV_PARTS = [(rows(0, 160), 1), (rows(160, 304), -1)]


def attend_back_kernel(lens, d8, h16, c16, r2, r1, g8, qo, qoa, kv, kva, n1p, n1a, qkvo, xb, cot_pre, cot_act, g2, g3, yt, h_own,
                       out_s2, out_s3, out_q, out_qa, out_kv, out_kva, out_x, out_y, out_g,
                       dv8, hv, cv, r2v, r1v, g8v, qov, qoav, kvv, kvav, npv, nav, qv, xv, cotv, g2v, g3v, yv, how,
                       mean, ghp, gha, dhb, dov, dqp, dqa, stat, gains, gsum, gains16, gains2, spare, outx, outy,
                       gq, gkv, gqa, gkva, kvb, blocks, yf, yn, l0, l1, l2, l3, l4, l5, l6, l7, k0, k1, k2, k3,
                       s2, s3, sq, skv, sqa, skva, t2, t3, tq, tkv, tqa, tkva, z2, z3, zq, zkv, zqa, zkva, *sems):
    comm = Comm(*sems)
    place = comm.place
    x, y, zh, zl, core = place.x, place.y, place.zh, place.zl, place.core
    side = pl.ds(2 * zh, 2)
    load = comm.local
    la = [load(d8, dv8), load(h16.at[:, side], hv), load(r2, r2v), load(g8, g8v), load(c16, cv)]
    lb = [load(qo, qov), load(qoa, qoav), load(qkvo, qv)]
    ly = load(yt, yv)
    lg = [load(g2, g2v), load(g3, g3v)]
    lc = [load(kv, kvv), load(kva, kvav), load(n1p, npv), load(n1a, nav), load(xb, xv), load(r1, r1v), load(h_own, how)]
    comm.enter(PEERS + FAR_PEERS)
    late = [wide_sum(comm, g2v, s2, t2.at[0], t2.at[1], t2.at[2], z2, 128, False),
            wide_sum(comm, g3v, s3, t3.at[0], t3.at[1], t3.at[2], z3, 128, False)]
    y_task = plane_sum(comm, yv, yf, yn)
    for i in range(2):
        cotv[240 * i:240 * i + 240, :] = cot_pre[i]
    cotv[480:544, :] = act_rows(cot_act, spare)
    mark("dh")
    for copy in la:
        copy.wait()
    for i in range(2):
        here = pl.ds(240 * i, 240)
        scale = r2v[here, 0:1]
        gain = lambda n: g8v[n // 2, n % 2, 1:2, :]
        grad = lambda n: dv8[n // 2, n % 2, here, :].astype(F32) * gain(n)
        unit = lambda n: hv[n // 2, n % 2, here, :].astype(F32) * scale
        m = sum(jnp.sum(grad(n) * unit(n), axis=1, keepdims=True) for n in range(8)) / 2048
        mean[here, :] = jnp.broadcast_to(m, (240, 128))
        for n in range(8):
            value = cv[n // 2, n % 2, here, :].astype(F32) + scale * (grad(n) - unit(n) * m)
            ghp[here, 256 * n:256 * n + 256] = value.astype(BF)
        here, there, lanes = pl.ds(480, 64), pl.ds(480 + 64 * i, 64), pl.ds(128 * i, 128)
        scale_a = r2v[there, 0:1]
        gain_a = lambda n: g8v[n // 2, n % 2, 2:3, 128:256]
        grad_a = lambda n: dv8[n // 2, n % 2, here, lanes].astype(F32) * gain_a(n)
        unit_a = lambda n: hv[n // 2, n % 2, here, lanes].astype(F32) * scale_a
        m = sum(jnp.sum(grad_a(n) * unit_a(n), axis=1, keepdims=True) for n in range(8)) / 1024
        mean[there, :] = jnp.broadcast_to(m, (64, 128))
        for n in range(8):
            value = cv[n // 2, n % 2, here, lanes].astype(F32) + scale_a * (grad_a(n) - unit_a(n) * m)
            gha[64 * i:64 * i + 64, 128 * n:128 * n + 128] = value.astype(BF)
    ly.wait()
    pump(y_task), pump(y_task)
    lg[0].wait()
    pump(late[0])
    lg[1].wait()
    pump(late[1])
    mark("attnback")
    for copy in lb:
        copy.wait()
    for i in range(2):
        here = pl.ds(240 * i, 240)
        dov[i, 0:240, :] = dot(ghp[here, :], qov[:, :, :, :, 256:512].reshape(2048, 256), 1, 0).astype(BF)
    low = dot(gha[...], qoav[:, :, :, :, 256:512].reshape(1024, 256), 1, 0).astype(BF)
    for i in range(2):
        dov[i, 240:304, :] = low[64 * i:64 * i + 64]
    for i in range(2):
        q, k, v, do = qv[0, i, 0:304, :], qv[1, i], qv[2, i], dov[i]
        probs = soft(q, k, lens[i])
        inner = probs * dot(do, v, 1, 1)
        dscores = (inner - probs * jnp.sum(inner, axis=1, keepdims=True)).astype(BF)
        dq = (dot(dscores, k, 1, 0) * 0.0625).astype(BF)
        dk = (dot(dscores, q, 0, 0) * 0.0625).astype(BF)[0:304]
        dv = dot(probs.astype(BF), do, 0, 0).astype(BF)[0:304]
        for j, value in enumerate((dq, dk, dv)):
            dqp[240 * i:240 * i + 240, 256 * j:256 * j + 256] = value[0:240]
            dqa[64 * i:64 * i + 64, 256 * j:256 * j + 256] = value[240:304]
        total = dq.astype(F32) * q.astype(F32) + dk.astype(F32) * k[0:304].astype(F32) + dv.astype(F32) * v[0:304].astype(F32)
        total = jnp.broadcast_to(jnp.sum(total, axis=1, keepdims=True), (304, 128))
        stat[240 * i:240 * i + 240, :] = total[0:240]
        stat[480 + 64 * i:544 + 64 * i, :] = total[240:304]
    stat[608:640, :] = jnp.zeros((32, 128), F32)
    line = stat[...].T[0:1]
    line = jnp.concatenate([line[:, 0:256], line[:, 256:512], jnp.concatenate([line[:, 512:640], jnp.zeros((1, 128), F32)], axis=1),
                            jnp.zeros((13, 256), F32)], axis=0).astype(BF)
    for n in range(8):
        blocks[n // 2, n % 2, T:TS, :] = line
    lane = lax.broadcasted_iota(jnp.int32, (512, 128), 1)
    col = lax.broadcasted_iota(jnp.int32, (512, 128), 0)
    kv_sum = block_sum(comm, kvb, (k0, k1, k2), k3, KV_PARTS)
    for n in range(8):
        total = []
        for i in range(2):
            at = lane - 64 * i
            pick = ((at >= 0) & (at < 32) & (col == 32 * n + at)) | ((at >= 32) & (at < 64) & (col == 224 + 32 * n + at))
            pick = pick.astype(F32).astype(BF)
            total.append((dot(dqp[240 * i:240 * i + 240, 256:768], pick, 1, 0), dot(dqa[64 * i:64 * i + 64, 256:768], pick, 1, 0)))
        kvb[n // 2, n % 2, 0:240, :] = (total[0][0] + total[1][0]).astype(BF)
        kvb[n // 2, n % 2, 240:304, :] = (total[0][1] + total[1][1]).astype(BF)
    pump(late[0])
    pump(kv_sum)
    for copy in lc:
        copy.wait()
    mark("terms")

    def terms(step):
        k = place.off("x", step)
        for j in range(2):
            weight = jnp.concatenate([qov[k, j, :, :, 0:256].reshape(256, 256), kvv[k, j].reshape(256, 512)], axis=1)
            blocks[k, j, 0:480, :] = dot(dqp[...], weight, 1, 1).astype(BF)
            weight = jnp.concatenate([qoav[k, j, :, :, 0:256].reshape(128, 256), kvav[k, j].reshape(128, 512)], axis=1)
            small = dot(dqa[...], weight, 1, 1).astype(BF)
            for i in range(2):
                blocks[k, j, 480:544, 128 * i:128 * i + 128] = small[64 * i:64 * i + 64]

    def outer(grad, n, left, right, lo, width):
        def block_rows(k, carry):
            here = pl.ds(pl.multiple_of(4 * n * k, 4 * n), 4 * n)
            value = dot(left[:, here], right, 0, 0).astype(BF)
            grad[k, :, :, :, lo:lo + width] = value.reshape(2, 2, n, width)
            return carry
        lax.fori_loop(0, 4, block_rows, 0)

    terms(2)
    sum_task = block_sum_both(comm, blocks, (l0, l1, l2, l3, l4, l5, l6, l7), TS)
    pump(sum_task)
    pump(late[1])
    terms(1), terms(3), terms(0)
    pump(sum_task)
    mark("attngrads")
    o_act = jnp.concatenate([qv[3, 0, 240:304, :], qv[3, 1, 240:304, :]], axis=0)
    o_pre = jnp.concatenate([qv[3, 0, 0:240, :], qv[3, 1, 0:240, :]], axis=0)
    outer(gq, 128, ghp, o_pre, 256, 256)
    outer(gqa, 64, gha, o_act, 256, 256)
    outer(gq, 128, npv, dqp[:, 0:256], 0, 256)
    outer(gqa, 64, nav, dqa[:, 0:256], 0, 256)
    q_tasks = [wide_sum(comm, gq, sq, tq.at[0], tq.at[1], tq.at[2], zq, 128, True),
               wide_sum(comm, gqa, sqa, tqa.at[0], tqa.at[1], tqa.at[2], zqa, 64, True)]
    kv_tasks = [wide_sum(comm, gkv, skv, tkv.at[0], tkv.at[1], tkv.at[2], zkv, 128, True),
                wide_sum(comm, gkva, skva, tkva.at[0], tkva.at[1], tkva.at[2], zkva, 64, True)]
    pump(*q_tasks)
    pump(kv_sum)
    pump(y_task)
    pump(late[0])
    pump(*q_tasks)
    pump(sum_task)
    pump(sum_task)
    pump(kv_sum)
    pump(late[1])
    pump(late[0])
    drain(kv_sum)
    own = kvb[x, zl]
    share = []
    for i in range(2):
        lane = lax.broadcasted_iota(jnp.int32, (128, 128), 0)
        col = lax.broadcasted_iota(jnp.int32, (128, 128), 1)
        pick = ((col < 64) & (lane == col + 64 * i)).astype(F32).astype(BF)
        share.append(dot(own, pick, 1, 0).astype(BF))
    outer(gkv, 128, npv, jnp.concatenate([share[0][0:240], share[1][0:240]], axis=0), 0, 128)
    outer(gkva, 64, nav, jnp.concatenate([share[0][240:304], share[1][240:304]], axis=0), 0, 128)
    pump(*kv_tasks)
    mark("late")
    pump(y_task)
    pump(sum_task)
    pump(*q_tasks)
    pump(*kv_tasks)
    pump(y_task)
    drain(sum_task)
    mark("dx")
    g_pre, g_act = g8v[x, zl, 0:1, :], g8v[x, zl, 2:3, 0:128]
    f_pre, f_act = g8v[x, zl, 1:2, :], g8v[x, zl, 2:3, 128:256]
    line = blocks[x, zl, T:TS, :].astype(F32)
    line = jnp.concatenate([line[0:1], line[1:2], line[2:3, 0:128]], axis=1)
    stat[...] = jnp.broadcast_to(line, (128, 640)).T

    def own_norm(here, there, lanes, gain_f, gain_a, width):
        s2_, s1_ = r2v[there, 0:1], r1v[there, 0:1]
        back, unit = dv8[x, zl, here, lanes].astype(F32), hv[x, zl, here, lanes].astype(F32) * s2_
        dh = cotv[here, lanes] + s2_ * (back * gain_f - unit * mean[there, 0:1])
        gain_f_grad = jnp.sum(back * unit, axis=0, keepdims=True)
        back, unit = blocks[x, zl, here, lanes].astype(F32), xv[here, lanes].astype(F32) * s1_
        outx[here, lanes] = dh + s1_ * (back * gain_a - unit * (stat[there, 0:1] / width))
        return jnp.sum(back * unit, axis=0, keepdims=True), gain_f_grad

    pre = [own_norm(pl.ds(240 * i, 240), pl.ds(240 * i, 240), pl.ds(0, 256), f_pre, g_pre, 2048) for i in range(2)]
    act = [own_norm(pl.ds(480, 64), pl.ds(480 + 64 * i, 64), pl.ds(128 * i, 128), f_act, g_act, 1024) for i in range(2)]
    gains[...] = jnp.concatenate(
        [pre[0][0] + pre[1][0], pre[0][1] + pre[1][1],
         jnp.concatenate([act[0][0] + act[1][0], act[0][1] + act[1][1]], axis=1), jnp.zeros((5, 256), F32)], axis=0)
    saves = [load(outx, out_x)]
    g_task = small_total(comm, gains16, gains2, gains, gsum)
    pump(g_task)
    mark("tail")
    pump(*q_tasks)
    pump(*kv_tasks)
    pump(late[1])
    drain(y_task)
    outy[...] = (yv[x, place.z].astype(F32) + how[...]).astype(BF)
    saves.append(load(outy, out_y))
    pump(*q_tasks)
    pump(*kv_tasks)
    pump(g_task)
    for task in q_tasks + kv_tasks + late:
        drain(task)
    drain(g_task)
    saves += [load(gsum, out_g), load(gkv.at[y, zh, core], out_kv), load(gkva.at[y, zh, core], out_kva), load(gq.at[y, zh, core], out_q), load(gqa.at[y, zh, core], out_qa)]
    saves += [load(g2v.at[y, zh, core], out_s2.at[zh]), load(z2, out_s2.at[1 - zh])]
    saves += [load(g3v.at[y, zh, core], out_s3.at[zh]), load(z3, out_s3.at[1 - zh])]
    for copy in saves:
        copy.wait()
    mark(None)
    comm.close()


def attend_back(lens, *args):
    outs = [((2, 128, 768), BF), ((2, 128, 768), BF), ((128, 512), BF), ((64, 512), BF), ((128, 128), BF), ((64, 128), BF), ((T, 256), F32),
            ((T, 256), BF), ((8, 256), F32)]
    vm = lambda *s: pltpu.VMEM(s, BF)
    vf = lambda *s: pltpu.VMEM(s, F32)
    wide = lambda n, c: (4, 2, 2, n, c)
    back = [(128, 768), (128, 768), (128, 512), (128, 128), (64, 512), (64, 128)]
    scratch = [vm(4, 2, T, 256), vm(4, 2, T, 256), vm(4, 2, T, 256), vf(608, 128), vf(608, 128), vf(4, 2, 8, 256),
               vm(4, 2, 2, 128, 512), vm(4, 2, 2, 64, 512), vm(4, 2, 2, 128, 512), vm(4, 2, 2, 64, 512),
               vm(480, 2048), vm(128, 1024), vm(4, 2, KEYS, 256), vm(T, 256), vf(T, 256), vm(*wide(128, 768)),
               vm(*wide(128, 768)), vm(4, 4, T, 256), vf(T, 256)]
    scratch += [vf(608, 128), vm(480, 2048), vm(128, 1024), vf(8, 128), vm(2, 304, 256), vm(480, 768), vm(128, 768),
                vf(640, 128), vf(8, 256), vf(8, 256), vf(8, 8, 256), vf(2, 8, 256), vf(64, 256), vf(T, 256), vm(T, 256)]
    scratch += [vm(*wide(n, c)) for n, c in back[2:]]
    scratch += [vm(4, 2, 304, 128), vm(4, 2, TS, 256)] + LAND_16 + block_lands(TS) + [vm(2, 304, 128)] * 3 + [vm(304, 128)]
    scratch += [vm(4, 2, n, c) for n, c in back] + [vm(3, 2, n, c) for n, c in back] + [vm(n, c) for n, c in back]
    return pl.pallas_call(
        attend_back_kernel,
        out_shape=[jax.ShapeDtypeStruct(s, d) for s, d in outs],
        in_specs=[pl.BlockSpec(memory_space=pltpu.SMEM)] + [ANY] * 14 + [INSIDE] * 2 + [ANY] * (len(args) - 16),
        out_specs=[ANY] * len(outs),
        scratch_shapes=scratch + SEM_SCRATCH,
        compiler_params=pltpu.CompilerParams(collective_id=3, has_side_effects=True, vmem_limit_bytes=VMEM_CAP),
        name="attend_back",
    )(lens, *args)
def result_kernel(s0, s1, s2, s3, sa, sq, sqa, skv, skva, y, gx, gains,
                  y_pre, y_act, x_pre, x_act, attn_gain_pre, query_pre, key_pre, value_pre, out_pre, ffn_gain_pre, gate_pre,
                  up_pre, down_pre, attn_gain_act, query_act, key_act, value_act, out_act, ffn_gain_act, gate_act, up_act,
                  down_act):
    for i in range(2):
        here, lanes = slice(240 * i, 240 * i + 240), slice(128 * i, 128 * i + 128)
        y_pre[i], x_pre[i] = y[here, :], gx[here, :]
        x_act[:, i, :] = gx[480:530, lanes]
    low = y[480:544, :].astype(F32)[0:50]
    y_act[...] = jnp.stack([low[:, 0:128], low[:, 128:256]], axis=1).astype(BF)
    attn_gain_pre[...], ffn_gain_pre[...] = gains[0:1, :], gains[1:2, :]
    attn_gain_act[...], ffn_gain_act[...] = gains[2:3, 0:128], gains[2:3, 128:256]
    for q, kv, query, key, value in ((sq, skv, query_pre, key_pre, value_pre),
                                     (sqa, skva, query_act, key_act, value_act)):
        query[...] = q[:, 0:256].astype(F32)
        both = kv[...].astype(F32).T
        key[...], value[...] = both[0:32], both[32:64]
    out_pre[...], out_act[...] = sq[:, 256:512].astype(F32).T, sqa[:, 256:512].astype(F32)
    for h in range(2):
        for i, s in enumerate((s0, s1, s2, s3)):
            here = slice(1024 * h + 256 * i, 1024 * h + 256 * i + 256)
            gate_pre[:, here], up_pre[:, here] = s[h, :, 0:256].astype(F32), s[h, :, 256:512].astype(F32)
            down_pre[here, :] = s[h, :, 512:768].astype(F32).T
        here = slice(256 * h, 256 * h + 256)
        gate_act[:, here], up_act[:, here] = sa[h, :, 0:256].astype(F32), sa[h, :, 256:512].astype(F32)
        down_act[:, here] = sa[h, :, 512:768].astype(F32)


def results(*args):
    tokens = lambda d: [((2, 240, 256), d), ((50, 2, 128), d)]
    expert = lambda n, h, out, down: [((1, n * 2), F32), ((n, 256), F32), ((32, n), F32), ((32, n), F32), (out, F32),
                                      ((1, n * 2), F32), ((n, h), F32), ((n, h), F32), (down, F32)]
    shapes = tokens(BF) + tokens(F32) + expert(128, 2048, (256, 128), (2048, 128)) + expert(64, 512, (64, 256), (64, 512))
    return pl.pallas_call(
        result_kernel,
        out_shape=[jax.ShapeDtypeStruct(s, d) for s, d in shapes],
        in_specs=[INSIDE] * len(args),
        out_specs=[INSIDE] * len(shapes),
        compiler_params=pltpu.CompilerParams(vmem_limit_bytes=VMEM_CAP),
        name="results",
    )(*args)


def local(x_pre, x_act, lengths, cot_pre, cot_act, attn_gain_pre, query_pre, key_pre, value_pre, out_pre, ffn_gain_pre,
          gate_pre, up_pre, down_pre, attn_gain_act, query_act, key_act, value_act, out_act, ffn_gain_act, gate_act,
          up_act, down_act):
    line = lambda gain: gain.reshape(1, -1)
    x_act, cot_act = x_act.transpose(1, 0, 2), cot_act.transpose(1, 0, 2)
    key_pre, value_pre, key_act, value_act, out_act, down_act = (
        m.T for m in (key_pre, value_pre, key_act, value_act, out_act, down_act))
    (xb, f, fa, qo, qoa, kv, kva, g8, n1p, n1a, qkvo, r1, h_own, h16, n2p, n2a, r2) = attend(
        lengths, x_pre, x_act, line(attn_gain_pre), query_pre, key_pre, value_pre, out_pre, line(ffn_gain_pre), gate_pre,
        up_pre, down_pre, line(attn_gain_act), query_act, key_act, value_act, out_act, line(ffn_gain_act), gate_act, up_act,
        down_act)
    s0, s1, sa, g2, g3, d8, yt, c8 = feed_forward(f, fa, n2p, n2a, cot_pre, cot_act)
    s2, s3, sq, sqa, skv, skva, gx, y, gains = attend_back(
        lengths, d8, h16, c8, r2, r1, g8, qo, qoa, kv, kva, n1p, n1a, qkvo, xb, cot_pre, cot_act, g2, g3, yt, h_own)
    outs = results(s0, s1, s2, s3, sa, sq, sqa, skv, skva, y, gx, gains)
    turn = lambda i, o: o.transpose(1, 0, 2) if i in (1, 3) else o.T if i in (6, 7, 15, 16, 17, 21) else o
    return tuple(o.reshape(-1) if o.shape[0] == 1 else turn(i, o) for i, o in enumerate(outs))


def solution(mesh):
    tok, row, col, vec = P("wide", None, "narrow"), P("wide", "narrow"), P("narrow", "wide"), P("narrow")
    expert = (vec, row, row, row, col, vec, row, row, col)
    return jax.shard_map(
        local, mesh=mesh, in_specs=(tok, tok, P("wide"), tok, tok) + expert + expert,
        out_specs=(tok,) * 4 + expert + expert, check_vma=False)
```

```python
import functools
import jax
import jax.numpy as jnp
from jax import lax
from jax.experimental import pallas as pl
from jax.experimental.pallas import tpu as pltpu
from jax.sharding import PartitionSpec as P

MESH = pl.DeviceIdType.MESH
BF = jnp.bfloat16
F32 = jnp.float32
SEMS = 256
LOCAL_SEMS = 48
VMEM_CAP = 62 * 1024 * 1024


class Place:
    def __init__(self):
        wide, narrow = lax.axis_index("wide"), lax.axis_index("narrow")
        self.core = lax.rem(wide, 2)
        self.zh = lax.rem(lax.div(wide, 2), 2)
        self.y = lax.div(wide, 4)
        self.zl = lax.rem(narrow, 2)
        self.x = lax.div(narrow, 2)
        self.z = self.zh * 2 + self.zl

    def wide_at(self, y, zh, core):
        return (y * 2 + zh) * 2 + core

    def coord(self, axis):
        return {"x": self.x, "y": self.y, "z": self.z}[axis]

    def off(self, axis, step):
        return lax.rem(self.coord(axis) + step + 4, 4)

    def peer(self, name):
        if name == "sib":
            return {"wide": self.wide_at(self.y, self.zh, 1 - self.core)}
        if name == "z2":
            return {"wide": self.wide_at(self.y, 1 - self.zh, self.core)}
        if name == "zl":
            return {"narrow": self.x * 2 + 1 - self.zl}
        if name[0] == "w":
            step, flip = int(name[1]), int(name[2])
            zh = 1 - self.zh if flip else self.zh
            return {"wide": self.wide_at(self.off("y", step), zh, self.core)}
        if name[0] == "n":
            zl = 1 - self.zl if int(name[2]) else self.zl
            return {"narrow": self.off("x", int(name[1])) * 2 + zl}
        axis, step = name[0], 1 if name[1] == "+" else -1
        at = self.off(axis, step)
        if axis == "y":
            return {"wide": self.wide_at(at, self.zh, self.core)}
        if axis == "x":
            return {"narrow": at * 2 + self.zl}
        return {"wide": self.wide_at(self.y, lax.div(at, 2), self.core), "narrow": self.x * 2 + lax.rem(at, 2)}


class Link:
    def __init__(self, out, into):
        self.out, self.into = out, into

    def arrive(self):
        self.into.wait_recv()

    def left(self):
        self.out.wait_send()


class Comm:
    def __init__(self, send_sems, recv_sems, local_sems):
        self.place = Place()
        self.send_sems, self.recv_sems, self.local_sems = send_sems, recv_sems, local_sems
        self.count, self.local_count = 0, 0
        self.links = []

    def greet(self, peers):
        for name in peers:
            pl.semaphore_signal(
                pltpu.get_barrier_semaphore(), inc=1, device_id=self.place.peer(name), device_id_type=MESH)

    def enter(self, peers):
        pl.semaphore_wait(pltpu.get_barrier_semaphore(), len(peers))

    def send(self, src, dst, name, incoming):
        index = self.count
        self.count += 1
        assert index < SEMS
        make = lambda to: pltpu.make_async_remote_copy(
            src_ref=src, dst_ref=to, send_sem=self.send_sems.at[index], recv_sem=self.recv_sems.at[index],
            device_id=self.place.peer(name), device_id_type=MESH)
        out = make(dst)
        out.start()
        link = Link(out, make(incoming))
        self.links.append(link)
        return link

    def local(self, src, dst):
        index = self.local_count
        self.local_count += 1
        assert index < LOCAL_SEMS
        copy = pltpu.make_async_copy(src, dst, self.local_sems.at[index])
        copy.start()
        return copy

    def settle(self):
        for link in self.links:
            link.left()
        self.links = []

    def close(self):
        self.settle()

    def ring_gather(self, axis, view, parts, own=None, staged=False):
        place = self.place
        at = lambda step: place.off(axis, step)
        src = own if own is not None else (lambda part: view(at(0), part))
        up_first = sorted(parts, key=lambda part: -part[1])
        plus = [(way, p, self.send(src(p), view(at(0), p), axis + "+", view(at(-1), p))) for p, way in up_first]
        minus = [(way, p, self.send(src(p), view(at(0), p), axis + "-", view(at(1), p))) for p, way in up_first[::-1]]
        yield
        rest = []
        for way, p, link in plus:
            if way > 0:
                link.arrive()
                rest.append(self.send(view(at(-1), p), view(at(-1), p), axis + "+", view(at(-2), p)))
        for way, p, link in minus:
            if way < 0:
                link.arrive()
                rest.append(self.send(view(at(1), p), view(at(1), p), axis + "-", view(at(2), p)))
        yield
        for way, p, link in plus:
            if way < 0:
                link.arrive()
        for way, p, link in minus:
            if way > 0:
                link.arrive()
        if staged:
            yield
        for link in rest:
            link.arrive()

    def pair_ring_gather(self, pair, axis, view, parts, own, give, whole, swap_first=False):
        place = self.place
        mine = {"z2": place.zh, "zl": place.zl}[pair]
        here = place.coord(axis)
        first = self.ring_gather(axis, lambda k, p: view(k, mine, p), parts, own)
        if not swap_first:
            next(first)
            yield
        swap = self.send(give, view(here, mine, whole), pair, view(here, 1 - mine, whole))
        yield
        if swap_first:
            next(first)
            yield
        next(first)
        yield
        swap.arrive()
        second = self.ring_gather(axis, lambda k, p: view(k, 1 - mine, p), parts)
        next(second)
        yield
        next(second)
        yield
        drain(first)
        drain(second)

    def plane_gather(self, view, parts_x, parts_z, own=None, ready=None):
        place = self.place
        ax = self.ring_gather("x", lambda k, p: view(k, place.z, p), parts_x, own, True)
        bz = self.ring_gather("z", lambda k, p: view(place.x, k, p), parts_z, own, True)
        onward = lambda step: [
            self.ring_gather("z", lambda k, p: view(place.off("x", step), k, p), parts_x),
            self.ring_gather("x", lambda k, p: view(k, place.off("z", step), p), parts_z)]
        next(ax), next(bz)
        yield
        next(ax), next(bz)
        next(ax)
        if ready is not None:
            ready()
        close = [onward(step) for step in (0, 1, -1)]
        for az, _ in close:
            next(az)
        next(bz)
        for _, bx in close:
            next(bx)
        yield
        drain(ax)
        last = onward(2)
        next(last[0])
        drain(bz)
        next(last[1])
        yield
        for az, bx in close:
            next(az), next(bx)
        yield
        next(last[0]), next(last[1])
        yield
        for az, bx in close + [last]:
            drain(az), drain(bx)

    def ring_sum(self, axis, view, parts, relay, plus, minus, split=False):
        place = self.place
        at = lambda step: place.off(axis, step)
        near = {1: lambda p: self.send(view(at(1), p), plus(p), axis + "+", plus(p)),
                -1: lambda p: self.send(view(at(-1), p), minus(p), axis + "-", minus(p))}
        far = [(p, way, self.send(view(at(2), p), relay(p), axis + ("+" if way > 0 else "-"), relay(p))) for p, way in parts]
        if split:
            yield
        links = [near[-way](p) for p, way in parts]
        yield
        for p, way, link in far:
            link.arrive()
            add_to(view(at(way), p), relay(p))
            links.append(near[way](p))
        yield
        for link in links:
            link.arrive()
        for p, _ in parts:
            add_to(view(at(0), p), plus(p), minus(p))


def add_to(ref, *others):
    total = ref[...].astype(F32)
    for other in others:
        total = total + other[...].astype(F32)
    ref[...] = total.astype(ref.dtype)


def drain(task):
    for _ in task:
        pass


def rows(lo, hi):
    return pl.ds(lo, hi - lo)
T = 544
CH = 4


def halves(n):
    return [(rows(0, n // 2), 1), (rows(n // 2, n), -1)]


PARTS_8 = [(rows(0, 272), 1), (rows(272, 544), -1)]
PARTS_A = [(rows(0, 144), 1), (rows(144, 272), -1)]
PARTS_B = [(rows(272, 416), 1), (rows(416, 544), -1)]
PEERS = ("y+", "y-", "z2", "sib", "x+", "x-", "z+", "z-")


def wide_gather(comm, out, own, give, n, parts=None, swap_first=False):
    place = comm.place
    core = place.core
    copy = comm.local(own, out.at[place.y, place.zh, core])
    task = comm.pair_ring_gather(
        "z2", "y", lambda k, j, p: out.at[k, j, core, p], parts or halves(n),
        lambda p: own.at[p], give, slice(None), swap_first)
    yield from task
    copy.wait()
    link = comm.send(out.at[:, :, core], out.at[:, :, core], "sib", out.at[:, :, 1 - core])
    yield
    link.arrive()


def block_gather(comm, out, own, parts):
    place = comm.place
    copy = comm.local(own, out.at[place.x, place.zl])
    yield from comm.pair_ring_gather(
        "zl", "x", lambda k, j, p: out.at[k, j, p], parts, lambda p: own.at[p], own, slice(None))
    copy.wait()


STEPS = [(step, flip) for flip in range(2) for step in range(4) if step or flip]


def small_gather(comm, out, own):
    place = comm.place
    copy = comm.local(own, out.at[place.x, place.zl])
    links = []
    for step, flip in STEPS:
        back = out.at[place.off("x", -step), 1 - place.zl if flip else place.zl]
        links.append(comm.send(own, out.at[place.x, place.zl], f"n{step}{flip}", back))
    yield
    copy.wait()
    for link in links:
        link.arrive()


def plane_spread(comm, out, own):
    place = comm.place
    copy = comm.local(own, out.at[place.x, place.z])
    yield from comm.plane_gather(lambda k, j, p: out.at[k, j, p], PARTS_A, PARTS_B, lambda p: own.at[p], copy.wait)


def block_sum(comm, blocks, lands, swap, parts, z=None):
    place = comm.place
    relay, plus, minus = lands
    upto = pl.ds(0, sum(p.size for p, _ in parts))
    xs = comm.ring_sum(
        "x", lambda k, p: blocks.at[k, :, p], parts,
        lambda p: relay.at[:, p], lambda p: plus.at[:, p], lambda p: minus.at[:, p], z is not None)
    next(xs)
    yield
    if z is not None:
        z_rows, z_parts, z_land, z_lands = z
        next(xs)
        link = comm.send(blocks.at[:, 1 - place.zl, z_rows], z_land, "zl", z_land)
        yield
    next(xs)
    yield
    if z is not None:
        link.arrive()
        add_to(blocks.at[:, place.zl, z_rows], z_land)
        zs = comm.ring_sum("x", lambda k, p: blocks.at[k, place.zl, p], z_parts,
                           *[(lambda p, land=land: land.at[pl.ds(p.start - z_rows.start, p.size)]) for land in z_lands])
        next(zs)
        yield
    drain(xs)
    last = comm.send(blocks.at[place.x, 1 - place.zl, upto], swap, "zl", swap)
    if z is not None:
        next(zs)
    yield
    last.arrive()
    add_to(blocks.at[place.x, place.zl, upto], swap)
    if z is not None:
        drain(zs)


def plane_sum(comm, blocks, lands_far, lands_near):
    place = comm.place
    az = comm.ring_sum("z", lambda k, p: blocks.at[:, k, p], PARTS_A,
                       lambda p: lands_far.at[0, :, p], lambda p: lands_far.at[1, :, p], lambda p: lands_far.at[2, :, p], True)
    bx = comm.ring_sum("x", lambda k, p: blocks.at[k, :, p], PARTS_B,
                       lambda p: lands_far.at[0, :, p], lambda p: lands_far.at[1, :, p], lambda p: lands_far.at[2, :, p], True)
    for _ in range(3):
        next(az), next(bx)
        yield
    drain(az)
    ax = comm.ring_sum("x", lambda k, p: blocks.at[k, place.z, p], PARTS_A,
                       lambda p: lands_near.at[0, p], lambda p: lands_near.at[1, p], lambda p: lands_near.at[2, p])
    next(ax)
    drain(bx)
    bz = comm.ring_sum("z", lambda k, p: blocks.at[place.x, k, p], PARTS_B,
                       lambda p: lands_near.at[0, p], lambda p: lands_near.at[1, p], lambda p: lands_near.at[2, p])
    next(bz)
    yield
    next(ax), next(bz)
    yield
    drain(ax), drain(bz)


CHIPS = [(step, flip) for flip in range(2) for step in range(4) if step or flip]


def small_total(comm, slots, pair, own, out):
    place = comm.place
    mine = place.y * 2 + place.zh
    links = []
    for step, flip in CHIPS:
        back = place.off("y", -step) * 2 + (1 - place.zh if flip else place.zh)
        links.append(comm.send(own, slots.at[mine], f"w{step}{flip}", slots.at[back]))
    slots[mine] = own[...]
    yield
    for link in links:
        link.arrive()
    pair[0] = sum(slots[i] for i in range(8))
    link = comm.send(pair.at[0], pair.at[1], "sib", pair.at[1])
    yield
    link.arrive()
    out[...] = pair[0] + pair[1]


def wide_sum(comm, grad, half, relay, plus, minus, swap, n, add):
    place = comm.place
    core, zh = place.core, place.zh
    link = comm.send(grad.at[:, :, 1 - core], half, "sib", half)
    yield
    link.arrive()
    def fold(k, carry):
        add_to(grad.at[k, :, core], half.at[k])
        return carry
    lax.fori_loop(0, 4, fold, 0)
    yield from comm.ring_sum(
        "y", lambda k, p: grad.at[k, :, core, p], halves(n),
        lambda p: relay.at[:, p], lambda p: plus.at[:, p], lambda p: minus.at[:, p])
    link = comm.send(grad.at[place.y, 1 - zh, core], swap, "z2", swap)
    yield
    link.arrive()
    if add:
        add_to(grad.at[place.y, zh, core], swap)


SEM_SCRATCH = [pltpu.SemaphoreType.DMA((SEMS,)), pltpu.SemaphoreType.DMA((SEMS,)), pltpu.SemaphoreType.DMA((LOCAL_SEMS,))]
ANY = pl.BlockSpec(memory_space=pl.ANY)
INSIDE = pl.BlockSpec(memory_space=pltpu.VMEM)


X_ROWS = 400
X_PARTS = [(rows(0, 208), 1), (rows(208, 400), -1)]


def block_lands(count):
    z = count - X_ROWS
    return ([pltpu.VMEM((2, X_ROWS, 256), BF)] * 3 + [pltpu.VMEM((X_ROWS, 256), BF), pltpu.VMEM((4, z, 256), BF)]
            + [pltpu.VMEM((z, 256), BF)] * 3)


def block_sum_both(comm, blocks, lands, count):
    z = (rows(X_ROWS, count), [(rows(X_ROWS, 480), 1), (rows(480, count), -1)], lands[4], lands[5:8])
    return block_sum(comm, blocks, lands[0:3], lands[3], X_PARTS, z)


LAND_16 = [pltpu.VMEM((3, 4, T, 256), BF), pltpu.VMEM((3, T, 256), BF)]


EPSILON = 1e-06
MASKED = -1000000000.0
KEYS = 384


def dot(a, b, ca, cb):
    return lax.dot_general(a, b, (((ca,), (cb,)), ((), ())), preferred_element_type=F32)


_open = []


def mark(name):
    if _open:
        _open.pop().__exit__(None, None, None)
    if name:
        scope = jax.named_scope(name)
        scope.__enter__()
        _open.append(scope)


def pump(*tasks):
    for task in tasks:
        next(task, None)


def seen(length):
    s = lax.broadcasted_iota(jnp.int32, (304, KEYS), 0)
    t = lax.broadcasted_iota(jnp.int32, (304, KEYS), 1)
    live = (t < 192) | ((t >= 240) & (t < 290)) | ((t < 240) & (t - 192 < length))
    return live & ((t < 240) | (s >= 240))


def soft(q, k, length):
    scores = dot(q, k, 1, 1) * 0.0625
    scores = jnp.where(seen(length), scores, MASKED)
    weights = jnp.exp(scores - jnp.max(scores, axis=1, keepdims=True))
    return weights / jnp.sum(weights, axis=1, keepdims=True)


def pairs8():
    return [(x, zl) for x in range(4) for zl in range(2)]


def norm_block_rows(get, gain, width, put):
    total = sum(jnp.sum(get(n) * get(n), axis=1, keepdims=True) for n in range(8))
    scale = lax.rsqrt(total / (8 * width) + EPSILON)
    for n in range(8):
        put(n, (get(n) * scale * gain(n)).astype(BF))
    return scale


def act_rows(act, spare):
    spare[...] = jnp.zeros((64, 256), F32)
    rows_of = act[...].astype(F32)
    for i in range(2):
        spare[0:50, 128 * i:128 * i + 128] = rows_of[:, i, :]
    return spare[...]


def turned(m):
    return m.astype(F32).T.astype(BF)


def attend_kernel(lens, x_pre, x_act, attn_gain_pre, query_pre, key_pre, value_pre, out_pre, ffn_gain_pre, gate_pre, up_pre,
                  down_pre, attn_gain_act, query_act, key_act, value_act, out_act, ffn_gain_act, gate_act, up_act, down_act,
                  out_xb, out_f, out_fa, out_q, out_qa, out_kv, out_kva, out_g, out_n1p, out_n1a, out_qkvo, out_r1,
                  out_h, out_h16, out_n2p, out_n2a, out_r2,
                  kv8, kvf, qo, qoa, kv, kva, x8, g8, n1p, n1a, qkvo, r1, xv, hv, full, n2p, n2a, r2,
                  blocks, l0, l1, l2, l3, l4, l5, l6, l7, wf, wfa, wq, wqa, kvs, gb, spare, *sems):
    comm = Comm(*sems)
    comm.greet(PEERS + ("n20", "n11", "n21", "n31"))
    place = comm.place
    zh = place.zh
    for i in range(2):
        xv[240 * i:240 * i + 240, :] = x_pre[i]
    xv[480:544, :] = act_rows(x_act, spare).astype(BF)
    lane = lax.broadcasted_iota(jnp.int32, (32, 128), 1)
    row = lax.broadcasted_iota(jnp.int32, (32, 128), 0)
    spread = [(lane == row + 32 * j).astype(F32).astype(BF) for j in range(4)]
    for base, half, key, value in ((0, 64, key_pre, value_pre), (64, 32, key_act, value_act)):
        kvs[base:base + half, :] = (
            dot(key[:, 0:half], spread[0], 0, 0) + dot(value[:, 0:half], spread[1], 0, 0)
            + dot(key[:, half:2 * half], spread[2], 0, 0) + dot(value[:, half:2 * half], spread[3], 0, 0)).astype(BF)
    gb[...] = jnp.concatenate([attn_gain_pre[...], ffn_gain_pre[...],
                               jnp.concatenate([attn_gain_act[...], ffn_gain_act[...]], axis=1), jnp.zeros((5, 256), F32)], axis=0)
    wq[:, 0:256], wqa[:, 0:256] = query_pre[...], query_act[...]
    wq[:, 256:512], wqa[:, 256:512] = turned(out_pre[...]), out_act[...]
    zero = jnp.zeros((KEYS - 304, 256), BF)
    for i in range(2):
        for j in (1, 2):
            qkvo[j, i, 304:KEYS, :] = zero
    comm.enter(PEERS + ("n20", "n11", "n21", "n31"))

    mark('start')
    kv_task = small_gather(comm, kv8, kvs)
    g_task = small_gather(comm, g8, gb)
    x_task = block_gather(comm, x8, xv, PARTS_8)
    q_tasks = [wide_gather(comm, qo, wq, wq, 128), wide_gather(comm, qoa, wqa, wqa, 64)]
    f_tasks = [wide_gather(comm, out_f.at[i], wf.at[zh, i], wf.at[1 - zh, i], 128, None, True) for i in range(CH)]
    f_tasks.append(wide_gather(comm, out_fa, wfa.at[zh], wfa.at[1 - zh], 64, None, True))
    pump(kv_task)
    pump(g_task)
    pump(x_task), pump(x_task)
    pump(*q_tasks), pump(*q_tasks)
    for h in range(2):
        for i in range(CH):
            here = slice(1024 * h + 256 * i, 1024 * h + 256 * i + 256)
            wf[h, i, :, 0:256], wf[h, i, :, 256:512] = gate_pre[:, here], up_pre[:, here]
            wf[h, i, :, 512:768] = turned(down_pre[here, :])
        here = slice(256 * h, 256 * h + 256)
        wfa[h, :, 0:256], wfa[h, :, 256:512] = gate_act[:, here], up_act[:, here]
        wfa[h, :, 512:768] = down_act[:, here]
    drain(kv_task)
    lane = lax.broadcasted_iota(jnp.int32, (128, 512), 0)
    col = lax.broadcasted_iota(jnp.int32, (128, 512), 1)
    for side in range(2):
        total = jnp.zeros((96, 512), F32)
        at = lane - 64 * side
        for n in range(8):
            pick = ((at >= 0) & (at < 32) & (col == 32 * n + at)) | ((at >= 32) & (at < 64) & (col == 224 + 32 * n + at))
            total = total + dot(kv8[n // 2, n % 2], pick.astype(F32).astype(BF), 1, 0)
        kvf[64 * side:64 * side + 64, :] = total[0:64].astype(BF)
        kvf[128 + 32 * side:160 + 32 * side, :] = total[64:96].astype(BF)
    kv_a, kv_b = kvf.at[0:128], kvf.at[128:192]
    kv_tasks = [wide_gather(comm, kv, kv_a, kv_a, 128), wide_gather(comm, kva, kv_b, kv_b, 64)]
    pump(*kv_tasks), pump(*kv_tasks)
    pump(x_task)
    pump(x_task)
    pump(*q_tasks)
    pump(*kv_tasks)
    pump(*f_tasks)
    pump(*q_tasks)
    pump(*kv_tasks)
    pump(x_task)
    pump(*q_tasks)
    pump(*kv_tasks)
    pump(*f_tasks)
    drain(g_task)
    drain(x_task)

    mark('norm1')
    for i in range(2):
        here = pl.ds(240 * i, 240)
        get = lambda n: x8[n // 2, n % 2, here, :].astype(F32)
        def put(n, v):
            n1p[here, 256 * n:256 * n + 256] = v
        r1[here, :] = jnp.broadcast_to(norm_block_rows(get, lambda n: g8[n // 2, n % 2, 0:1, :], 256, put), (240, 128))
        low = pl.ds(480, 64)
        get = lambda n: x8[n // 2, n % 2, low, 128 * i:128 * i + 128].astype(F32)
        def put(n, v):
            n1a[64 * i:64 * i + 64, 128 * n:128 * n + 128] = v
        r1[480 + 64 * i:544 + 64 * i, :] = jnp.broadcast_to(
            norm_block_rows(get, lambda n: g8[n // 2, n % 2, 2:3, 0:128], 128, put), (64, 128))
    pump(*q_tasks)
    pump(*kv_tasks)
    for task in q_tasks:
        drain(task)
    mark('qkv')
    def queries(i, carry):
        here = pl.ds(pl.multiple_of(240 * i, 16), 240)
        qkvo[0, i, 0:240, :] = dot(n1p[here, :], qo[:, :, :, :, 0:256].reshape(2048, 256), 1, 0).astype(BF)
        return carry
    lax.fori_loop(0, 2, queries, 0)
    for task in kv_tasks:
        drain(task)
    def keys(i, carry):
        here = pl.ds(pl.multiple_of(240 * i, 16), 240)
        for j in range(2):
            qkvo[1 + j, i, 0:240, :] = dot(
                n1p[here, :], kv[:, :, :, :, 256 * j:256 * j + 256].reshape(2048, 256), 1, 0).astype(BF)
        return carry
    lax.fori_loop(0, 2, keys, 0)
    low = [dot(n1a[...], qoa[:, :, :, :, 0:256].reshape(1024, 256), 1, 0).astype(BF)]
    for j in range(2):
        low.append(dot(n1a[...], kva[:, :, :, :, 256 * j:256 * j + 256].reshape(1024, 256), 1, 0).astype(BF))
    for i in range(2):
        for j in range(3):
            qkvo[j, i, 240:304, :] = low[j][64 * i:64 * i + 64]
    saves = [comm.local(qo, out_q), comm.local(qoa, out_qa), comm.local(kv, out_kv), comm.local(kva, out_kva),
             comm.local(n1p, out_n1p), comm.local(n1a, out_n1a), comm.local(r1, out_r1), comm.local(g8, out_g)]
    mark('attn')
    for i in range(2):
        probs = soft(qkvo[0, i, 0:304, :], qkvo[1, i], lens[i])
        qkvo[3, i, 0:304, :] = dot(probs.astype(BF), qkvo[2, i], 1, 0).astype(BF)
    saves.append(comm.local(qkvo, out_qkvo))
    mark('outproj')
    oa = jnp.concatenate([qkvo[3, 0, 240:304, :], qkvo[3, 1, 240:304, :]], axis=0)

    def terms(step):
        k = place.off("x", step)
        for j in range(2):
            weight = qo[k, j, :, :, 256:512].reshape(256, 256)
            for i in range(2):
                blocks[k, j, 240 * i:240 * i + 240, :] = dot(qkvo[3, i, 0:240, :], weight, 1, 1).astype(BF)
            small = dot(oa, qoa[k, j, :, :, 256:512].reshape(128, 256), 1, 1).astype(BF)
            for i in range(2):
                blocks[k, j, 480:544, 128 * i:128 * i + 128] = small[64 * i:64 * i + 64]

    mark('rs8')
    sum_task = block_sum_both(comm, blocks, (l0, l1, l2, l3, l4, l5, l6, l7), T)
    terms(2)
    pump(sum_task)
    terms(1), terms(3), terms(0)
    pump(sum_task)
    pump(f_tasks[0], f_tasks[1])
    pump(f_tasks[0], f_tasks[1])
    pump(sum_task)
    pump(f_tasks[2])
    pump(f_tasks[2])
    pump(sum_task)
    pump(f_tasks[3], f_tasks[4])
    pump(f_tasks[3], f_tasks[4])
    pump(sum_task)
    drain(sum_task)
    mark('hmake')
    hv[...] = xv[...].astype(F32) + blocks[place.x, place.zl].astype(F32)
    full[place.x, place.z] = hv[...].astype(BF)
    saves += [comm.local(hv, out_h), comm.local(xv, out_xb)]
    mark('hplane')
    h_task = comm.plane_gather(lambda k, j, p: full.at[k, j, p], PARTS_A, PARTS_B)
    pump(h_task)
    pump(h_task)
    pump(f_tasks[0])
    pump(h_task)
    pump(f_tasks[1])
    pump(h_task)
    pump(f_tasks[2])
    pump(h_task)
    pump(f_tasks[3], f_tasks[4])
    pump(f_tasks[0], f_tasks[1])
    drain(h_task)
    saves.append(comm.local(full, out_h16))
    mark('norm2')
    for zhi in range(2):
        def rows_norm(i, carry):
            here = pl.ds(pl.multiple_of(240 * i, 16), 240)
            there = pl.ds(pl.multiple_of(480 * zhi + 240 * i, 16), 240)
            get = lambda n: full[n // 2, 2 * zhi + n % 2, here, :].astype(F32)
            def put(n, v):
                n2p[there, 256 * n:256 * n + 256] = v
            scale = norm_block_rows(get, lambda n: g8[n // 2, n % 2, 1:2, :], 256, put)
            r2[zhi, here, :] = jnp.broadcast_to(scale, (240, 128))
            return carry
        lax.fori_loop(0, 2, rows_norm, 0)
        for i in range(2):
            get = lambda n: full[n // 2, 2 * zhi + n % 2, 480:544, 128 * i:128 * i + 128].astype(F32)
            base = 128 * zhi + 64 * i
            def put(n, v):
                n2a[base:base + 64, 128 * n:128 * n + 128] = v
            scale = norm_block_rows(get, lambda n: g8[n // 2, n % 2, 2:3, 128:256], 128, put)
            r2[zhi, 480 + 64 * i:544 + 64 * i, :] = jnp.broadcast_to(scale, (64, 128))
    mark('tail')
    saves += [comm.local(n2p, out_n2p), comm.local(n2a, out_n2a), comm.local(r2.at[zh], out_r2)]
    pump(*f_tasks[2:])
    for task in f_tasks:
        drain(task)
    for copy in saves:
        copy.wait()
    mark(None)
    comm.close()


def attend(lens, *args):
    wide5 = lambda n, c: (4, 2, 2, n, c)
    outs = [((T, 256), BF), ((CH,) + wide5(128, 768), BF), (wide5(64, 768), BF), (wide5(128, 512), BF), (wide5(64, 512), BF),
            (wide5(128, 512), BF), (wide5(64, 512), BF), ((4, 2, 8, 256), F32),
            ((480, 2048), BF), ((128, 1024), BF), ((4, 2, KEYS, 256), BF), ((608, 128), F32), ((T, 256), F32),
            ((4, 4, T, 256), BF), ((960, 2048), BF), ((256, 1024), BF), ((608, 128), F32)]
    vm = pltpu.VMEM
    scratch = [vm((4, 2, 96, 128), BF), vm((192, 512), BF)] + [vm(s, d) for s, d in outs[3:7]] + [
        vm((4, 2, T, 256), BF), vm((4, 2, 8, 256), F32), vm((480, 2048), BF), vm((128, 1024), BF),
        vm((4, 2, KEYS, 256), BF), vm((608, 128), F32), vm((T, 256), BF), vm((T, 256), F32), vm((4, 4, T, 256), BF),
        vm((960, 2048), BF), vm((256, 1024), BF), vm((2, 608, 128), F32), vm((4, 2, T, 256), BF)] + block_lands(T)
    scratch += [vm((2, CH, 128, 768), BF), vm((2, 64, 768), BF), vm((128, 512), BF), vm((64, 512), BF), vm((96, 128), BF),
                vm((8, 256), F32), vm((64, 256), F32)]
    return pl.pallas_call(
        attend_kernel,
        out_shape=[jax.ShapeDtypeStruct(s, d) for s, d in outs],
        in_specs=[pl.BlockSpec(memory_space=pltpu.SMEM)] + [INSIDE] * len(args),
        out_specs=[ANY] * len(outs),
        scratch_shapes=scratch + SEM_SCRATCH,
        compiler_params=pltpu.CompilerParams(collective_id=0, has_side_effects=True, vmem_limit_bytes=VMEM_CAP),
        name="attend",
    )(lens, *args)
EARLY = 2
TILE = 240


def gelu_parts(z):
    a, b = 0.7978845608028654, 0.044715
    t = jnp.tanh(a * (z + b * z * z * z))
    half = 0.5 * (1.0 + t)
    return z * half, half + 0.5 * z * (1.0 - t * t) * a * (1.0 + 3.0 * b * z * z)


def side_rows(full, z_low, base, count):
    return jnp.concatenate([full[x, z_low + zl, pl.ds(base, count), :] for x, zl in pairs8()], axis=1)


def feed_forward_kernel(f, fa, n2p, n2a, cot_pre, cot_act, *refs):
    out_s, out_late, refs = refs[:EARLY + 1], refs[EARLY + 1:CH + 1], refs[CH + 1:]
    out_d8, out_y, out_c, wv, wav, np_, na, gc, ga, dd, aa, dda, aaa, bb, bf, bn, d8, grad_act, cb, spare = refs[:20]
    lands = [refs[20 + 3 * i:23 + 3 * i] for i in range(EARLY + 1)]
    comm = Comm(*refs[-3:])
    comm.greet(PEERS)
    place = comm.place
    loads = [comm.local(n2p, np_), comm.local(f.at[0], wv.at[0]), comm.local(n2a, na),
             comm.local(f.at[1], wv.at[1]), comm.local(f.at[2], wv.at[2]), comm.local(f.at[3], wv.at[3]),
             comm.local(fa, wav)]
    for i in range(2):
        cb[240 * i:240 * i + 240, :] = cot_pre[i].astype(BF)
    cb[480:544, :] = act_rows(cot_act, spare).astype(BF)
    c_task = plane_spread(comm, gc, cb)
    comm.enter(PEERS)
    pump(c_task)
    mark("units")
    loads[0].wait()

    def gate_up(left, weight):
        both = dot(left, weight, 1, 0)
        up = both[:, 256:512]
        value, slope = gelu_parts(both[:, 0:256])
        return (value * up).astype(BF), (up * slope).astype(BF), value.astype(BF)

    for i in range(CH):
        loads[(1, 3, 4, 5)[i]].wait()
        def unit(t, carry):
            here = pl.ds(pl.multiple_of(TILE * t, 16), TILE)
            a, b, c = gate_up(np_[here, :], wv[i, :, :, :, :, 0:512].reshape(2048, 512))
            aa[here, 256 * i:256 * i + 256] = a
            dd[here, 512 * i:512 * i + 256] = b
            dd[here, 512 * i + 256:512 * i + 512] = c
            return carry
        lax.fori_loop(0, 4, unit, 0)
        if i in (0, 1):
            pump(c_task)
    loads[2].wait(), loads[6].wait()
    aaa[...], dda[:, 0:256], dda[:, 256:512] = gate_up(na[...], wav[:, :, :, :, 0:512].reshape(1024, 512))

    def product(ref, x, z, left, left_a, lo, hi):
        zh_, zl_ = lax.div(z, 2), lax.rem(z, 2)
        here = pl.ds(pl.multiple_of(480 * zh_, 16), 480)
        rows_w = jnp.concatenate([wv[i, x, zl_, :, :, lo:hi].reshape(256, hi - lo) for i in range(CH)], axis=1)
        ref[0:480, :] = dot(left[here, :], rows_w, 1, 1).astype(BF)
        there = pl.ds(pl.multiple_of(128 * zh_, 16), 128)
        small = dot(left_a[there, :], wav[x, zl_, :, :, lo:hi].reshape(128, hi - lo), 1, 1).astype(BF)
        ref[480:544, 0:128] = small[0:64]
        ref[480:544, 128:256] = small[64:128]

    def down_terms(t, carry):
        x, z = lax.div(t, 4), lax.rem(t, 4)
        product(bb.at[x, z], x, z, aa, aaa, 512, 768)
        return carry

    mark("ydown")
    pump(c_task)
    lax.fori_loop(0, 8, down_terms, 0)
    pump(c_task)
    lax.fori_loop(8, 16, down_terms, 0)
    saves = [comm.local(bb, out_y)]
    mark("cwait")
    drain(c_task)
    saves.append(comm.local(gc.at[:, pl.ds(2 * place.zh, 2)], out_c))
    mark("dact")
    for i in range(CH):
        def dact_unit(t, carry):
            here = pl.ds(pl.multiple_of(TILE * t, 16), TILE)
            rows_c = side_rows(gc, 2 * lax.div(t, 2), pl.multiple_of(TILE * lax.rem(t, 2), 16), TILE)
            dact = dot(rows_c, wv[i, :, :, :, :, 512:768].reshape(2048, 256), 1, 0)
            for j in range(2):
                there = slice(512 * i + 256 * j, 512 * i + 256 * j + 256)
                dd[here, there] = (dact * dd[here, there].astype(F32)).astype(BF)
            return carry
        lax.fori_loop(0, 4, dact_unit, 0)
    for zhi in range(2):
        for i in range(2):
            base = 128 * zhi + 64 * i
            for n in range(8):
                ga[base:base + 64, 128 * n:128 * n + 128] = gc[n // 2, 2 * zhi + n % 2, 480:544, 128 * i:128 * i + 128]
    dact = dot(ga[...], wav[:, :, :, :, 512:768].reshape(1024, 256), 1, 0)
    for j in range(2):
        there = slice(256 * j, 256 * j + 256)
        dda[:, there] = (dact * dda[:, there].astype(F32)).astype(BF)
    saves[0].wait()

    mark("back")
    far_x, far_z = place.off("x", 2), place.off("z", 2)

    def far_terms(t, carry):
        x = jnp.where(t < 4, t, far_x)
        z = jnp.where(t < 4, far_z, lax.rem(far_z + jnp.where(t < 4, 0, t - 3), 4))
        product(bb.at[x, z], x, z, dd, dda, 0, 512)
        return carry

    def near_terms(t, carry):
        x, z = lax.rem(far_x + 1 + lax.div(t, 3), 4), lax.rem(far_z + 1 + lax.rem(t, 3), 4)
        product(bb.at[x, z], x, z, dd, dda, 0, 512)
        return carry

    lax.fori_loop(0, 7, far_terms, 0)
    b_task = plane_sum(comm, bb, bf, bn)
    pump(b_task)
    lax.fori_loop(0, 9, near_terms, 0)
    pump(b_task)
    pump(b_task)

    mark("grads")

    def weight_grads(i):
        def block_rows(y, carry):
            here = pl.ds(pl.multiple_of(512 * y, 512), 512)
            left_n = np_[:, here]
            left_c = jnp.concatenate(
                [jnp.concatenate([gc[y, zl, 0:480, :], gc[y, 2 + zl, 0:480, :]], axis=0) for zl in range(2)], axis=1)
            for j in range(3):
                if j < 2:
                    value = dot(left_n, dd[:, 512 * i + 256 * j:512 * i + 256 * j + 256], 0, 0).astype(BF)
                else:
                    value = dot(left_c, aa[:, 256 * i:256 * i + 256], 0, 0).astype(BF)
                wv[i, y, :, :, :, 256 * j:256 * j + 256] = value.reshape(2, 2, 128, 256)
            return carry
        lax.fori_loop(0, 4, block_rows, 0)

    def act_grads():
        for y in range(4):
            left_n, left_c = na[:, 256 * y:256 * y + 256], ga[:, 256 * y:256 * y + 256]
            for j in range(3):
                value = dot(left_n, dda[:, 256 * j:256 * j + 256], 0, 0) if j < 2 else dot(left_c, aaa[...], 0, 0)
                grad_act[y, :, :, :, 256 * j:256 * j + 256] = value.astype(BF).reshape(2, 2, 64, 256)

    grads = [wv.at[i] for i in range(EARLY)] + [grad_act]
    sums = [wide_sum(comm, grad, s, r.at[0], r.at[1], r.at[2], z, 64 if i == EARLY else 128, False)
            for i, (grad, (s, r, z)) in enumerate(zip(grads, lands))]
    weight_grads(0)
    pump(sums[0])
    weight_grads(1)
    pump(sums[0], sums[1])
    pump(b_task)
    act_grads()
    pump(sums[2])
    pump(b_task)
    pump(sums[1])
    drain(b_task)
    mark("dn2")
    d8[place.x, place.zl] = bb[place.x, place.z]
    d_task = comm.pair_ring_gather("zl", "x", lambda k, j, p: d8.at[k, j, p], PARTS_8,
                                   lambda p: d8.at[place.x, place.zl, p], d8.at[place.x, place.zl], slice(None))
    pump(d_task), pump(d_task)
    pump(sums[0], sums[2])
    weight_grads(2)
    saves.append(comm.local(wv.at[2], out_late[0]))
    pump(d_task)
    pump(sums[1])
    weight_grads(3)
    saves.append(comm.local(wv.at[3], out_late[1]))
    pump(d_task)
    pump(sums[2], sums[0])
    pump(d_task)
    pump(sums[1], sums[2])
    drain(d_task)
    saves.append(comm.local(d8, out_d8))
    mark("sums")
    for task in sums:
        drain(task)
    for grad, (_, _, swap), out in zip(grads, lands, out_s):
        saves.append(comm.local(grad.at[place.y, place.zh, place.core], out.at[place.zh]))
        saves.append(comm.local(swap, out.at[1 - place.zh]))
    for copy in saves[1:]:
        copy.wait()
    mark(None)
    comm.close()


def feed_forward(f, fa, n2p, n2a, cot_pre, cot_act):
    grad = (4, 2, 2, 128, 768)
    outs = [(2, 128, 768)] * EARLY + [(2, 64, 768)] + [grad] * (CH - EARLY) + [(4, 2, T, 256), (4, 4, T, 256), (4, 2, T, 256)]
    vm = lambda *s: pltpu.VMEM(s, BF)
    scratch = [vm(CH, *grad), vm(4, 2, 2, 64, 768), vm(960, 2048), vm(256, 1024), vm(4, 4, T, 256),
               vm(256, 1024), vm(960, 2048), vm(960, 1024), vm(256, 512), vm(256, 256)]
    scratch += [vm(4, 4, T, 256)] + LAND_16 + [vm(4, 2, T, 256), vm(4, 2, 2, 64, 768), vm(T, 256), pltpu.VMEM((64, 256), F32)]
    for n in [128] * EARLY + [64]:
        scratch += [vm(4, 2, n, 768), vm(3, 2, n, 768), vm(n, 768)]
    return pl.pallas_call(
        feed_forward_kernel,
        out_shape=[jax.ShapeDtypeStruct(s, BF) for s in outs],
        in_specs=[ANY] * 4 + [INSIDE] * 2,
        out_specs=[ANY] * len(outs),
        scratch_shapes=scratch + SEM_SCRATCH,
        compiler_params=pltpu.CompilerParams(collective_id=2, has_side_effects=True, vmem_limit_bytes=VMEM_CAP),
        name="feed_forward",
    )(f, fa, n2p, n2a, cot_pre, cot_act)
TS = T + 16
FAR_PEERS = tuple(f"w{step}{flip}" for step, flip in CHIPS if (step, flip) not in ((1, 0), (3, 0), (0, 1)))
KV_PARTS = [(rows(0, 160), 1), (rows(160, 304), -1)]


def attend_back_kernel(lens, d8, h16, c16, r2, r1, g8, qo, qoa, kv, kva, n1p, n1a, qkvo, xb, cot_pre, cot_act, g2, g3, yt, h_own,
                       out_s2, out_s3, out_q, out_qa, out_kv, out_kva, out_x, out_y, out_g,
                       dv8, hv, cv, r2v, r1v, g8v, qov, qoav, kvv, kvav, npv, nav, qv, xv, cotv, g2v, g3v, yv, how,
                       mean, ghp, gha, dhb, dov, dqp, dqa, stat, gains, gsum, gains16, gains2, spare, outx, outy,
                       gq, gkv, gqa, gkva, kvb, blocks, yf, yn, l0, l1, l2, l3, l4, l5, l6, l7, k0, k1, k2, k3,
                       s2, s3, sq, skv, sqa, skva, t2, t3, tq, tkv, tqa, tkva, z2, z3, zq, zkv, zqa, zkva, *sems):
    comm = Comm(*sems)
    comm.greet(PEERS + FAR_PEERS)
    place = comm.place
    x, y, zh, zl, core = place.x, place.y, place.zh, place.zl, place.core
    side = pl.ds(2 * zh, 2)
    load = comm.local
    la = [load(d8, dv8), load(h16.at[:, side], hv), load(r2, r2v), load(g8, g8v), load(c16, cv)]
    lb = [load(qo, qov), load(qoa, qoav), load(qkvo, qv)]
    ly = load(yt, yv)
    lg = [load(g2, g2v), load(g3, g3v)]
    lc = [load(kv, kvv), load(kva, kvav), load(n1p, npv), load(n1a, nav), load(xb, xv), load(r1, r1v), load(h_own, how)]
    comm.enter(PEERS + FAR_PEERS)
    late = [wide_sum(comm, g2v, s2, t2.at[0], t2.at[1], t2.at[2], z2, 128, False),
            wide_sum(comm, g3v, s3, t3.at[0], t3.at[1], t3.at[2], z3, 128, False)]
    y_task = plane_sum(comm, yv, yf, yn)
    for i in range(2):
        cotv[240 * i:240 * i + 240, :] = cot_pre[i]
    cotv[480:544, :] = act_rows(cot_act, spare)
    mark("dh")
    for copy in la:
        copy.wait()
    for i in range(2):
        here = pl.ds(240 * i, 240)
        scale = r2v[here, 0:1]
        gain = lambda n: g8v[n // 2, n % 2, 1:2, :]
        grad = lambda n: dv8[n // 2, n % 2, here, :].astype(F32) * gain(n)
        unit = lambda n: hv[n // 2, n % 2, here, :].astype(F32) * scale
        m = sum(jnp.sum(grad(n) * unit(n), axis=1, keepdims=True) for n in range(8)) / 2048
        mean[here, :] = jnp.broadcast_to(m, (240, 128))
        for n in range(8):
            value = cv[n // 2, n % 2, here, :].astype(F32) + scale * (grad(n) - unit(n) * m)
            ghp[here, 256 * n:256 * n + 256] = value.astype(BF)
        here, there, lanes = pl.ds(480, 64), pl.ds(480 + 64 * i, 64), pl.ds(128 * i, 128)
        scale_a = r2v[there, 0:1]
        gain_a = lambda n: g8v[n // 2, n % 2, 2:3, 128:256]
        grad_a = lambda n: dv8[n // 2, n % 2, here, lanes].astype(F32) * gain_a(n)
        unit_a = lambda n: hv[n // 2, n % 2, here, lanes].astype(F32) * scale_a
        m = sum(jnp.sum(grad_a(n) * unit_a(n), axis=1, keepdims=True) for n in range(8)) / 1024
        mean[there, :] = jnp.broadcast_to(m, (64, 128))
        for n in range(8):
            value = cv[n // 2, n % 2, here, lanes].astype(F32) + scale_a * (grad_a(n) - unit_a(n) * m)
            gha[64 * i:64 * i + 64, 128 * n:128 * n + 128] = value.astype(BF)
    ly.wait()
    pump(y_task), pump(y_task)
    lg[0].wait()
    pump(late[0])
    lg[1].wait()
    pump(late[1])
    mark("attnback")
    for copy in lb:
        copy.wait()
    for i in range(2):
        here = pl.ds(240 * i, 240)
        dov[i, 0:240, :] = dot(ghp[here, :], qov[:, :, :, :, 256:512].reshape(2048, 256), 1, 0).astype(BF)
    low = dot(gha[...], qoav[:, :, :, :, 256:512].reshape(1024, 256), 1, 0).astype(BF)
    for i in range(2):
        dov[i, 240:304, :] = low[64 * i:64 * i + 64]
    for i in range(2):
        q, k, v, do = qv[0, i, 0:304, :], qv[1, i], qv[2, i], dov[i]
        probs = soft(q, k, lens[i])
        inner = probs * dot(do, v, 1, 1)
        dscores = (inner - probs * jnp.sum(inner, axis=1, keepdims=True)).astype(BF)
        dq = (dot(dscores, k, 1, 0) * 0.0625).astype(BF)
        dk = (dot(dscores, q, 0, 0) * 0.0625).astype(BF)[0:304]
        dv = dot(probs.astype(BF), do, 0, 0).astype(BF)[0:304]
        for j, value in enumerate((dq, dk, dv)):
            dqp[240 * i:240 * i + 240, 256 * j:256 * j + 256] = value[0:240]
            dqa[64 * i:64 * i + 64, 256 * j:256 * j + 256] = value[240:304]
        total = dq.astype(F32) * q.astype(F32) + dk.astype(F32) * k[0:304].astype(F32) + dv.astype(F32) * v[0:304].astype(F32)
        total = jnp.broadcast_to(jnp.sum(total, axis=1, keepdims=True), (304, 128))
        stat[240 * i:240 * i + 240, :] = total[0:240]
        stat[480 + 64 * i:544 + 64 * i, :] = total[240:304]
    stat[608:640, :] = jnp.zeros((32, 128), F32)
    line = stat[...].T[0:1]
    line = jnp.concatenate([line[:, 0:256], line[:, 256:512], jnp.concatenate([line[:, 512:640], jnp.zeros((1, 128), F32)], axis=1),
                            jnp.zeros((13, 256), F32)], axis=0).astype(BF)
    for n in range(8):
        blocks[n // 2, n % 2, T:TS, :] = line
    lane = lax.broadcasted_iota(jnp.int32, (512, 128), 1)
    col = lax.broadcasted_iota(jnp.int32, (512, 128), 0)
    kv_sum = block_sum(comm, kvb, (k0, k1, k2), k3, KV_PARTS)
    for n in range(8):
        total = []
        for i in range(2):
            at = lane - 64 * i
            pick = ((at >= 0) & (at < 32) & (col == 32 * n + at)) | ((at >= 32) & (at < 64) & (col == 224 + 32 * n + at))
            pick = pick.astype(F32).astype(BF)
            total.append((dot(dqp[240 * i:240 * i + 240, 256:768], pick, 1, 0), dot(dqa[64 * i:64 * i + 64, 256:768], pick, 1, 0)))
        kvb[n // 2, n % 2, 0:240, :] = (total[0][0] + total[1][0]).astype(BF)
        kvb[n // 2, n % 2, 240:304, :] = (total[0][1] + total[1][1]).astype(BF)
    pump(late[0])
    pump(kv_sum)
    for copy in lc:
        copy.wait()
    mark("terms")

    def terms(step):
        k = place.off("x", step)
        for j in range(2):
            weight = jnp.concatenate([qov[k, j, :, :, 0:256].reshape(256, 256), kvv[k, j].reshape(256, 512)], axis=1)
            blocks[k, j, 0:480, :] = dot(dqp[...], weight, 1, 1).astype(BF)
            weight = jnp.concatenate([qoav[k, j, :, :, 0:256].reshape(128, 256), kvav[k, j].reshape(128, 512)], axis=1)
            small = dot(dqa[...], weight, 1, 1).astype(BF)
            for i in range(2):
                blocks[k, j, 480:544, 128 * i:128 * i + 128] = small[64 * i:64 * i + 64]

    def outer(grad, n, left, right, lo, width):
        def block_rows(k, carry):
            here = pl.ds(pl.multiple_of(4 * n * k, 4 * n), 4 * n)
            value = dot(left[:, here], right, 0, 0).astype(BF)
            grad[k, :, :, :, lo:lo + width] = value.reshape(2, 2, n, width)
            return carry
        lax.fori_loop(0, 4, block_rows, 0)

    terms(2)
    sum_task = block_sum_both(comm, blocks, (l0, l1, l2, l3, l4, l5, l6, l7), TS)
    pump(sum_task)
    pump(late[1])
    terms(1), terms(3), terms(0)
    pump(sum_task)
    mark("attngrads")
    o_act = jnp.concatenate([qv[3, 0, 240:304, :], qv[3, 1, 240:304, :]], axis=0)
    o_pre = jnp.concatenate([qv[3, 0, 0:240, :], qv[3, 1, 0:240, :]], axis=0)
    outer(gq, 128, ghp, o_pre, 256, 256)
    outer(gqa, 64, gha, o_act, 256, 256)
    outer(gq, 128, npv, dqp[:, 0:256], 0, 256)
    outer(gqa, 64, nav, dqa[:, 0:256], 0, 256)
    q_tasks = [wide_sum(comm, gq, sq, tq.at[0], tq.at[1], tq.at[2], zq, 128, True),
               wide_sum(comm, gqa, sqa, tqa.at[0], tqa.at[1], tqa.at[2], zqa, 64, True)]
    kv_tasks = [wide_sum(comm, gkv, skv, tkv.at[0], tkv.at[1], tkv.at[2], zkv, 128, True),
                wide_sum(comm, gkva, skva, tkva.at[0], tkva.at[1], tkva.at[2], zkva, 64, True)]
    pump(*q_tasks)
    pump(kv_sum)
    pump(y_task)
    pump(late[0])
    pump(*q_tasks)
    pump(sum_task)
    pump(sum_task)
    pump(kv_sum)
    pump(late[1])
    pump(late[0])
    drain(kv_sum)
    own = kvb[x, zl]
    share = []
    for i in range(2):
        lane = lax.broadcasted_iota(jnp.int32, (128, 128), 0)
        col = lax.broadcasted_iota(jnp.int32, (128, 128), 1)
        pick = ((col < 64) & (lane == col + 64 * i)).astype(F32).astype(BF)
        share.append(dot(own, pick, 1, 0).astype(BF))
    outer(gkv, 128, npv, jnp.concatenate([share[0][0:240], share[1][0:240]], axis=0), 0, 128)
    outer(gkva, 64, nav, jnp.concatenate([share[0][240:304], share[1][240:304]], axis=0), 0, 128)
    pump(*kv_tasks)
    mark("late")
    pump(y_task)
    pump(sum_task)
    pump(*q_tasks)
    pump(*kv_tasks)
    pump(y_task)
    drain(sum_task)
    mark("dx")
    g_pre, g_act = g8v[x, zl, 0:1, :], g8v[x, zl, 2:3, 0:128]
    f_pre, f_act = g8v[x, zl, 1:2, :], g8v[x, zl, 2:3, 128:256]
    line = blocks[x, zl, T:TS, :].astype(F32)
    line = jnp.concatenate([line[0:1], line[1:2], line[2:3, 0:128]], axis=1)
    stat[...] = jnp.broadcast_to(line, (128, 640)).T

    def own_norm(here, there, lanes, gain_f, gain_a, width):
        s2_, s1_ = r2v[there, 0:1], r1v[there, 0:1]
        back, unit = dv8[x, zl, here, lanes].astype(F32), hv[x, zl, here, lanes].astype(F32) * s2_
        dh = cotv[here, lanes] + s2_ * (back * gain_f - unit * mean[there, 0:1])
        gain_f_grad = jnp.sum(back * unit, axis=0, keepdims=True)
        back, unit = blocks[x, zl, here, lanes].astype(F32), xv[here, lanes].astype(F32) * s1_
        outx[here, lanes] = dh + s1_ * (back * gain_a - unit * (stat[there, 0:1] / width))
        return jnp.sum(back * unit, axis=0, keepdims=True), gain_f_grad

    pre = [own_norm(pl.ds(240 * i, 240), pl.ds(240 * i, 240), pl.ds(0, 256), f_pre, g_pre, 2048) for i in range(2)]
    act = [own_norm(pl.ds(480, 64), pl.ds(480 + 64 * i, 64), pl.ds(128 * i, 128), f_act, g_act, 1024) for i in range(2)]
    gains[...] = jnp.concatenate(
        [pre[0][0] + pre[1][0], pre[0][1] + pre[1][1],
         jnp.concatenate([act[0][0] + act[1][0], act[0][1] + act[1][1]], axis=1), jnp.zeros((5, 256), F32)], axis=0)
    saves = [load(outx, out_x)]
    g_task = small_total(comm, gains16, gains2, gains, gsum)
    pump(g_task)
    mark("tail")
    pump(*q_tasks)
    pump(*kv_tasks)
    pump(late[1])
    drain(y_task)
    outy[...] = (yv[x, place.z].astype(F32) + how[...]).astype(BF)
    saves.append(load(outy, out_y))
    pump(*q_tasks)
    pump(*kv_tasks)
    pump(g_task)
    for task in q_tasks + kv_tasks + late:
        drain(task)
    drain(g_task)
    saves += [load(gsum, out_g), load(gkv.at[y, zh, core], out_kv), load(gkva.at[y, zh, core], out_kva), load(gq.at[y, zh, core], out_q), load(gqa.at[y, zh, core], out_qa)]
    saves += [load(g2v.at[y, zh, core], out_s2.at[zh]), load(z2, out_s2.at[1 - zh])]
    saves += [load(g3v.at[y, zh, core], out_s3.at[zh]), load(z3, out_s3.at[1 - zh])]
    for copy in saves:
        copy.wait()
    mark(None)
    comm.close()


def attend_back(lens, *args):
    outs = [((2, 128, 768), BF), ((2, 128, 768), BF), ((128, 512), BF), ((64, 512), BF), ((128, 128), BF), ((64, 128), BF), ((T, 256), F32),
            ((T, 256), BF), ((8, 256), F32)]
    vm = lambda *s: pltpu.VMEM(s, BF)
    vf = lambda *s: pltpu.VMEM(s, F32)
    wide = lambda n, c: (4, 2, 2, n, c)
    back = [(128, 768), (128, 768), (128, 512), (128, 128), (64, 512), (64, 128)]
    scratch = [vm(4, 2, T, 256), vm(4, 2, T, 256), vm(4, 2, T, 256), vf(608, 128), vf(608, 128), vf(4, 2, 8, 256),
               vm(4, 2, 2, 128, 512), vm(4, 2, 2, 64, 512), vm(4, 2, 2, 128, 512), vm(4, 2, 2, 64, 512),
               vm(480, 2048), vm(128, 1024), vm(4, 2, KEYS, 256), vm(T, 256), vf(T, 256), vm(*wide(128, 768)),
               vm(*wide(128, 768)), vm(4, 4, T, 256), vf(T, 256)]
    scratch += [vf(608, 128), vm(480, 2048), vm(128, 1024), vf(8, 128), vm(2, 304, 256), vm(480, 768), vm(128, 768),
                vf(640, 128), vf(8, 256), vf(8, 256), vf(8, 8, 256), vf(2, 8, 256), vf(64, 256), vf(T, 256), vm(T, 256)]
    scratch += [vm(*wide(n, c)) for n, c in back[2:]]
    scratch += [vm(4, 2, 304, 128), vm(4, 2, TS, 256)] + LAND_16 + block_lands(TS) + [vm(2, 304, 128)] * 3 + [vm(304, 128)]
    scratch += [vm(4, 2, n, c) for n, c in back] + [vm(3, 2, n, c) for n, c in back] + [vm(n, c) for n, c in back]
    return pl.pallas_call(
        attend_back_kernel,
        out_shape=[jax.ShapeDtypeStruct(s, d) for s, d in outs],
        in_specs=[pl.BlockSpec(memory_space=pltpu.SMEM)] + [ANY] * 14 + [INSIDE] * 2 + [ANY] * (len(args) - 16),
        out_specs=[ANY] * len(outs),
        scratch_shapes=scratch + SEM_SCRATCH,
        compiler_params=pltpu.CompilerParams(collective_id=3, has_side_effects=True, vmem_limit_bytes=VMEM_CAP),
        name="attend_back",
    )(lens, *args)
def result_kernel(s0, s1, s2, s3, sa, sq, sqa, skv, skva, y, gx, gains,
                  y_pre, y_act, x_pre, x_act, attn_gain_pre, query_pre, key_pre, value_pre, out_pre, ffn_gain_pre, gate_pre,
                  up_pre, down_pre, attn_gain_act, query_act, key_act, value_act, out_act, ffn_gain_act, gate_act, up_act,
                  down_act):
    for i in range(2):
        here, lanes = slice(240 * i, 240 * i + 240), slice(128 * i, 128 * i + 128)
        y_pre[i], x_pre[i] = y[here, :], gx[here, :]
        x_act[:, i, :] = gx[480:530, lanes]
    low = y[480:544, :].astype(F32)[0:50]
    y_act[...] = jnp.stack([low[:, 0:128], low[:, 128:256]], axis=1).astype(BF)
    attn_gain_pre[...], ffn_gain_pre[...] = gains[0:1, :], gains[1:2, :]
    attn_gain_act[...], ffn_gain_act[...] = gains[2:3, 0:128], gains[2:3, 128:256]
    for q, kv, query, key, value in ((sq, skv, query_pre, key_pre, value_pre),
                                     (sqa, skva, query_act, key_act, value_act)):
        query[...] = q[:, 0:256].astype(F32)
        both = kv[...].astype(F32).T
        key[...], value[...] = both[0:32], both[32:64]
    out_pre[...], out_act[...] = sq[:, 256:512].astype(F32).T, sqa[:, 256:512].astype(F32)
    for h in range(2):
        for i, s in enumerate((s0, s1, s2, s3)):
            here = slice(1024 * h + 256 * i, 1024 * h + 256 * i + 256)
            gate_pre[:, here], up_pre[:, here] = s[h, :, 0:256].astype(F32), s[h, :, 256:512].astype(F32)
            down_pre[here, :] = s[h, :, 512:768].astype(F32).T
        here = slice(256 * h, 256 * h + 256)
        gate_act[:, here], up_act[:, here] = sa[h, :, 0:256].astype(F32), sa[h, :, 256:512].astype(F32)
        down_act[:, here] = sa[h, :, 512:768].astype(F32)


def results(*args):
    tokens = lambda d: [((2, 240, 256), d), ((50, 2, 128), d)]
    expert = lambda n, h, out, down: [((1, n * 2), F32), ((n, 256), F32), ((32, n), F32), ((32, n), F32), (out, F32),
                                      ((1, n * 2), F32), ((n, h), F32), ((n, h), F32), (down, F32)]
    shapes = tokens(BF) + tokens(F32) + expert(128, 2048, (256, 128), (2048, 128)) + expert(64, 512, (64, 256), (64, 512))
    return pl.pallas_call(
        result_kernel,
        out_shape=[jax.ShapeDtypeStruct(s, d) for s, d in shapes],
        in_specs=[INSIDE] * len(args),
        out_specs=[INSIDE] * len(shapes),
        compiler_params=pltpu.CompilerParams(vmem_limit_bytes=VMEM_CAP),
        name="results",
    )(*args)


def local(x_pre, x_act, lengths, cot_pre, cot_act, attn_gain_pre, query_pre, key_pre, value_pre, out_pre, ffn_gain_pre,
          gate_pre, up_pre, down_pre, attn_gain_act, query_act, key_act, value_act, out_act, ffn_gain_act, gate_act,
          up_act, down_act):
    line = lambda gain: gain.reshape(1, -1)
    x_act, cot_act = x_act.transpose(1, 0, 2), cot_act.transpose(1, 0, 2)
    key_pre, value_pre, key_act, value_act, out_act, down_act = (
        m.T for m in (key_pre, value_pre, key_act, value_act, out_act, down_act))
    (xb, f, fa, qo, qoa, kv, kva, g8, n1p, n1a, qkvo, r1, h_own, h16, n2p, n2a, r2) = attend(
        lengths, x_pre, x_act, line(attn_gain_pre), query_pre, key_pre, value_pre, out_pre, line(ffn_gain_pre), gate_pre,
        up_pre, down_pre, line(attn_gain_act), query_act, key_act, value_act, out_act, line(ffn_gain_act), gate_act, up_act,
        down_act)
    s0, s1, sa, g2, g3, d8, yt, c8 = feed_forward(f, fa, n2p, n2a, cot_pre, cot_act)
    s2, s3, sq, sqa, skv, skva, gx, y, gains = attend_back(
        lengths, d8, h16, c8, r2, r1, g8, qo, qoa, kv, kva, n1p, n1a, qkvo, xb, cot_pre, cot_act, g2, g3, yt, h_own)
    outs = results(s0, s1, s2, s3, sa, sq, sqa, skv, skva, y, gx, gains)
    turn = lambda i, o: o.transpose(1, 0, 2) if i in (1, 3) else o.T if i in (6, 7, 15, 16, 17, 21) else o
    return tuple(o.reshape(-1) if o.shape[0] == 1 else turn(i, o) for i, o in enumerate(outs))


def solution(mesh):
    tok, row, col, vec = P("wide", None, "narrow"), P("wide", "narrow"), P("narrow", "wide"), P("narrow")
    expert = (vec, row, row, row, col, vec, row, row, col)
    return jax.shard_map(
        local, mesh=mesh, in_specs=(tok, tok, P("wide"), tok, tok) + expert + expert,
        out_specs=(tok,) * 4 + expert + expert, check_vma=False)
```
